32 devices in a mesh: dp: 8 (over y, x, core), vocab: 4 (over z).
Axes of the slice: x: 2, y: 2, z: 4, core: 2. Of those that a mesh axis runs over, the one named last changes fastest.
Arguments:
- final_states: bfloat16 [4096, 5376], P(('dp', 'vocab')), may hold values from -12 to 12
- head_blocks: bfloat16 [4, 128, 5376], P('vocab'), may hold values from -0.17048273 to 0.17048273
- block_order: int32 [4], replicated, may hold values from 0 to 3, as said below
- row_tags: int32 [4096], P(('dp', 'vocab')), may hold values from 0 to 3, as said below
- target_word: int32 [4096], P(('dp', 'vocab')), may hold values from 0 to 127
- row_weight: bfloat16 [4096], P(('dp', 'vocab')), may hold values from 0.25 to 2
Outputs:
- row_loss: float32 [4096], P(('dp', 'vocab'))
- state_grad: bfloat16 [4096, 5376], P(('dp', 'vocab'))
- head_grad: float32 [4, 128, 5376], P('vocab', 'dp')
The draws below stay inside these ranges and needn't reach their ends.
Inputs may be any that keep to these rules, and one draw needn't show every extreme that they name: `row_tags`: among the rows of one device at most 40 carry any one tag; one tag, the same on every device, is carried by exactly 40 rows of each device. Each block number appears once; the shortlist of tag l is block_order[l] to block_order[(l + 1) - 1].
All inputs are finite; a program needn't handle non-finite values.
Results may differ from the reference program's by a relative error of at most 0.0052.
Values may be sent and summed in bfloat16 or wider, within the bound.
A program may use at most 128 MiB of HBM per device.

```python
import math
import jax
import jax.numpy as jnp
from jax import lax

D = 5376
BLOCK = 128
LANGS = 4
TOK_DEV = 128
CAP = 40
HEAD_BLOCKS = 4
SHORT_BLOCKS = 1
TOKENS = 4096


def layout_draw(key):
    block_perm = jax.random.permutation(jax.random.fold_in(key, 21), HEAD_BLOCKS).astype(jnp.int32)
    hot_tag = jax.random.randint(jax.random.fold_in(key, 22), (), 0, LANGS)
    device_keys = jax.random.split(jax.random.fold_in(key, 23), TOKENS // TOK_DEV)
    rest_rows = TOK_DEV - CAP

    def device_tags(dev_key):
        key_one, key_two, key_three, key_four = jax.random.split(dev_key, 4)
        count_one = jax.random.randint(key_one, (), max(0, rest_rows - 2 * CAP), min(CAP, rest_rows) + 1)
        remain = rest_rows - count_one
        count_two = jax.random.randint(key_two, (), jnp.maximum(0, remain - CAP), jnp.minimum(CAP, remain) + 1)
        count_three = remain - count_two
        others = jax.random.permutation(key_three, (hot_tag + 1 + jnp.arange(3, dtype=jnp.int32)) % LANGS)
        counts = jnp.zeros((LANGS,), jnp.int32).at[hot_tag].set(CAP)
        counts = counts.at[others[0]].set(count_one).at[others[1]].set(count_two).at[others[2]].set(count_three)
        bounds = jnp.cumsum(counts)
        sorted_tags = jnp.sum((jnp.arange(TOK_DEV, dtype=jnp.int32)[:, None] >= bounds[None, :]).astype(jnp.int32), axis=1)
        return jax.random.permutation(key_four, sorted_tags)
    tag_rows = jax.vmap(device_tags)(device_keys).reshape(-1).astype(jnp.int32)
    return (block_perm, tag_rows)


def head_table(key):
    normal_part = jax.random.truncated_normal(jax.random.fold_in(key, 31), -4.0, 4.0, (HEAD_BLOCKS, BLOCK, D), jnp.float32)
    return normal_part * (3.0 / math.sqrt(D))


def draw_head_blocks(key, part):
    return head_table(key).astype(jnp.bfloat16)


def draw_block_order(key, part):
    return layout_draw(key)[0]


def draw_row_tags(key, part):
    return layout_draw(key)[1]


def draw_final_states(key, part):
    return jax.random.truncated_normal(jax.random.fold_in(key, 41), -5.0, 5.0, (TOKENS, D), jnp.float32).astype(jnp.bfloat16)


def touch_ends(result, rng, least, top_value):
    longest = result.shape.index(max(result.shape))
    spots = []
    for shift in (0, 1):
        where = [jax.random.randint(jax.random.fold_in(rng, axis), (), 0, length) for axis, length in enumerate(result.shape)]
        where[longest] = (where[longest] + shift) % result.shape[longest]
        spots.append(tuple(where))
    return result.at[spots[0]].set(least).at[spots[1]].set(top_value)


def block_levels(stream_key, shape, shards, low, high):
    gain = 1.0
    for dim, shards_of in shards:
        heights = jax.random.uniform(jax.random.fold_in(jax.random.fold_in(stream_key, 6), dim), (shards_of,), jnp.float32, low / len(shards), high / len(shards))
        gain = gain * jnp.repeat(jnp.exp(heights), shape[dim] // shards_of).reshape((-1,) + (1,) * (len(shape) - 1 - dim))
    return gain


def setup_inputs(seed: int = 0) -> dict:
    seeds = jax.random.split(jax.random.key(seed), 7)
    return {
        "final_states": draw_final_states(jax.random.fold_in(seeds[6], 71), 0),
        "head_blocks": draw_head_blocks(jax.random.fold_in(seeds[6], 71), 0),
        "block_order": draw_block_order(jax.random.fold_in(seeds[6], 71), 0),
        "row_tags": draw_row_tags(jax.random.fold_in(seeds[6], 71), 0),
        "target_word": touch_ends(jax.random.randint(seeds[4], (TOKENS,), 0, SHORT_BLOCKS * BLOCK), jax.random.fold_in(seeds[4], 1), 0, (SHORT_BLOCKS * BLOCK) - 1).astype(jnp.int32),
        "row_weight": jnp.clip(0.25 + 1.75 * jax.random.uniform(seeds[5], (TOKENS,), jnp.float32) ** block_levels(seeds[5], (TOKENS,), ((0, 32),), -0.2, 0.2), 0.25, 2.0).astype(jnp.bfloat16),
    }


def reference(final_states, head_blocks, block_order, row_tags, target_word, row_weight):
    block_count = head_blocks.shape[0]
    short_len = block_count // LANGS
    model_width = head_blocks.shape[2]
    columns = block_count * BLOCK
    flat_head = head_blocks.reshape(columns, model_width)
    head_wide = head_blocks.astype(jnp.float32)
    block_ids = jnp.arange(block_count, dtype=jnp.int32)
    placed = jnp.sum(block_ids[:, None] * (block_order[:, None] == block_ids[None, :]).astype(jnp.int32), axis=0)
    owner_tag = placed // short_len
    column_ids = jnp.arange(columns, dtype=jnp.int32)
    column_owner = owner_tag[column_ids // BLOCK]
    row_block = 512
    block_steps = final_states.shape[0] // row_block

    def one_block(grad_total, block_items):
        states, tag_block, target, weight = block_items
        logits = jnp.dot(states, flat_head.T, preferred_element_type=jnp.float32)
        inside = column_owner[None, :] == tag_block[:, None]
        target_block = block_order[tag_block * short_len + target // BLOCK]
        target_col = target_block * BLOCK + target % BLOCK
        target_hit = column_ids[None, :] == target_col[:, None]
        row_peak = jnp.max(jnp.where(inside, logits, -1e30), axis=1)
        exp_total = jnp.sum(jnp.where(inside, jnp.exp(logits - row_peak[:, None]), 0.0), axis=1)
        log_total = row_peak + jnp.log(exp_total)
        picked = jnp.sum(jnp.where(target_hit, logits, 0.0), axis=1)
        row_losses = log_total - picked
        row_probs = jnp.exp(logits - log_total[:, None])
        slot_grads = jnp.where(inside, weight.astype(jnp.float32)[:, None] * (row_probs - target_hit.astype(jnp.float32)), 0.0).astype(jnp.bfloat16)
        grads_wide = slot_grads.astype(jnp.float32).reshape(-1, block_count, BLOCK)
        partial_value = jnp.einsum('rbw,bwd->rbd', grads_wide, head_wide).astype(jnp.bfloat16)
        partial_value = lax.optimization_barrier(partial_value)
        state_rows = jnp.sum(partial_value.astype(jnp.float32), axis=1).astype(jnp.bfloat16)
        grad_total = grad_total + jnp.einsum('rbw,rd->bwd', grads_wide, states.astype(jnp.float32))
        return grad_total, (row_losses, state_rows)

    block_items = (final_states.reshape(block_steps, row_block, model_width),
                   row_tags.reshape(block_steps, row_block),
                   target_word.reshape(block_steps, row_block),
                   row_weight.reshape(block_steps, row_block))
    start_grad = jnp.zeros((block_count, BLOCK, model_width), jnp.float32)
    head_grad, outputs = lax.scan(one_block, start_grad, block_items)
    row_loss = outputs[0].reshape(-1)
    state_grad = outputs[1].reshape(-1, model_width)
    return row_loss, state_grad, head_grad
```

```python
import jax
import jax.numpy as jnp
from jax import lax
from jax.experimental import pallas as pl
from jax.experimental.pallas import tpu as pltpu
from jax.sharding import PartitionSpec as P

BLOCK = 128
LANGS = 4
MESH = pl.DeviceIdType.MESH
F32 = jnp.float32
BF16 = jnp.bfloat16
PARTS = 8


def dot(a, b, dims):
    return lax.dot_general(a, b, ((dims[:1], dims[1:]), ((), ())), preferred_element_type=F32)


def iota(shape, dim):
    return lax.broadcasted_iota(jnp.int32, shape, dim)


def routed_kernel(
    order, tags, words, weights, states, block,
    loss_out, state_out, head_out,
    head_here, send_rows, got_rows, send_meta, got_meta, send_back, got_back, send_loss, got_loss,
    pick_lo, pick_hi, grads_lo, grads_hi, term, pair_send, pair_got, plane_send, plane_got, line_got,
    row_s, row_r, meta_s, meta_r, back_s, back_r, loss_s, loss_r, pair_s, pair_r, plane_s, plane_r,
    line_s, line_r, up_s, down_s, head_r, twin_s, twin_r,
):
    rows, width = states.shape
    half = width // 2
    cap = rows * 5 // 16
    tall = 2 * cap
    words_each = BLOCK // (2 * LANGS)
    step = max(s for s in range(128, 513, 128) if half % s == 0)
    steps = half // step

    dp, z = lax.axis_index("dp"), lax.axis_index("vocab")
    last = lax.axis_size("vocab") - 1
    core = lax.rem(dp, 2)
    x = lax.rem(lax.div(dp, 2), 2)
    y = lax.div(dp, 4)
    chips = [(y if r < 2 else 1 - y) * 2 + (x if r % 2 == 0 else 1 - x) for r in range(4)]
    own = chips[0]
    plane = [(c * 2 + core, z) for c in chips]
    twin = (own * 2 + 1 - core, z)
    line = [(dp, lax.rem(z + d, LANGS)) for d in range(LANGS)]

    barrier = pltpu.get_barrier_semaphore()
    friends = plane[1:] + line[1:] + [twin]
    for friend in friends:
        pl.semaphore_signal(barrier, inc=1, device_id=friend, device_id_type=MESH)

    def remote(src, dst, send, recv, to):
        return pltpu.make_async_remote_copy(
            src_ref=src, dst_ref=dst, send_sem=send, recv_sem=recv, device_id=to, device_id_type=MESH
        )

    sub = iota((16, rows), 0)
    wanted = jnp.full((16, rows), -1, jnp.int32)
    for r in range(4):
        tag = jnp.int32(0)
        for l in range(LANGS):
            tag = tag + jnp.where(order[l] == chips[r], l, 0)
        wanted = jnp.where(sub == r, tag, wanted)
    mask = wanted == jnp.broadcast_to(tags[...], (16, rows))
    before = jnp.where(iota((rows, rows), 0) < iota((rows, rows), 1), 1.0, 0.0).astype(BF16)
    rank = dot(jnp.where(mask, 1.0, 0.0).astype(BF16), before, (1, 0))
    rank = jnp.where(mask, rank, -1000.0).astype(jnp.int32)
    meta = jnp.where(
        sub == 0,
        jnp.broadcast_to(words[...].astype(F32), (16, rows)),
        jnp.where(sub == 1, jnp.broadcast_to(weights[...].astype(F32), (16, rows)), 0.0),
    ).astype(BF16)

    def slots(r, height):
        return iota((height, rows), 0) == jnp.broadcast_to(rank[r : r + 1], (height, rows))

    spans = [pl.ds(r * tall, tall) for r in range(4)]
    for r in range(4):
        slot = iota((tall, rows), 0)
        key = jnp.broadcast_to(rank[r : r + 1], (tall, rows))
        pick_lo[spans[r], :] = jnp.where(slot == key, 1.0, 0.0).astype(BF16)
        pick_hi[spans[r], :] = jnp.where(slot == key + cap, 1.0, 0.0).astype(BF16)
        here = dot(meta, jnp.where(slots(r, rows), 1.0, 0.0).astype(BF16), (1, 1)).astype(BF16)
        if r:
            send_meta[r] = here
        else:
            got_meta[0] = here

    pl.semaphore_wait(barrier, len(friends))

    def part(ref, i):
        row = pl.multiple_of((BLOCK // 2) * core + 16 * lax.div(i, 2), 16)
        col = pl.multiple_of(half * lax.rem(i, 2), 128)
        return ref.at[pl.ds(row, 16), pl.ds(col, half)]

    def up(src, i):
        return remote(part(src, i), part(head_here, i), up_s.at[i], head_r.at[i], (dp, lax.rem(z + 1, LANGS)))

    def down(src, i):
        return remote(
            part(src, i), part(head_here, i), down_s.at[i], head_r.at[i], (dp, lax.rem(z + LANGS - 1, LANGS))
        )

    def to_twin(i):
        return remote(part(head_here, i), part(head_here, i), twin_s.at[i], twin_r.at[i], twin)

    goes_up = (z >= own) & (z < last)
    goes_down = (z <= own) & (z > 0)
    is_source = z == own

    @pl.when(is_source)
    def _():
        @pl.loop(0, PARTS)
        def _(i):
            @pl.when(z < last)
            def _():
                up(block, i).start()

            @pl.when(z > 0)
            def _():
                down(block, i).start()

    row_copies = {}
    for r in (3, 1, 2, 0):
        target = send_rows if r else got_rows

        @pl.loop(0, steps)
        def _(j, r=r, target=target):
            lo = pl.ds(pl.multiple_of(j * step, 128), step)
            hi = pl.ds(pl.multiple_of(half + j * step, 128), step)
            target[spans[r], lo] = (
                dot(pick_lo[spans[r], :], states[:, lo], (1, 0)) + dot(pick_hi[spans[r], :], states[:, hi], (1, 0))
            ).astype(BF16)

        if r:
            row_copies[r] = (
                remote(send_meta.at[r], got_meta.at[r], meta_s.at[r - 1], meta_r.at[r - 1], plane[r]),
                remote(
                    send_rows.at[spans[r], :], got_rows.at[spans[r], :], row_s.at[r - 1], row_r.at[r - 1], plane[r]
                ),
            )
            for copy in row_copies[r]:
                copy.start()

    @pl.when(is_source)
    def _():
        head_here[...] = block[...]

    @pl.when(jnp.logical_not(is_source))
    def _():
        @pl.loop(0, PARTS)
        def _(i):
            up(head_here, i).wait_recv()

            @pl.when(goes_up)
            def _():
                up(head_here, i).start()

            @pl.when(goes_down)
            def _():
                down(head_here, i).start()

            to_twin(i).start()

        @pl.loop(0, PARTS)
        def _(i):
            to_twin(i).wait_recv()

    for r in (1, 2, 3):
        for copy in row_copies[r]:
            copy.wait_recv()

    first = dot(got_rows[...], head_here[:, :half], (1, 1)).reshape(4, tall, BLOCK)
    second = dot(got_rows[...], head_here[:, half:], (1, 1)).reshape(4, tall, BLOCK)
    eye = jnp.where(iota((cap, BLOCK), 0) == iota((cap, BLOCK), 1), 1.0, 0.0)
    lane = iota((cap, BLOCK), 1)
    empty = jnp.zeros((cap, BLOCK), F32)
    for r in range(4):
        logits = first[r, :cap] + second[r, cap:]
        facts = dot(eye.astype(BF16), got_meta[r], (1, 1))
        hit = lane == facts[:, 0:1].astype(jnp.int32)
        peak = jnp.max(logits, axis=1, keepdims=True)
        total = peak + jnp.log(jnp.sum(jnp.exp(logits - peak), axis=1, keepdims=True))
        picked = jnp.sum(jnp.where(hit, logits, 0.0), axis=1, keepdims=True)
        losses = jnp.sum(jnp.where(eye > 0.0, total - picked, 0.0), axis=0, keepdims=True)
        losses = jnp.broadcast_to(losses, (8, BLOCK))
        if r:
            send_loss[r] = losses
        else:
            got_loss[0] = losses
        grads = facts[:, 1:2] * (jnp.exp(logits - total) - jnp.where(hit, 1.0, 0.0))
        grads_lo[spans[r], :] = jnp.concatenate([grads, empty], axis=0).astype(BF16)
        grads_hi[spans[r], :] = jnp.concatenate([empty, grads], axis=0).astype(BF16)

    @pl.loop(0, steps)
    def _(j):
        lo = pl.ds(pl.multiple_of(j * step, 128), step)
        hi = pl.ds(pl.multiple_of(half + j * step, 128), step)
        term[:, lo] = dot(grads_lo[...], got_rows[:, lo], (0, 0))
        term[:, hi] = dot(grads_hi[...], got_rows[:, lo], (0, 0))

    def words_of(r, which):
        return pl.ds(pl.multiple_of(chips[r] * 2 * words_each + which * words_each, 16), words_each)

    for r in range(4):
        pair_send[r] = term[words_of(r, 1 - core), :].astype(BF16)
    pair = remote(pair_send, pair_got, pair_s, pair_r, twin)
    pair.start()

    back_copies = {}

    def give_back(r):
        target = send_back if r else got_back

        @pl.loop(0, steps)
        def _(j):
            lo = pl.ds(pl.multiple_of(j * step, 128), step)
            hi = pl.ds(pl.multiple_of(half + j * step, 128), step)
            target[spans[r], lo] = (
                dot(grads_lo[spans[r], :], head_here[:, lo], (1, 0))
                + dot(grads_hi[spans[r], :], head_here[:, hi], (1, 0))
            ).astype(BF16)

        if r:
            back_copies[r] = (
                remote(send_loss.at[r], got_loss.at[r], loss_s.at[r - 1], loss_r.at[r - 1], plane[r]),
                remote(
                    send_back.at[spans[r], :], got_back.at[spans[r], :], back_s.at[r - 1], back_r.at[r - 1], plane[r]
                ),
            )
            for copy in back_copies[r]:
                copy.start()

    give_back(3)
    pair.wait_recv()
    plane_copies = {}
    for r in (3, 1, 2, 0):
        whole = (term[words_of(r, core), :] + pair_got[r].astype(F32)).astype(BF16)
        if r:
            plane_send[r] = whole
            plane_copies[r] = remote(
                plane_send.at[r], plane_got.at[r], plane_s.at[r - 1], plane_r.at[r - 1], plane[r]
            )
            plane_copies[r].start()
        else:
            plane_got[0] = whole
    for r in (1, 2, 0):
        give_back(r)
    for r in (1, 2, 3):
        plane_copies[r].wait_recv()

    def place_of(chip):
        return 2 * lax.rem(lax.div(chip, 2) + y, 2) + lax.rem(lax.rem(chip, 2) + x, 2)

    line_copies = []
    for d in range(1, LANGS):
        copy = remote(
            plane_got.at[place_of(line[d][1])], line_got.at[d - 1], line_s.at[d - 1], line_r.at[d - 1], line[d]
        )
        copy.start()
        line_copies.append(copy)

    for r in (1, 2, 3):
        for copy in back_copies[r]:
            copy.wait_recv()

    @pl.loop(0, steps)
    def _(j):
        lo = pl.ds(pl.multiple_of(j * step, 128), step)
        hi = pl.ds(pl.multiple_of(half + j * step, 128), step)
        state_out[:, lo] = dot(pick_lo[...], got_back[:, lo], (0, 0)).astype(BF16)
        state_out[:, hi] = dot(pick_hi[...], got_back[:, lo], (0, 0)).astype(BF16)

    square = iota((rows, rows), 0) == iota((rows, rows), 1)
    loss = jnp.zeros((1, rows), F32)
    for r in range(4):
        column = jnp.sum(
            jnp.where(square, jnp.broadcast_to(got_loss[r, 0:1, :], (rows, rows)), 0.0), axis=1, keepdims=True
        )
        loss = loss + jnp.sum(jnp.where(slots(r, rows), column, 0.0), axis=0, keepdims=True)
    loss_out[...] = loss

    for copy in line_copies:
        copy.wait_recv()
    head_out[0] = (
        plane_got[place_of(z)].astype(F32)
        + line_got[0].astype(F32)
        + line_got[1].astype(F32)
        + line_got[2].astype(F32)
    )

    for r in (1, 2, 3):
        for copy in (*row_copies[r], *back_copies[r], plane_copies[r]):
            copy.wait_send()
    pair.wait_send()
    for copy in line_copies:
        copy.wait_send()

    @pl.loop(0, PARTS)
    def _(i):
        @pl.when(goes_up)
        def _():
            up(head_here, i).wait_send()

        @pl.when(goes_down)
        def _():
            down(head_here, i).wait_send()

        @pl.when(jnp.logical_not(is_source))
        def _():
            to_twin(i).wait_send()


def routed(final_states, head_blocks, block_order, row_tags, target_word, row_weight):
    rows, width = final_states.shape
    cap = rows * 5 // 16
    half = width // 2
    stack = LANGS * 2 * cap
    share = BLOCK // (2 * LANGS)
    vmem = pl.BlockSpec(memory_space=pltpu.VMEM)
    dma = pltpu.SemaphoreType.DMA
    loss, state_grad, head_grad = pl.pallas_call(
        routed_kernel,
        out_shape=(
            jax.ShapeDtypeStruct((1, rows), F32),
            jax.ShapeDtypeStruct((rows, width), BF16),
            jax.ShapeDtypeStruct((1, share, width), F32),
        ),
        in_specs=[pl.BlockSpec(memory_space=pltpu.SMEM)] + [vmem] * 5,
        out_specs=(vmem, vmem, vmem),
        scratch_shapes=[
            pltpu.VMEM((BLOCK, width), BF16),
            pltpu.VMEM((stack, half), BF16),
            pltpu.VMEM((stack, half), BF16),
            pltpu.VMEM((LANGS, 16, rows), BF16),
            pltpu.VMEM((LANGS, 16, rows), BF16),
            pltpu.VMEM((stack, half), BF16),
            pltpu.VMEM((stack, half), BF16),
            pltpu.VMEM((LANGS, 8, BLOCK), F32),
            pltpu.VMEM((LANGS, 8, BLOCK), F32),
            pltpu.VMEM((stack, rows), BF16),
            pltpu.VMEM((stack, rows), BF16),
            pltpu.VMEM((stack, BLOCK), BF16),
            pltpu.VMEM((stack, BLOCK), BF16),
            pltpu.VMEM((BLOCK, width), F32),
            pltpu.VMEM((LANGS, share, width), BF16),
            pltpu.VMEM((LANGS, share, width), BF16),
            pltpu.VMEM((LANGS, share, width), BF16),
            pltpu.VMEM((LANGS, share, width), BF16),
            pltpu.VMEM((LANGS - 1, share, width), BF16),
            dma((3,)), dma((3,)), dma((3,)), dma((3,)),
            dma((3,)), dma((3,)), dma((3,)), dma((3,)),
            dma, dma, dma((3,)), dma((3,)),
            dma((3,)), dma((3,)),
            dma((PARTS,)), dma((PARTS,)), dma((PARTS,)), dma((PARTS,)), dma((PARTS,)),
        ],
        compiler_params=pltpu.CompilerParams(
            collective_id=0, has_side_effects=True, vmem_limit_bytes=40 * 1024 * 1024
        ),
        name="routed",
    )(
        block_order,
        row_tags.reshape(1, rows),
        target_word.reshape(1, rows),
        row_weight.reshape(1, rows),
        final_states,
        head_blocks.reshape(BLOCK, width),
    )
    return loss.reshape(rows), state_grad, head_grad


def shards(final_states, head_blocks, block_order, row_tags, target_word, row_weight):
    shard_count = lax.axis_size("vocab")
    rows_here = final_states.shape[0]
    short_len = shard_count // LANGS
    capacity = rows_here * 5 // 16
    block_ids = jnp.arange(shard_count, dtype=jnp.int32)
    placed = jnp.sum(
        block_ids[:, None] * (block_order[:, None] == block_ids[None, :]).astype(jnp.int32), axis=0
    )
    owner_tag = placed // short_len
    owner_slot = placed % short_len
    tag_ids = jnp.arange(LANGS, dtype=jnp.int32)
    tag_onehot = (row_tags[:, None] == tag_ids[None, :]).astype(jnp.int32)
    row_rank = jnp.sum((jnp.cumsum(tag_onehot, axis=0) - 1) * tag_onehot, axis=1)
    routed = owner_tag[:, None] == row_tags[None, :]
    slot_ids = jnp.arange(capacity, dtype=jnp.int32)
    chosen = routed[:, None, :] & (row_rank[None, None, :] == slot_ids[None, :, None])
    chosen_int = chosen.astype(jnp.int32)
    slot_used = jnp.sum(chosen_int, axis=2) > 0
    row_ids = jnp.arange(rows_here, dtype=jnp.int32)
    slot_row = jnp.sum(chosen_int * row_ids[None, None, :], axis=2)
    sent_rows = jnp.where(
        slot_used[:, :, None], jnp.take(final_states, slot_row, axis=0), jnp.zeros((), jnp.bfloat16)
    )
    local_word = jnp.where(
        target_word[None, :] // BLOCK == owner_slot[:, None], target_word[None, :] % BLOCK, -1
    )
    slot_word = jnp.sum(chosen_int * (local_word[:, None, :] + 1), axis=2) - 1
    slot_label = jnp.where(slot_used, slot_row, -1)
    slot_weight = jnp.sum(
        jnp.where(chosen, row_weight.astype(jnp.float32)[None, None, :], 0.0), axis=2
    ).astype(jnp.bfloat16)
    got_rows, got_label, got_word, got_weight = (
        lax.all_to_all(sent_rows, "vocab", split_axis=0, concat_axis=0, tiled=True),
        lax.all_to_all(slot_label, "vocab", split_axis=0, concat_axis=0, tiled=True),
        lax.all_to_all(slot_word, "vocab", split_axis=0, concat_axis=0, tiled=True),
        lax.all_to_all(slot_weight, "vocab", split_axis=0, concat_axis=0, tiled=True),
    )
    own_block = head_blocks[0]
    logits = jnp.einsum("scd,wd->scw", got_rows, own_block, preferred_element_type=jnp.float32)
    word_ids = jnp.arange(BLOCK, dtype=jnp.int32)
    target_hit = word_ids[None, None, :] == got_word[:, :, None]
    slot_peak = jnp.max(logits, axis=2)
    slot_total = jnp.sum(jnp.exp(logits - slot_peak[:, :, None]), axis=2)
    slot_picked = jnp.sum(jnp.where(target_hit, logits, 0.0), axis=2)
    back_peak, back_total, back_picked = (
        lax.all_to_all(slot_peak, "vocab", split_axis=0, concat_axis=0, tiled=True),
        lax.all_to_all(slot_total, "vocab", split_axis=0, concat_axis=0, tiled=True),
        lax.all_to_all(slot_picked, "vocab", split_axis=0, concat_axis=0, tiled=True),
    )
    row_peak = jnp.take(back_peak, row_rank, axis=1)
    row_total = jnp.take(back_total, row_rank, axis=1)
    row_picked = jnp.take(back_picked, row_rank, axis=1)
    peak_max = jnp.max(jnp.where(routed, row_peak, -1e30), axis=0)
    summed = jnp.sum(
        jnp.where(routed, row_total * jnp.exp(row_peak - peak_max[None, :]), 0.0), axis=0
    )
    log_total = peak_max + jnp.log(summed)
    row_loss = log_total - jnp.sum(jnp.where(routed, row_picked, 0.0), axis=0)
    slot_lse = jnp.where(slot_used, jnp.take(log_total, slot_row), 0.0)
    got_lse = lax.all_to_all(slot_lse, "vocab", split_axis=0, concat_axis=0, tiled=True)
    slot_probs = jnp.exp(logits - got_lse[:, :, None])
    slot_grads = (
        got_weight.astype(jnp.float32)[:, :, None] * (slot_probs - target_hit.astype(jnp.float32))
    ).astype(jnp.bfloat16)
    part_grads = jnp.einsum(
        "scw,wd->scd", slot_grads, own_block, preferred_element_type=jnp.float32
    ).astype(jnp.bfloat16)
    back_grads = lax.all_to_all(part_grads, "vocab", split_axis=0, concat_axis=0, tiled=True)
    state_grad = jnp.einsum(
        "sct,scd->td", chosen.astype(jnp.bfloat16), back_grads, preferred_element_type=jnp.float32
    ).astype(jnp.bfloat16)
    head_term = jnp.einsum("scw,scd->wd", slot_grads, got_rows, preferred_element_type=jnp.float32)
    head_share = lax.psum_scatter(head_term, "dp", scatter_dimension=0, tiled=True)
    return (row_loss, state_grad, head_share[None])


def solution(mesh):
    one_each = mesh.shape["vocab"] == LANGS and mesh.shape["dp"] == 2 * LANGS
    return jax.shard_map(
        routed if one_each else shards,
        mesh=mesh,
        in_specs=(
            P(("dp", "vocab"), None),
            P("vocab", None, None),
            P(),
            P(("dp", "vocab")),
            P(("dp", "vocab")),
            P(("dp", "vocab")),
        ),
        out_specs=(P(("dp", "vocab")), P(("dp", "vocab"), None), P("vocab", "dp", None)),
        check_vma=False,
    )
```

```python
import jax
import jax.numpy as jnp
from jax import lax
from jax.experimental import pallas as pl
from jax.experimental.pallas import tpu as pltpu
from jax.sharding import PartitionSpec as P

BLOCK = 128
LANGS = 4
MESH = pl.DeviceIdType.MESH
F32 = jnp.float32
BF16 = jnp.bfloat16
BATCHES = 2


def dot(a, b, dims):
    return lax.dot_general(a, b, ((dims[:1], dims[1:]), ((), ())), preferred_element_type=F32)


def iota(shape, dim):
    return lax.broadcasted_iota(jnp.int32, shape, dim)


def slice_width(width):
    return 128 * (-(-width // (128 * LANGS)))


def sliced_kernel(
    order_in, tags_in, words_in, weights_in, states, block,
    loss_out, back_out, head_out,
    order, tags, words, weights, cols, head, owner, part_send, part_got, grads, spread,
    back_send, term, pair_send, pair_got, line_send, line_got, plane_send,
    small_s, own_s, tag_s, tag_r, head_s, head_r, twin_s, twin_r, row_s, row_r,
    part_s, part_r, grad_s, grad_r, back_s, back_r, pair_s, pair_r, line_s, line_r, plane_s, plane_r,
):
    rows, width = states.shape
    wide = slice_width(width)
    over = LANGS * wide - width
    batch = rows // BATCHES
    half = BLOCK // 2
    share = BLOCK // (2 * LANGS)

    dp, z = lax.axis_index("dp"), lax.axis_index("vocab")
    core = lax.rem(dp, 2)
    x = lax.rem(lax.div(dp, 2), 2)
    y = lax.div(dp, 4)
    chips = [(y if r < 2 else 1 - y) * 2 + (x if r % 2 == 0 else 1 - x) for r in range(4)]
    own = chips[0]
    plane = [(c * 2 + core, z) for c in chips]
    twin = (own * 2 + 1 - core, z)
    planes = [lax.rem(z + d, LANGS) for d in range(LANGS)]
    sources = [lax.rem(z + LANGS - d, LANGS) for d in range(LANGS)]

    def remote(src, dst, send, recv, to):
        return pltpu.make_async_remote_copy(
            src_ref=src, dst_ref=dst, send_sem=send, recv_sem=recv, device_id=to, device_id_type=MESH
        )

    def features(chip):
        return pl.ds(pl.multiple_of(jnp.minimum(chip * wide, width - wide), 128), wide)

    def span(b, r):
        return pl.ds((b * 4 + r) * batch, batch)

    def words_at(plane_id, first, count):
        return pl.ds(pl.multiple_of(plane_id * BLOCK + first, 16), count)

    barrier = pltpu.get_barrier_semaphore()
    friends = plane[1:] + [(dp, planes[d]) for d in range(1, LANGS)] + [twin]
    for friend in friends:
        pl.semaphore_signal(barrier, inc=1, device_id=friend, device_id_type=MESH)

    small = [
        pltpu.make_async_copy(order_in, order, small_s.at[0]),
        pltpu.make_async_copy(tags_in, tags.at[0], small_s.at[1]),
        pltpu.make_async_copy(words_in, words, small_s.at[2]),
        pltpu.make_async_copy(weights_in, weights, small_s.at[3]),
    ]
    mine = [pltpu.make_async_copy(block.at[:, features(own)], head.at[words_at(z, 0, BLOCK), :], own_s.at[BATCHES])]
    for b in range(BATCHES):
        here = states.at[pl.ds(b * batch, batch), features(own)]
        mine.append(pltpu.make_async_copy(here, cols.at[span(b, 0), :], own_s.at[b]))
    for copy in small + mine:
        copy.start()

    pl.semaphore_wait(barrier, len(friends))

    head_copies = []
    for d in (2, 1, 3):
        copy = remote(
            block.at[pl.ds(pl.multiple_of(half * core, 16), half), features(own)],
            head.at[words_at(z, half * core, half), :],
            head_s.at[d - 1], head_r.at[d - 1], (dp, planes[d]),
        )
        copy.start()
        head_copies.append(copy)
    tag_copies = []
    for r in (3, 1, 2):
        copy = remote(tags_in, tags.at[r], tag_s.at[r - 1], tag_r.at[r - 1], plane[r])
        copy.start()
        tag_copies.append(copy)
    row_copies = [[], []]
    for b in range(BATCHES):
        for r in (3, 1, 2):
            n = b * 3 + r - 1
            copy = remote(
                states.at[pl.ds(b * batch, batch), features(chips[r])],
                cols.at[span(b, r), :],
                row_s.at[n], row_r.at[n], plane[r],
            )
            copy.start()
            row_copies[b].append(copy)

    for copy in small:
        copy.wait()
    square = iota((rows, rows), 0) == iota((rows, rows), 1)
    lane = iota((rows, BLOCK), 1)

    def column(values):
        wide_values = jnp.broadcast_to(values, (rows, rows))
        return jnp.sum(jnp.where(square, wide_values, 0.0), axis=1, keepdims=True)

    for copy in tag_copies:
        copy.wait_recv()
    for r in range(4):
        tag = column(tags[r].astype(F32))
        number = jnp.zeros((rows, 1), F32)
        for l in range(LANGS):
            number = jnp.where(tag == l, order[l].astype(F32), number)
        number = jnp.broadcast_to(number, (rows, BLOCK))
        for b in range(BATCHES):
            owner[span(b, r), :] = number[b * batch : (b + 1) * batch]
    target = column(words[...].astype(F32)).astype(jnp.int32)
    weight = column(weights[...].astype(F32))

    twin_copies = []
    for d in (1, 2, 3):
        remote(
            head.at[words_at(sources[d], half * core, half), :],
            head.at[words_at(sources[d], half * core, half), :],
            head_s.at[d - 1], head_r.at[d - 1], (dp, planes[d]),
        ).wait_recv()
        copy = remote(
            head.at[words_at(sources[d], half * core, half), :],
            head.at[words_at(sources[d], half * core, half), :],
            twin_s.at[d - 1], twin_r.at[d - 1], twin,
        )
        copy.start()
        twin_copies.append(copy)
    for copy in twin_copies:
        copy.wait_recv()
    mine[0].wait()

    part_copies = [[] for _ in range(BATCHES)]
    grad_copies = [[] for _ in range(BATCHES)]
    back_copies = []
    losses = []

    def whole(b):
        return pl.ds(b * 4 * batch, 4 * batch)

    def partial_logits(b):
        mine[1 + b].wait()
        for copy in row_copies[b]:
            copy.wait_recv()

        if over:
            @pl.when(own == LANGS - 1)
            def _():
                cols[whole(b), :over] = jnp.zeros((4 * batch, over), BF16)

        every = dot(cols[whole(b), :], head[...], (1, 1))
        number = owner[whole(b), :]
        kept = jnp.zeros((4 * batch, BLOCK), F32)
        for n in range(LANGS):
            kept = jnp.where(number == n, every[:, n * BLOCK : (n + 1) * BLOCK], kept)
        part_got[span(b, 0), :] = kept[:batch]
        for r in (3, 1, 2):
            n = b * 3 + r - 1
            part_send[span(b, r), :] = kept[r * batch : (r + 1) * batch]
            copy = remote(part_send.at[span(b, r), :], part_got.at[span(b, r), :], part_s.at[n], part_r.at[n], plane[r])
            copy.start()
            part_copies[b].append(copy)

    def softmax_grads(b):
        for copy in part_copies[b]:
            copy.wait_recv()
        pick = slice(b * batch, (b + 1) * batch)
        logits = (part_got[span(b, 0), :] + part_got[span(b, 1), :]) + (
            part_got[span(b, 2), :] + part_got[span(b, 3), :]
        )
        hit = lane[pick] == target[pick]
        peak = jnp.max(logits, axis=1, keepdims=True)
        total = peak + jnp.log(jnp.sum(jnp.exp(logits - peak), axis=1, keepdims=True))
        losses.append(total - jnp.sum(jnp.where(hit, logits, 0.0), axis=1, keepdims=True))
        grads[span(b, 0), :] = (weight[pick] * (jnp.exp(logits - total) - jnp.where(hit, 1.0, 0.0))).astype(BF16)
        for r in (3, 1, 2):
            n = b * 3 + r - 1
            copy = remote(grads.at[span(b, 0), :], grads.at[span(b, r), :], grad_s.at[n], grad_r.at[n], plane[r])
            copy.start()
            grad_copies[b].append(copy)

    def spread_grads(b):
        for copy in grad_copies[b]:
            copy.wait_recv()
        number = owner[whole(b), :]
        values = grads[whole(b), :].astype(F32)
        for n in range(LANGS):
            spread[whole(b), pl.ds(n * BLOCK, BLOCK)] = jnp.where(number == n, values, 0.0).astype(BF16)

    def give_back(b):
        back_send[whole(b), :] = dot(spread[whole(b), :], head[...], (1, 0)).astype(BF16)
        for r in (3, 1, 2):
            n = b * 3 + r - 1
            copy = remote(
                back_send.at[span(b, r), :],
                back_out.at[own, pl.ds(b * batch, batch), :],
                back_s.at[n], back_r.at[n], plane[r],
            )
            copy.start()
            back_copies.append(copy)
        copy = pltpu.make_async_copy(
            back_send.at[span(b, 0), :], back_out.at[own, pl.ds(b * batch, batch), :], own_s.at[BATCHES + 1 + b]
        )
        copy.start()
        mine.append(copy)

    for b in range(BATCHES):
        partial_logits(b)
    for b in range(BATCHES):
        softmax_grads(b)
    for b in range(BATCHES):
        spread_grads(b)
        if b == 0:
            give_back(0)

    def mine_of(e, which):
        return pl.ds(pl.multiple_of(2 * share * e + share * which, 16), share)

    pair_copies = {}
    for d in (2, 1, 3, 0):
        picked = spread[:, pl.ds(pl.multiple_of(planes[d] * BLOCK, 128), BLOCK)]
        term[d] = dot(picked, cols[...], (0, 0))
        for e in range(LANGS):
            pair_send[d, pl.ds(e * share, share), :] = term[d, mine_of(e, 1 - core), :].astype(BF16)
        pair_copies[d] = remote(pair_send.at[d], pair_got.at[d], pair_s.at[d], pair_r.at[d], twin)
        pair_copies[d].start()

    line_copies = []

    def both(d, e):
        return term[d, mine_of(e, core), :] + pair_got[d, pl.ds(e * share, share), :].astype(F32)

    for d in (2, 1, 3):
        pair_copies[d].wait_recv()
        for e in range(LANGS):
            line_send[d - 1, pl.ds(e * share, share), :] = both(d, e).astype(BF16)
        copy = remote(
            line_send.at[d - 1], line_got.at[d - 1], line_s.at[d - 1], line_r.at[d - 1], (dp, planes[d])
        )
        copy.start()
        line_copies.append(copy)

    for b in range(1, BATCHES):
        give_back(b)

    loss = jnp.concatenate(losses, axis=0)
    loss_out[...] = jnp.sum(jnp.where(square, loss, 0.0), axis=0, keepdims=True)

    pair_copies[0].wait_recv()
    for copy in line_copies:
        copy.wait_recv()
    for e in range(LANGS):
        part = pl.ds(e * share, share)
        plane_send[e] = (
            (both(0, e) + line_got[0, part, :].astype(F32))
            + (line_got[1, part, :].astype(F32) + line_got[2, part, :].astype(F32))
        ).astype(BF16)
    plane_copies = []
    for r in (3, 1, 2):
        copy = remote(
            plane_send.at[chips[r]], head_out.at[own], plane_s.at[r - 1], plane_r.at[r - 1], plane[r]
        )
        copy.start()
        plane_copies.append(copy)
    copy = pltpu.make_async_copy(plane_send.at[own], head_out.at[own], own_s.at[2 * BATCHES + 1])
    copy.start()
    mine.append(copy)

    for copy in back_copies + plane_copies:
        copy.wait_recv()
    for copy in mine[1 + BATCHES :]:
        copy.wait()
    everything = (
        head_copies + tag_copies + twin_copies + back_copies + line_copies + plane_copies
        + [c for group in row_copies + part_copies + grad_copies for c in group]
        + [pair_copies[d] for d in range(LANGS)]
    )
    for copy in everything:
        copy.wait_send()


def joined_kernel(loss_in, back_in, head_in, loss_out, state_out, head_out, head_got, head_done, sems):
    wide = back_in.shape[2]
    over = LANGS * wide - state_out.shape[1]
    fetch = pltpu.make_async_copy(head_in, head_got, sems.at[0])
    fetch.start()
    copies = [pltpu.make_async_copy(loss_in, loss_out, sems.at[1])]
    for e in range(LANGS):
        skip = over if e == LANGS - 1 else 0
        here = pl.ds(e * wide, wide - skip)
        copies.append(
            pltpu.make_async_copy(back_in.at[e, :, pl.ds(skip, wide - skip)], state_out.at[:, here], sems.at[2 + e])
        )
    for copy in copies:
        copy.start()
    fetch.wait()
    for e in range(LANGS):
        skip = over if e == LANGS - 1 else 0
        head_done[0, :, pl.ds(e * wide, wide - skip)] = head_got[e, :, pl.ds(skip, wide - skip)].astype(F32)
    store = pltpu.make_async_copy(head_done, head_out, sems.at[2 + LANGS])
    store.start()
    for copy in copies:
        copy.wait()
    store.wait()


def sliced(final_states, head_blocks, block_order, row_tags, target_word, row_weight):
    rows, width = final_states.shape
    wide = slice_width(width)
    over = LANGS * wide - width
    share = BLOCK // (2 * LANGS)
    half = BLOCK // 2
    group = LANGS * rows
    hbm = pl.BlockSpec(memory_space=pl.ANY)
    vmem = pl.BlockSpec(memory_space=pltpu.VMEM)
    dma = pltpu.SemaphoreType.DMA
    three, batches = dma((3,)), dma((3 * BATCHES,))
    loss, back, head = pl.pallas_call(
        sliced_kernel,
        out_shape=(
            jax.ShapeDtypeStruct((1, rows), F32),
            jax.ShapeDtypeStruct((LANGS, rows, wide), BF16),
            jax.ShapeDtypeStruct((LANGS, share, wide), BF16),
        ),
        in_specs=[hbm] * 6,
        out_specs=(vmem, hbm, hbm),
        scratch_shapes=[
            pltpu.SMEM((LANGS,), jnp.int32),
            pltpu.VMEM((LANGS, 1, rows), jnp.int32),
            pltpu.VMEM((1, rows), jnp.int32),
            pltpu.VMEM((1, rows), BF16),
            pltpu.VMEM((group, wide), BF16),
            pltpu.VMEM((LANGS * BLOCK, wide), BF16),
            pltpu.VMEM((group, BLOCK), F32),
            pltpu.VMEM((group, BLOCK), F32),
            pltpu.VMEM((group, BLOCK), F32),
            pltpu.VMEM((group, BLOCK), BF16),
            pltpu.VMEM((group, LANGS * BLOCK), BF16),
            pltpu.VMEM((group, wide), BF16),
            pltpu.VMEM((LANGS, BLOCK, wide), F32),
            pltpu.VMEM((LANGS, half, wide), BF16),
            pltpu.VMEM((LANGS, half, wide), BF16),
            pltpu.VMEM((LANGS - 1, half, wide), BF16),
            pltpu.VMEM((LANGS - 1, half, wide), BF16),
            pltpu.VMEM((LANGS, share, wide), BF16),
            dma((4,)), dma((2 * BATCHES + 2,)), three, three, three, three, three, three, batches, batches,
            batches, batches, batches, batches, batches, batches, dma((LANGS,)), dma((LANGS,)),
            three, three, three, three,
        ],
        compiler_params=pltpu.CompilerParams(
            collective_id=0, has_side_effects=True, vmem_limit_bytes=60 * 1024 * 1024
        ),
        name="sliced",
    )(
        block_order,
        row_tags.reshape(1, rows),
        target_word.reshape(1, rows),
        row_weight.reshape(1, rows),
        final_states,
        head_blocks.reshape(BLOCK, width),
    )
    loss, state_grad, head_grad = pl.pallas_call(
        joined_kernel,
        out_shape=(
            jax.ShapeDtypeStruct((1, rows), F32),
            jax.ShapeDtypeStruct((rows, width), BF16),
            jax.ShapeDtypeStruct((1, share, width), F32),
        ),
        in_specs=[hbm] * 3,
        out_specs=[hbm] * 3,
        scratch_shapes=[
            pltpu.VMEM((LANGS, share, wide), BF16),
            pltpu.VMEM((1, share, width), F32),
            dma((LANGS + 3,)),
        ],
        compiler_params=pltpu.CompilerParams(vmem_limit_bytes=60 * 1024 * 1024),
        name="joined",
    )(loss, back, head)
    return loss.reshape(rows), state_grad, head_grad


def shards(final_states, head_blocks, block_order, row_tags, target_word, row_weight):
    shard_count = lax.axis_size("vocab")
    rows_here = final_states.shape[0]
    short_len = shard_count // LANGS
    capacity = rows_here * 5 // 16
    block_ids = jnp.arange(shard_count, dtype=jnp.int32)
    placed = jnp.sum(
        block_ids[:, None] * (block_order[:, None] == block_ids[None, :]).astype(jnp.int32), axis=0
    )
    owner_tag = placed // short_len
    owner_slot = placed % short_len
    tag_ids = jnp.arange(LANGS, dtype=jnp.int32)
    tag_onehot = (row_tags[:, None] == tag_ids[None, :]).astype(jnp.int32)
    row_rank = jnp.sum((jnp.cumsum(tag_onehot, axis=0) - 1) * tag_onehot, axis=1)
    routed = owner_tag[:, None] == row_tags[None, :]
    slot_ids = jnp.arange(capacity, dtype=jnp.int32)
    chosen = routed[:, None, :] & (row_rank[None, None, :] == slot_ids[None, :, None])
    chosen_int = chosen.astype(jnp.int32)
    slot_used = jnp.sum(chosen_int, axis=2) > 0
    row_ids = jnp.arange(rows_here, dtype=jnp.int32)
    slot_row = jnp.sum(chosen_int * row_ids[None, None, :], axis=2)
    sent_rows = jnp.where(
        slot_used[:, :, None], jnp.take(final_states, slot_row, axis=0), jnp.zeros((), jnp.bfloat16)
    )
    local_word = jnp.where(
        target_word[None, :] // BLOCK == owner_slot[:, None], target_word[None, :] % BLOCK, -1
    )
    slot_word = jnp.sum(chosen_int * (local_word[:, None, :] + 1), axis=2) - 1
    slot_label = jnp.where(slot_used, slot_row, -1)
    slot_weight = jnp.sum(
        jnp.where(chosen, row_weight.astype(jnp.float32)[None, None, :], 0.0), axis=2
    ).astype(jnp.bfloat16)
    got_rows, got_label, got_word, got_weight = (
        lax.all_to_all(sent_rows, "vocab", split_axis=0, concat_axis=0, tiled=True),
        lax.all_to_all(slot_label, "vocab", split_axis=0, concat_axis=0, tiled=True),
        lax.all_to_all(slot_word, "vocab", split_axis=0, concat_axis=0, tiled=True),
        lax.all_to_all(slot_weight, "vocab", split_axis=0, concat_axis=0, tiled=True),
    )
    own_block = head_blocks[0]
    logits = jnp.einsum("scd,wd->scw", got_rows, own_block, preferred_element_type=jnp.float32)
    word_ids = jnp.arange(BLOCK, dtype=jnp.int32)
    target_hit = word_ids[None, None, :] == got_word[:, :, None]
    slot_peak = jnp.max(logits, axis=2)
    slot_total = jnp.sum(jnp.exp(logits - slot_peak[:, :, None]), axis=2)
    slot_picked = jnp.sum(jnp.where(target_hit, logits, 0.0), axis=2)
    back_peak, back_total, back_picked = (
        lax.all_to_all(slot_peak, "vocab", split_axis=0, concat_axis=0, tiled=True),
        lax.all_to_all(slot_total, "vocab", split_axis=0, concat_axis=0, tiled=True),
        lax.all_to_all(slot_picked, "vocab", split_axis=0, concat_axis=0, tiled=True),
    )
    row_peak = jnp.take(back_peak, row_rank, axis=1)
    row_total = jnp.take(back_total, row_rank, axis=1)
    row_picked = jnp.take(back_picked, row_rank, axis=1)
    peak_max = jnp.max(jnp.where(routed, row_peak, -1e30), axis=0)
    summed = jnp.sum(
        jnp.where(routed, row_total * jnp.exp(row_peak - peak_max[None, :]), 0.0), axis=0
    )
    log_total = peak_max + jnp.log(summed)
    row_loss = log_total - jnp.sum(jnp.where(routed, row_picked, 0.0), axis=0)
    slot_lse = jnp.where(slot_used, jnp.take(log_total, slot_row), 0.0)
    got_lse = lax.all_to_all(slot_lse, "vocab", split_axis=0, concat_axis=0, tiled=True)
    slot_probs = jnp.exp(logits - got_lse[:, :, None])
    slot_grads = (
        got_weight.astype(jnp.float32)[:, :, None] * (slot_probs - target_hit.astype(jnp.float32))
    ).astype(jnp.bfloat16)
    part_grads = jnp.einsum(
        "scw,wd->scd", slot_grads, own_block, preferred_element_type=jnp.float32
    ).astype(jnp.bfloat16)
    back_grads = lax.all_to_all(part_grads, "vocab", split_axis=0, concat_axis=0, tiled=True)
    state_grad = jnp.einsum(
        "sct,scd->td", chosen.astype(jnp.bfloat16), back_grads, preferred_element_type=jnp.float32
    ).astype(jnp.bfloat16)
    head_term = jnp.einsum("scw,scd->wd", slot_grads, got_rows, preferred_element_type=jnp.float32)
    head_share = lax.psum_scatter(head_term, "dp", scatter_dimension=0, tiled=True)
    return (row_loss, state_grad, head_share[None])


def solution(mesh):
    one_each = mesh.shape["vocab"] == LANGS and mesh.shape["dp"] == 2 * LANGS
    return jax.shard_map(
        sliced if one_each else shards,
        mesh=mesh,
        in_specs=(
            P(("dp", "vocab"), None),
            P("vocab", None, None),
            P(),
            P(("dp", "vocab")),
            P(("dp", "vocab")),
            P(("dp", "vocab")),
        ),
        out_specs=(P(("dp", "vocab")), P(("dp", "vocab"), None), P("vocab", "dp", None)),
        check_vma=False,
    )
```

```python
import jax
import jax.numpy as jnp
from jax import lax
from jax.experimental import pallas as pl
from jax.experimental.pallas import tpu as pltpu
from jax.sharding import PartitionSpec as P

BLOCK = 128
LANGS = 4
MESH = pl.DeviceIdType.MESH
F32 = jnp.float32
BF16 = jnp.bfloat16
BATCHES = 2


def dot(a, b, dims):
    return lax.dot_general(a, b, ((dims[:1], dims[1:]), ((), ())), preferred_element_type=F32)


def iota(shape, dim):
    return lax.broadcasted_iota(jnp.int32, shape, dim)


def slice_width(width):
    return 128 * (-(-width // (128 * LANGS)))


def sliced_kernel(
    order_in, tags_in, words_in, weights_in, states, block,
    loss_out, back_out, head_out,
    order, tags, words, weights, cols, head, owner, part_send, part_got, grads, spread,
    back_send, term, pair_send, pair_got, line_send, line_got, plane_send,
    small_s, own_s, tag_s, tag_r, head_s, head_r, twin_s, twin_r, row_s, row_r,
    part_s, part_r, grad_s, grad_r, back_s, back_r, pair_s, pair_r, line_s, line_r, plane_s, plane_r,
):
    rows, width = states.shape
    wide = slice_width(width)
    over = LANGS * wide - width
    batch = rows // BATCHES
    half = BLOCK // 2
    share = BLOCK // (2 * LANGS)

    dp, z = lax.axis_index("dp"), lax.axis_index("vocab")
    core = lax.rem(dp, 2)
    x = lax.rem(lax.div(dp, 2), 2)
    y = lax.div(dp, 4)
    chips = [(y if r < 2 else 1 - y) * 2 + (x if r % 2 == 0 else 1 - x) for r in range(4)]
    own = chips[0]
    plane = [(c * 2 + core, z) for c in chips]
    twin = (own * 2 + 1 - core, z)
    planes = [lax.rem(z + d, LANGS) for d in range(LANGS)]
    sources = [lax.rem(z + LANGS - d, LANGS) for d in range(LANGS)]

    def remote(src, dst, send, recv, to):
        return pltpu.make_async_remote_copy(
            src_ref=src, dst_ref=dst, send_sem=send, recv_sem=recv, device_id=to, device_id_type=MESH
        )

    def features(chip):
        return pl.ds(pl.multiple_of(jnp.minimum(chip * wide, width - wide), 128), wide)

    def span(b, r):
        return pl.ds((b * 4 + r) * batch, batch)

    def words_at(plane_id, first, count):
        return pl.ds(pl.multiple_of(plane_id * BLOCK + first, 16), count)

    barrier = pltpu.get_barrier_semaphore()
    friends = plane[1:] + [(dp, planes[d]) for d in range(1, LANGS)] + [twin]
    for friend in friends:
        pl.semaphore_signal(barrier, inc=1, device_id=friend, device_id_type=MESH)

    small = [
        pltpu.make_async_copy(order_in, order, small_s.at[0]),
        pltpu.make_async_copy(tags_in, tags.at[0], small_s.at[1]),
        pltpu.make_async_copy(words_in, words, small_s.at[2]),
        pltpu.make_async_copy(weights_in, weights, small_s.at[3]),
    ]
    mine = [pltpu.make_async_copy(block.at[:, features(own)], head.at[words_at(z, 0, BLOCK), :], own_s.at[BATCHES])]
    for b in range(BATCHES):
        here = states.at[pl.ds(b * batch, batch), features(own)]
        mine.append(pltpu.make_async_copy(here, cols.at[span(b, 0), :], own_s.at[b]))
    for copy in small + mine:
        copy.start()

    pl.semaphore_wait(barrier, len(friends))

    head_copies = []
    for d in (2, 1, 3):
        copy = remote(
            block.at[pl.ds(pl.multiple_of(half * core, 16), half), features(own)],
            head.at[words_at(z, half * core, half), :],
            head_s.at[d - 1], head_r.at[d - 1], (dp, planes[d]),
        )
        copy.start()
        head_copies.append(copy)
    tag_copies = []
    for r in (3, 1, 2):
        copy = remote(tags_in, tags.at[r], tag_s.at[r - 1], tag_r.at[r - 1], plane[r])
        copy.start()
        tag_copies.append(copy)
    row_copies = [[], []]
    for b in range(BATCHES):
        for r in (3, 1, 2):
            n = b * 3 + r - 1
            copy = remote(
                states.at[pl.ds(b * batch, batch), features(chips[r])],
                cols.at[span(b, r), :],
                row_s.at[n], row_r.at[n], plane[r],
            )
            copy.start()
            row_copies[b].append(copy)

    for copy in small:
        copy.wait()
    square = iota((rows, rows), 0) == iota((rows, rows), 1)
    lane = iota((rows, BLOCK), 1)

    def column(values):
        wide_values = jnp.broadcast_to(values, (rows, rows))
        return jnp.sum(jnp.where(square, wide_values, 0.0), axis=1, keepdims=True)

    for copy in tag_copies:
        copy.wait_recv()
    for r in range(4):
        tag = column(tags[r].astype(F32))
        number = jnp.zeros((rows, 1), F32)
        for l in range(LANGS):
            number = jnp.where(tag == l, order[l].astype(F32), number)
        number = jnp.broadcast_to(number, (rows, BLOCK))
        for b in range(BATCHES):
            owner[span(b, r), :] = number[b * batch : (b + 1) * batch]
    target = column(words[...].astype(F32)).astype(jnp.int32)
    weight = column(weights[...].astype(F32))

    twin_copies = []
    for d in (1, 2, 3):
        remote(
            head.at[words_at(sources[d], half * core, half), :],
            head.at[words_at(sources[d], half * core, half), :],
            head_s.at[d - 1], head_r.at[d - 1], (dp, planes[d]),
        ).wait_recv()
        copy = remote(
            head.at[words_at(sources[d], half * core, half), :],
            head.at[words_at(sources[d], half * core, half), :],
            twin_s.at[d - 1], twin_r.at[d - 1], twin,
        )
        copy.start()
        twin_copies.append(copy)
    for copy in twin_copies:
        copy.wait_recv()
    mine[0].wait()

    part_copies = [[] for _ in range(BATCHES)]
    grad_copies = [[] for _ in range(BATCHES)]
    back_copies = []
    losses = []

    def whole(b):
        return pl.ds(b * 4 * batch, 4 * batch)

    def partial_logits(b):
        mine[1 + b].wait()
        for copy in row_copies[b]:
            copy.wait_recv()

        if over:
            @pl.when(own == LANGS - 1)
            def _():
                cols[whole(b), :over] = jnp.zeros((4 * batch, over), BF16)

        every = dot(cols[whole(b), :], head[...], (1, 1))
        number = owner[whole(b), :]
        kept = jnp.zeros((4 * batch, BLOCK), F32)
        for n in range(LANGS):
            kept = jnp.where(number == n, every[:, n * BLOCK : (n + 1) * BLOCK], kept)
        part_got[span(b, 0), :] = kept[:batch]
        for r in (3, 1, 2):
            n = b * 3 + r - 1
            part_send[span(b, r), :] = kept[r * batch : (r + 1) * batch]
            copy = remote(part_send.at[span(b, r), :], part_got.at[span(b, r), :], part_s.at[n], part_r.at[n], plane[r])
            copy.start()
            part_copies[b].append(copy)

    def softmax_grads(b):
        for copy in part_copies[b]:
            copy.wait_recv()
        pick = slice(b * batch, (b + 1) * batch)
        logits = (part_got[span(b, 0), :] + part_got[span(b, 1), :]) + (
            part_got[span(b, 2), :] + part_got[span(b, 3), :]
        )
        hit = lane[pick] == target[pick]
        peak = jnp.max(logits, axis=1, keepdims=True)
        total = peak + jnp.log(jnp.sum(jnp.exp(logits - peak), axis=1, keepdims=True))
        losses.append(total - jnp.sum(jnp.where(hit, logits, 0.0), axis=1, keepdims=True))
        grads[span(b, 0), :] = (weight[pick] * (jnp.exp(logits - total) - jnp.where(hit, 1.0, 0.0))).astype(BF16)
        for r in (3, 1, 2):
            n = b * 3 + r - 1
            copy = remote(grads.at[span(b, 0), :], grads.at[span(b, r), :], grad_s.at[n], grad_r.at[n], plane[r])
            copy.start()
            grad_copies[b].append(copy)

    def spread_grads(b):
        for copy in grad_copies[b]:
            copy.wait_recv()
        number = owner[whole(b), :]
        values = grads[whole(b), :].astype(F32)
        for n in range(LANGS):
            spread[whole(b), pl.ds(n * BLOCK, BLOCK)] = jnp.where(number == n, values, 0.0).astype(BF16)

    def give_back(b):
        back_send[whole(b), :] = dot(spread[whole(b), :], head[...], (1, 0)).astype(BF16)
        for r in (3, 1, 2):
            n = b * 3 + r - 1
            copy = remote(
                back_send.at[span(b, r), :],
                back_out.at[own, pl.ds(b * batch, batch), :],
                back_s.at[n], back_r.at[n], plane[r],
            )
            copy.start()
            back_copies.append(copy)
        copy = pltpu.make_async_copy(
            back_send.at[span(b, 0), :], back_out.at[own, pl.ds(b * batch, batch), :], own_s.at[BATCHES + 1 + b]
        )
        copy.start()
        mine.append(copy)

    for b in range(BATCHES):
        partial_logits(b)
    for b in range(BATCHES):
        softmax_grads(b)
    for b in range(BATCHES):
        spread_grads(b)
        if b == 0:
            give_back(0)

    def mine_of(e, which):
        return pl.ds(pl.multiple_of(2 * share * e + share * which, 16), share)

    pair_copies = {}
    for d in (2, 1, 3, 0):
        picked = spread[:, pl.ds(pl.multiple_of(planes[d] * BLOCK, 128), BLOCK)]
        term[d] = dot(picked, cols[...], (0, 0))
        for e in range(LANGS):
            pair_send[d, pl.ds(e * share, share), :] = term[d, mine_of(e, 1 - core), :].astype(BF16)
        pair_copies[d] = remote(pair_send.at[d], pair_got.at[d], pair_s.at[d], pair_r.at[d], twin)
        pair_copies[d].start()

    line_copies = []

    def both(d, e):
        return term[d, mine_of(e, core), :] + pair_got[d, pl.ds(e * share, share), :].astype(F32)

    for d in (2, 1, 3):
        pair_copies[d].wait_recv()
        for e in range(LANGS):
            line_send[d - 1, pl.ds(e * share, share), :] = both(d, e).astype(BF16)
        copy = remote(
            line_send.at[d - 1], line_got.at[d - 1], line_s.at[d - 1], line_r.at[d - 1], (dp, planes[d])
        )
        copy.start()
        line_copies.append(copy)

    for b in range(1, BATCHES):
        give_back(b)

    loss = jnp.concatenate(losses, axis=0)
    loss_out[...] = jnp.sum(jnp.where(square, loss, 0.0), axis=0, keepdims=True)

    pair_copies[0].wait_recv()
    for copy in line_copies:
        copy.wait_recv()
    for e in range(LANGS):
        part = pl.ds(e * share, share)
        plane_send[e] = (
            (both(0, e) + line_got[0, part, :].astype(F32))
            + (line_got[1, part, :].astype(F32) + line_got[2, part, :].astype(F32))
        ).astype(BF16)
    plane_copies = []
    for r in (3, 1, 2):
        copy = remote(
            plane_send.at[chips[r]], head_out.at[own], plane_s.at[r - 1], plane_r.at[r - 1], plane[r]
        )
        copy.start()
        plane_copies.append(copy)
    copy = pltpu.make_async_copy(plane_send.at[own], head_out.at[own], own_s.at[2 * BATCHES + 1])
    copy.start()
    mine.append(copy)

    for copy in back_copies + plane_copies:
        copy.wait_recv()
    for copy in mine[1 + BATCHES :]:
        copy.wait()
    everything = (
        head_copies + tag_copies + twin_copies + back_copies + line_copies + plane_copies
        + [c for group in row_copies + part_copies + grad_copies for c in group]
        + [pair_copies[d] for d in range(LANGS)]
    )
    for copy in everything:
        copy.wait_send()


def joined_kernel(
    loss_in, back_in, head_in, loss_out, state_out, head_out, loss_got, back_got, head_got, head_done, got, put
):
    wide = back_in.shape[2]
    over = LANGS * wide - state_out.shape[1]
    loads = [
        pltpu.make_async_copy(head_in, head_got, got.at[LANGS]),
        pltpu.make_async_copy(loss_in, loss_got, got.at[LANGS + 1]),
    ]
    loads += [pltpu.make_async_copy(back_in.at[e], back_got.at[e], got.at[e]) for e in range(LANGS)]
    for copy in loads:
        copy.start()
    skips = [over if e == LANGS - 1 else 0 for e in range(LANGS)]
    stores = []

    def store(src, dst, n):
        copy = pltpu.make_async_copy(src, dst, put.at[n])
        copy.start()
        stores.append(copy)

    loads[0].wait()
    for e, skip in enumerate(skips):
        head_done[0, :, pl.ds(e * wide, wide - skip)] = head_got[e, :, pl.ds(skip, wide - skip)].astype(F32)
    store(head_done, head_out, LANGS)
    loads[1].wait()
    store(loss_got, loss_out, LANGS + 1)
    for e, skip in enumerate(skips):
        loads[2 + e].wait()
        store(
            back_got.at[e, :, pl.ds(skip, wide - skip)], state_out.at[:, pl.ds(e * wide, wide - skip)], e
        )
    for copy in stores:
        copy.wait()


def sliced(final_states, head_blocks, block_order, row_tags, target_word, row_weight):
    rows, width = final_states.shape
    wide = slice_width(width)
    over = LANGS * wide - width
    share = BLOCK // (2 * LANGS)
    half = BLOCK // 2
    group = LANGS * rows
    hbm = pl.BlockSpec(memory_space=pl.ANY)
    vmem = pl.BlockSpec(memory_space=pltpu.VMEM)
    dma = pltpu.SemaphoreType.DMA
    three, batches = dma((3,)), dma((3 * BATCHES,))
    loss, back, head = pl.pallas_call(
        sliced_kernel,
        out_shape=(
            jax.ShapeDtypeStruct((1, rows), F32),
            jax.ShapeDtypeStruct((LANGS, rows, wide), BF16),
            jax.ShapeDtypeStruct((LANGS, share, wide), BF16),
        ),
        in_specs=[hbm] * 6,
        out_specs=(vmem, hbm, hbm),
        scratch_shapes=[
            pltpu.SMEM((LANGS,), jnp.int32),
            pltpu.VMEM((LANGS, 1, rows), jnp.int32),
            pltpu.VMEM((1, rows), jnp.int32),
            pltpu.VMEM((1, rows), BF16),
            pltpu.VMEM((group, wide), BF16),
            pltpu.VMEM((LANGS * BLOCK, wide), BF16),
            pltpu.VMEM((group, BLOCK), F32),
            pltpu.VMEM((group, BLOCK), F32),
            pltpu.VMEM((group, BLOCK), F32),
            pltpu.VMEM((group, BLOCK), BF16),
            pltpu.VMEM((group, LANGS * BLOCK), BF16),
            pltpu.VMEM((group, wide), BF16),
            pltpu.VMEM((LANGS, BLOCK, wide), F32),
            pltpu.VMEM((LANGS, half, wide), BF16),
            pltpu.VMEM((LANGS, half, wide), BF16),
            pltpu.VMEM((LANGS - 1, half, wide), BF16),
            pltpu.VMEM((LANGS - 1, half, wide), BF16),
            pltpu.VMEM((LANGS, share, wide), BF16),
            dma((4,)), dma((2 * BATCHES + 2,)), three, three, three, three, three, three, batches, batches,
            batches, batches, batches, batches, batches, batches, dma((LANGS,)), dma((LANGS,)),
            three, three, three, three,
        ],
        compiler_params=pltpu.CompilerParams(
            collective_id=0, has_side_effects=True, vmem_limit_bytes=60 * 1024 * 1024
        ),
        name="sliced",
    )(
        block_order,
        row_tags.reshape(1, rows),
        target_word.reshape(1, rows),
        row_weight.reshape(1, rows),
        final_states,
        head_blocks.reshape(BLOCK, width),
    )
    loss, state_grad, head_grad = pl.pallas_call(
        joined_kernel,
        out_shape=(
            jax.ShapeDtypeStruct((1, rows), F32),
            jax.ShapeDtypeStruct((rows, width), BF16),
            jax.ShapeDtypeStruct((1, share, width), F32),
        ),
        in_specs=[hbm] * 3,
        out_specs=[hbm] * 3,
        scratch_shapes=[
            pltpu.VMEM((1, rows), F32),
            pltpu.VMEM((LANGS, rows, wide), BF16),
            pltpu.VMEM((LANGS, share, wide), BF16),
            pltpu.VMEM((1, share, width), F32),
            dma((LANGS + 2,)),
            dma((LANGS + 2,)),
        ],
        compiler_params=pltpu.CompilerParams(vmem_limit_bytes=60 * 1024 * 1024),
        name="joined",
    )(loss, back, head)
    return loss.reshape(rows), state_grad, head_grad


def shards(final_states, head_blocks, block_order, row_tags, target_word, row_weight):
    shard_count = lax.axis_size("vocab")
    rows_here = final_states.shape[0]
    short_len = shard_count // LANGS
    capacity = rows_here * 5 // 16
    block_ids = jnp.arange(shard_count, dtype=jnp.int32)
    placed = jnp.sum(
        block_ids[:, None] * (block_order[:, None] == block_ids[None, :]).astype(jnp.int32), axis=0
    )
    owner_tag = placed // short_len
    owner_slot = placed % short_len
    tag_ids = jnp.arange(LANGS, dtype=jnp.int32)
    tag_onehot = (row_tags[:, None] == tag_ids[None, :]).astype(jnp.int32)
    row_rank = jnp.sum((jnp.cumsum(tag_onehot, axis=0) - 1) * tag_onehot, axis=1)
    routed = owner_tag[:, None] == row_tags[None, :]
    slot_ids = jnp.arange(capacity, dtype=jnp.int32)
    chosen = routed[:, None, :] & (row_rank[None, None, :] == slot_ids[None, :, None])
    chosen_int = chosen.astype(jnp.int32)
    slot_used = jnp.sum(chosen_int, axis=2) > 0
    row_ids = jnp.arange(rows_here, dtype=jnp.int32)
    slot_row = jnp.sum(chosen_int * row_ids[None, None, :], axis=2)
    sent_rows = jnp.where(
        slot_used[:, :, None], jnp.take(final_states, slot_row, axis=0), jnp.zeros((), jnp.bfloat16)
    )
    local_word = jnp.where(
        target_word[None, :] // BLOCK == owner_slot[:, None], target_word[None, :] % BLOCK, -1
    )
    slot_word = jnp.sum(chosen_int * (local_word[:, None, :] + 1), axis=2) - 1
    slot_label = jnp.where(slot_used, slot_row, -1)
    slot_weight = jnp.sum(
        jnp.where(chosen, row_weight.astype(jnp.float32)[None, None, :], 0.0), axis=2
    ).astype(jnp.bfloat16)
    got_rows, got_label, got_word, got_weight = (
        lax.all_to_all(sent_rows, "vocab", split_axis=0, concat_axis=0, tiled=True),
        lax.all_to_all(slot_label, "vocab", split_axis=0, concat_axis=0, tiled=True),
        lax.all_to_all(slot_word, "vocab", split_axis=0, concat_axis=0, tiled=True),
        lax.all_to_all(slot_weight, "vocab", split_axis=0, concat_axis=0, tiled=True),
    )
    own_block = head_blocks[0]
    logits = jnp.einsum("scd,wd->scw", got_rows, own_block, preferred_element_type=jnp.float32)
    word_ids = jnp.arange(BLOCK, dtype=jnp.int32)
    target_hit = word_ids[None, None, :] == got_word[:, :, None]
    slot_peak = jnp.max(logits, axis=2)
    slot_total = jnp.sum(jnp.exp(logits - slot_peak[:, :, None]), axis=2)
    slot_picked = jnp.sum(jnp.where(target_hit, logits, 0.0), axis=2)
    back_peak, back_total, back_picked = (
        lax.all_to_all(slot_peak, "vocab", split_axis=0, concat_axis=0, tiled=True),
        lax.all_to_all(slot_total, "vocab", split_axis=0, concat_axis=0, tiled=True),
        lax.all_to_all(slot_picked, "vocab", split_axis=0, concat_axis=0, tiled=True),
    )
    row_peak = jnp.take(back_peak, row_rank, axis=1)
    row_total = jnp.take(back_total, row_rank, axis=1)
    row_picked = jnp.take(back_picked, row_rank, axis=1)
    peak_max = jnp.max(jnp.where(routed, row_peak, -1e30), axis=0)
    summed = jnp.sum(
        jnp.where(routed, row_total * jnp.exp(row_peak - peak_max[None, :]), 0.0), axis=0
    )
    log_total = peak_max + jnp.log(summed)
    row_loss = log_total - jnp.sum(jnp.where(routed, row_picked, 0.0), axis=0)
    slot_lse = jnp.where(slot_used, jnp.take(log_total, slot_row), 0.0)
    got_lse = lax.all_to_all(slot_lse, "vocab", split_axis=0, concat_axis=0, tiled=True)
    slot_probs = jnp.exp(logits - got_lse[:, :, None])
    slot_grads = (
        got_weight.astype(jnp.float32)[:, :, None] * (slot_probs - target_hit.astype(jnp.float32))
    ).astype(jnp.bfloat16)
    part_grads = jnp.einsum(
        "scw,wd->scd", slot_grads, own_block, preferred_element_type=jnp.float32
    ).astype(jnp.bfloat16)
    back_grads = lax.all_to_all(part_grads, "vocab", split_axis=0, concat_axis=0, tiled=True)
    state_grad = jnp.einsum(
        "sct,scd->td", chosen.astype(jnp.bfloat16), back_grads, preferred_element_type=jnp.float32
    ).astype(jnp.bfloat16)
    head_term = jnp.einsum("scw,scd->wd", slot_grads, got_rows, preferred_element_type=jnp.float32)
    head_share = lax.psum_scatter(head_term, "dp", scatter_dimension=0, tiled=True)
    return (row_loss, state_grad, head_share[None])


def solution(mesh):
    one_each = mesh.shape["vocab"] == LANGS and mesh.shape["dp"] == 2 * LANGS
    return jax.shard_map(
        sliced if one_each else shards,
        mesh=mesh,
        in_specs=(
            P(("dp", "vocab"), None),
            P("vocab", None, None),
            P(),
            P(("dp", "vocab")),
            P(("dp", "vocab")),
            P(("dp", "vocab")),
        ),
        out_specs=(P(("dp", "vocab")), P(("dp", "vocab"), None), P("vocab", "dp", None)),
        check_vma=False,
    )
```

```python
import jax
import jax.numpy as jnp
from jax import lax
from jax.experimental import pallas as pl
from jax.experimental.pallas import tpu as pltpu
from jax.sharding import PartitionSpec as P

BLOCK = 128
LANGS = 4
MESH = pl.DeviceIdType.MESH
F32 = jnp.float32
BF16 = jnp.bfloat16
BATCHES = 2


def dot(a, b, dims):
    return lax.dot_general(a, b, ((dims[:1], dims[1:]), ((), ())), preferred_element_type=F32)


def iota(shape, dim):
    return lax.broadcasted_iota(jnp.int32, shape, dim)


def slice_width(width):
    return 128 * (-(-width // (128 * LANGS)))


def sliced_kernel(
    order_in, tags_in, words_in, weights_in, states, block,
    loss_out, back_out, head_out,
    order, tags, words, weights, cols, head, owner, part_send, part_got, grads, spread,
    back_send, term, pair_send, pair_got, line_send, line_got, plane_send,
    small_s, own_s, tag_s, tag_r, head_s, head_r, twin_s, twin_r, row_s, row_r,
    part_s, part_r, grad_s, grad_r, back_s, back_r, pair_s, pair_r, line_s, line_r, plane_s, plane_r,
):
    rows, width = states.shape
    wide = slice_width(width)
    over = LANGS * wide - width
    batch = rows // BATCHES
    half = BLOCK // 2
    share = BLOCK // (2 * LANGS)

    dp, z = lax.axis_index("dp"), lax.axis_index("vocab")
    core = lax.rem(dp, 2)
    x = lax.rem(lax.div(dp, 2), 2)
    y = lax.div(dp, 4)
    chips = [(y if r < 2 else 1 - y) * 2 + (x if r % 2 == 0 else 1 - x) for r in range(4)]
    own = chips[0]
    plane = [(c * 2 + core, z) for c in chips]
    twin = (own * 2 + 1 - core, z)
    planes = [lax.rem(z + d, LANGS) for d in range(LANGS)]
    sources = [lax.rem(z + LANGS - d, LANGS) for d in range(LANGS)]

    def remote(src, dst, send, recv, to):
        return pltpu.make_async_remote_copy(
            src_ref=src, dst_ref=dst, send_sem=send, recv_sem=recv, device_id=to, device_id_type=MESH
        )

    def features(chip):
        return pl.ds(pl.multiple_of(jnp.minimum(chip * wide, width - wide), 128), wide)

    def span(b, r):
        return pl.ds((b * 4 + r) * batch, batch)

    def words_at(plane_id, first, count):
        return pl.ds(pl.multiple_of(plane_id * BLOCK + first, 16), count)

    barrier = pltpu.get_barrier_semaphore()
    friends = plane[1:] + [(dp, planes[d]) for d in range(1, LANGS)] + [twin]
    for friend in friends:
        pl.semaphore_signal(barrier, inc=1, device_id=friend, device_id_type=MESH)

    small = [
        pltpu.make_async_copy(order_in, order, small_s.at[0]),
        pltpu.make_async_copy(tags_in, tags.at[0], small_s.at[1]),
        pltpu.make_async_copy(words_in, words, small_s.at[2]),
        pltpu.make_async_copy(weights_in, weights, small_s.at[3]),
    ]
    mine = [pltpu.make_async_copy(block.at[:, features(own)], head.at[words_at(z, 0, BLOCK), :], own_s.at[BATCHES])]
    for b in range(BATCHES):
        here = states.at[pl.ds(b * batch, batch), features(own)]
        mine.append(pltpu.make_async_copy(here, cols.at[span(b, 0), :], own_s.at[b]))
    for copy in small + mine:
        copy.start()

    pl.semaphore_wait(barrier, len(friends))

    head_copies = []
    for d in (2, 1, 3):
        copy = remote(
            block.at[pl.ds(pl.multiple_of(half * core, 16), half), features(own)],
            head.at[words_at(z, half * core, half), :],
            head_s.at[d - 1], head_r.at[d - 1], (dp, planes[d]),
        )
        copy.start()
        head_copies.append(copy)
    tag_copies = []
    for r in (3, 1, 2):
        copy = remote(tags_in, tags.at[r], tag_s.at[r - 1], tag_r.at[r - 1], plane[r])
        copy.start()
        tag_copies.append(copy)
    row_copies = [[], []]
    for b in range(BATCHES):
        for r in (3, 1, 2):
            n = b * 3 + r - 1
            copy = remote(
                states.at[pl.ds(b * batch, batch), features(chips[r])],
                cols.at[span(b, r), :],
                row_s.at[n], row_r.at[n], plane[r],
            )
            copy.start()
            row_copies[b].append(copy)

    for copy in small:
        copy.wait()
    square = iota((rows, rows), 0) == iota((rows, rows), 1)
    lane = iota((rows, BLOCK), 1)

    def column(values):
        wide_values = jnp.broadcast_to(values, (rows, rows))
        return jnp.sum(jnp.where(square, wide_values, 0.0), axis=1, keepdims=True)

    for copy in tag_copies:
        copy.wait_recv()
    for r in range(4):
        tag = column(tags[r].astype(F32))
        number = jnp.zeros((rows, 1), F32)
        for l in range(LANGS):
            number = jnp.where(tag == l, order[l].astype(F32), number)
        number = jnp.broadcast_to(number, (rows, BLOCK))
        for b in range(BATCHES):
            owner[span(b, r), :] = number[b * batch : (b + 1) * batch]
    target = column(words[...].astype(F32)).astype(jnp.int32)
    weight = column(weights[...].astype(F32))

    twin_copies = []
    for d in (1, 2, 3):
        remote(
            head.at[words_at(sources[d], half * core, half), :],
            head.at[words_at(sources[d], half * core, half), :],
            head_s.at[d - 1], head_r.at[d - 1], (dp, planes[d]),
        ).wait_recv()
        copy = remote(
            head.at[words_at(sources[d], half * core, half), :],
            head.at[words_at(sources[d], half * core, half), :],
            twin_s.at[d - 1], twin_r.at[d - 1], twin,
        )
        copy.start()
        twin_copies.append(copy)
    for copy in twin_copies:
        copy.wait_recv()
    mine[0].wait()

    part_copies = [[] for _ in range(BATCHES)]
    grad_copies = [[] for _ in range(BATCHES)]
    back_copies = []
    losses = []

    def whole(b):
        return pl.ds(b * 4 * batch, 4 * batch)

    def partial_logits(b):
        mine[1 + b].wait()
        for copy in row_copies[b]:
            copy.wait_recv()

        if over:
            @pl.when(own == LANGS - 1)
            def _():
                cols[whole(b), :over] = jnp.zeros((4 * batch, over), BF16)

        every = dot(cols[whole(b), :], head[...], (1, 1))
        number = owner[whole(b), :]
        kept = jnp.zeros((4 * batch, BLOCK), F32)
        for n in range(LANGS):
            kept = jnp.where(number == n, every[:, n * BLOCK : (n + 1) * BLOCK], kept)
        part_got[span(b, 0), :] = kept[:batch]
        for r in (3, 1, 2):
            n = b * 3 + r - 1
            part_send[span(b, r), :] = kept[r * batch : (r + 1) * batch]
            copy = remote(part_send.at[span(b, r), :], part_got.at[span(b, r), :], part_s.at[n], part_r.at[n], plane[r])
            copy.start()
            part_copies[b].append(copy)

    def softmax_grads(b):
        for copy in part_copies[b]:
            copy.wait_recv()
        pick = slice(b * batch, (b + 1) * batch)
        logits = (part_got[span(b, 0), :] + part_got[span(b, 1), :]) + (
            part_got[span(b, 2), :] + part_got[span(b, 3), :]
        )
        hit = lane[pick] == target[pick]
        peak = jnp.max(logits, axis=1, keepdims=True)
        total = peak + jnp.log(jnp.sum(jnp.exp(logits - peak), axis=1, keepdims=True))
        losses.append(total - jnp.sum(jnp.where(hit, logits, 0.0), axis=1, keepdims=True))
        grads[span(b, 0), :] = (weight[pick] * (jnp.exp(logits - total) - jnp.where(hit, 1.0, 0.0))).astype(BF16)
        for r in (3, 1, 2):
            n = b * 3 + r - 1
            copy = remote(grads.at[span(b, 0), :], grads.at[span(b, r), :], grad_s.at[n], grad_r.at[n], plane[r])
            copy.start()
            grad_copies[b].append(copy)

    def spread_grads(b):
        for copy in grad_copies[b]:
            copy.wait_recv()
        number = owner[whole(b), :]
        values = grads[whole(b), :].astype(F32)
        for n in range(LANGS):
            spread[whole(b), pl.ds(n * BLOCK, BLOCK)] = jnp.where(number == n, values, 0.0).astype(BF16)

    def give_back(b):
        back_send[whole(b), :] = dot(spread[whole(b), :], head[...], (1, 0)).astype(BF16)
        for r in (3, 1, 2):
            n = b * 3 + r - 1
            copy = remote(
                back_send.at[span(b, r), :],
                back_out.at[own, pl.ds(b * batch, batch), :],
                back_s.at[n], back_r.at[n], plane[r],
            )
            copy.start()
            back_copies.append(copy)
        copy = pltpu.make_async_copy(
            back_send.at[span(b, 0), :], back_out.at[own, pl.ds(b * batch, batch), :], own_s.at[BATCHES + 1 + b]
        )
        copy.start()
        mine.append(copy)

    for b in range(BATCHES):
        partial_logits(b)
    for b in range(BATCHES):
        softmax_grads(b)
    for b in range(BATCHES):
        spread_grads(b)
        if b == 0:
            give_back(0)

    def mine_of(e, which):
        return pl.ds(pl.multiple_of(2 * share * e + share * which, 16), share)

    pair_copies = {}
    line_copies = []

    def both(d, e):
        return term[d, mine_of(e, core), :] + pair_got[d, pl.ds(e * share, share), :].astype(F32)

    def head_term(d):
        picked = spread[:, pl.ds(pl.multiple_of(planes[d] * BLOCK, 128), BLOCK)]
        term[d] = dot(picked, cols[...], (0, 0))
        for e in range(LANGS):
            pair_send[d, pl.ds(e * share, share), :] = term[d, mine_of(e, 1 - core), :].astype(BF16)
        pair_copies[d] = remote(pair_send.at[d], pair_got.at[d], pair_s.at[d], pair_r.at[d], twin)
        pair_copies[d].start()

    def along_line(d):
        pair_copies[d].wait_recv()
        for e in range(LANGS):
            line_send[d - 1, pl.ds(e * share, share), :] = both(d, e).astype(BF16)
        copy = remote(
            line_send.at[d - 1], line_got.at[d - 1], line_s.at[d - 1], line_r.at[d - 1], (dp, planes[d])
        )
        copy.start()
        line_copies.append(copy)

    head_term(2)
    head_term(1)
    along_line(2)
    head_term(3)
    along_line(1)
    along_line(3)
    for b in range(1, BATCHES):
        give_back(b)
    head_term(0)

    loss = jnp.concatenate(losses, axis=0)
    loss_out[...] = jnp.sum(jnp.where(square, loss, 0.0), axis=0, keepdims=True)

    pair_copies[0].wait_recv()
    for copy in line_copies:
        copy.wait_recv()
    for e in range(LANGS):
        part = pl.ds(e * share, share)
        plane_send[e] = (
            (both(0, e) + line_got[0, part, :].astype(F32))
            + (line_got[1, part, :].astype(F32) + line_got[2, part, :].astype(F32))
        ).astype(BF16)
    plane_copies = []
    for r in (3, 1, 2):
        copy = remote(
            plane_send.at[chips[r]], head_out.at[own], plane_s.at[r - 1], plane_r.at[r - 1], plane[r]
        )
        copy.start()
        plane_copies.append(copy)
    copy = pltpu.make_async_copy(plane_send.at[own], head_out.at[own], own_s.at[2 * BATCHES + 1])
    copy.start()
    mine.append(copy)

    for copy in back_copies + plane_copies:
        copy.wait_recv()
    for copy in mine[1 + BATCHES :]:
        copy.wait()
    everything = (
        head_copies + tag_copies + twin_copies + back_copies + line_copies + plane_copies
        + [c for group in row_copies + part_copies + grad_copies for c in group]
        + [pair_copies[d] for d in range(LANGS)]
    )
    for copy in everything:
        copy.wait_send()


def joined_kernel(
    loss_in, back_in, head_in, loss_out, state_out, head_out, loss_got, back_got, head_got, head_done, got, put
):
    wide = back_in.shape[2]
    over = LANGS * wide - state_out.shape[1]
    loads = [
        pltpu.make_async_copy(head_in, head_got, got.at[LANGS]),
        pltpu.make_async_copy(loss_in, loss_got, got.at[LANGS + 1]),
    ]
    loads += [pltpu.make_async_copy(back_in.at[e], back_got.at[e], got.at[e]) for e in range(LANGS)]
    for copy in loads:
        copy.start()
    skips = [over if e == LANGS - 1 else 0 for e in range(LANGS)]
    stores = []

    def store(src, dst, n):
        copy = pltpu.make_async_copy(src, dst, put.at[n])
        copy.start()
        stores.append(copy)

    loads[0].wait()
    for e, skip in enumerate(skips):
        head_done[0, :, pl.ds(e * wide, wide - skip)] = head_got[e, :, pl.ds(skip, wide - skip)].astype(F32)
    store(head_done, head_out, LANGS)
    loads[1].wait()
    store(loss_got, loss_out, LANGS + 1)
    for e, skip in enumerate(skips):
        loads[2 + e].wait()
        store(
            back_got.at[e, :, pl.ds(skip, wide - skip)], state_out.at[:, pl.ds(e * wide, wide - skip)], e
        )
    for copy in stores:
        copy.wait()


def sliced(final_states, head_blocks, block_order, row_tags, target_word, row_weight):
    rows, width = final_states.shape
    wide = slice_width(width)
    over = LANGS * wide - width
    share = BLOCK // (2 * LANGS)
    half = BLOCK // 2
    group = LANGS * rows
    hbm = pl.BlockSpec(memory_space=pl.ANY)
    vmem = pl.BlockSpec(memory_space=pltpu.VMEM)
    dma = pltpu.SemaphoreType.DMA
    three, batches = dma((3,)), dma((3 * BATCHES,))
    loss, back, head = pl.pallas_call(
        sliced_kernel,
        out_shape=(
            jax.ShapeDtypeStruct((1, rows), F32),
            jax.ShapeDtypeStruct((LANGS, rows, wide), BF16),
            jax.ShapeDtypeStruct((LANGS, share, wide), BF16),
        ),
        in_specs=[hbm] * 6,
        out_specs=(vmem, hbm, hbm),
        scratch_shapes=[
            pltpu.SMEM((LANGS,), jnp.int32),
            pltpu.VMEM((LANGS, 1, rows), jnp.int32),
            pltpu.VMEM((1, rows), jnp.int32),
            pltpu.VMEM((1, rows), BF16),
            pltpu.VMEM((group, wide), BF16),
            pltpu.VMEM((LANGS * BLOCK, wide), BF16),
            pltpu.VMEM((group, BLOCK), F32),
            pltpu.VMEM((group, BLOCK), F32),
            pltpu.VMEM((group, BLOCK), F32),
            pltpu.VMEM((group, BLOCK), BF16),
            pltpu.VMEM((group, LANGS * BLOCK), BF16),
            pltpu.VMEM((group, wide), BF16),
            pltpu.VMEM((LANGS, BLOCK, wide), F32),
            pltpu.VMEM((LANGS, half, wide), BF16),
            pltpu.VMEM((LANGS, half, wide), BF16),
            pltpu.VMEM((LANGS - 1, half, wide), BF16),
            pltpu.VMEM((LANGS - 1, half, wide), BF16),
            pltpu.VMEM((LANGS, share, wide), BF16),
            dma((4,)), dma((2 * BATCHES + 2,)), three, three, three, three, three, three, batches, batches,
            batches, batches, batches, batches, batches, batches, dma((LANGS,)), dma((LANGS,)),
            three, three, three, three,
        ],
        compiler_params=pltpu.CompilerParams(
            collective_id=0, has_side_effects=True, vmem_limit_bytes=60 * 1024 * 1024
        ),
        name="sliced",
    )(
        block_order,
        row_tags.reshape(1, rows),
        target_word.reshape(1, rows),
        row_weight.reshape(1, rows),
        final_states,
        head_blocks.reshape(BLOCK, width),
    )
    loss, state_grad, head_grad = pl.pallas_call(
        joined_kernel,
        out_shape=(
            jax.ShapeDtypeStruct((1, rows), F32),
            jax.ShapeDtypeStruct((rows, width), BF16),
            jax.ShapeDtypeStruct((1, share, width), F32),
        ),
        in_specs=[hbm] * 3,
        out_specs=[hbm] * 3,
        scratch_shapes=[
            pltpu.VMEM((1, rows), F32),
            pltpu.VMEM((LANGS, rows, wide), BF16),
            pltpu.VMEM((LANGS, share, wide), BF16),
            pltpu.VMEM((1, share, width), F32),
            dma((LANGS + 2,)),
            dma((LANGS + 2,)),
        ],
        compiler_params=pltpu.CompilerParams(vmem_limit_bytes=60 * 1024 * 1024),
        name="joined",
    )(loss, back, head)
    return loss.reshape(rows), state_grad, head_grad


def shards(final_states, head_blocks, block_order, row_tags, target_word, row_weight):
    shard_count = lax.axis_size("vocab")
    rows_here = final_states.shape[0]
    short_len = shard_count // LANGS
    capacity = rows_here * 5 // 16
    block_ids = jnp.arange(shard_count, dtype=jnp.int32)
    placed = jnp.sum(
        block_ids[:, None] * (block_order[:, None] == block_ids[None, :]).astype(jnp.int32), axis=0
    )
    owner_tag = placed // short_len
    owner_slot = placed % short_len
    tag_ids = jnp.arange(LANGS, dtype=jnp.int32)
    tag_onehot = (row_tags[:, None] == tag_ids[None, :]).astype(jnp.int32)
    row_rank = jnp.sum((jnp.cumsum(tag_onehot, axis=0) - 1) * tag_onehot, axis=1)
    routed = owner_tag[:, None] == row_tags[None, :]
    slot_ids = jnp.arange(capacity, dtype=jnp.int32)
    chosen = routed[:, None, :] & (row_rank[None, None, :] == slot_ids[None, :, None])
    chosen_int = chosen.astype(jnp.int32)
    slot_used = jnp.sum(chosen_int, axis=2) > 0
    row_ids = jnp.arange(rows_here, dtype=jnp.int32)
    slot_row = jnp.sum(chosen_int * row_ids[None, None, :], axis=2)
    sent_rows = jnp.where(
        slot_used[:, :, None], jnp.take(final_states, slot_row, axis=0), jnp.zeros((), jnp.bfloat16)
    )
    local_word = jnp.where(
        target_word[None, :] // BLOCK == owner_slot[:, None], target_word[None, :] % BLOCK, -1
    )
    slot_word = jnp.sum(chosen_int * (local_word[:, None, :] + 1), axis=2) - 1
    slot_label = jnp.where(slot_used, slot_row, -1)
    slot_weight = jnp.sum(
        jnp.where(chosen, row_weight.astype(jnp.float32)[None, None, :], 0.0), axis=2
    ).astype(jnp.bfloat16)
    got_rows, got_label, got_word, got_weight = (
        lax.all_to_all(sent_rows, "vocab", split_axis=0, concat_axis=0, tiled=True),
        lax.all_to_all(slot_label, "vocab", split_axis=0, concat_axis=0, tiled=True),
        lax.all_to_all(slot_word, "vocab", split_axis=0, concat_axis=0, tiled=True),
        lax.all_to_all(slot_weight, "vocab", split_axis=0, concat_axis=0, tiled=True),
    )
    own_block = head_blocks[0]
    logits = jnp.einsum("scd,wd->scw", got_rows, own_block, preferred_element_type=jnp.float32)
    word_ids = jnp.arange(BLOCK, dtype=jnp.int32)
    target_hit = word_ids[None, None, :] == got_word[:, :, None]
    slot_peak = jnp.max(logits, axis=2)
    slot_total = jnp.sum(jnp.exp(logits - slot_peak[:, :, None]), axis=2)
    slot_picked = jnp.sum(jnp.where(target_hit, logits, 0.0), axis=2)
    back_peak, back_total, back_picked = (
        lax.all_to_all(slot_peak, "vocab", split_axis=0, concat_axis=0, tiled=True),
        lax.all_to_all(slot_total, "vocab", split_axis=0, concat_axis=0, tiled=True),
        lax.all_to_all(slot_picked, "vocab", split_axis=0, concat_axis=0, tiled=True),
    )
    row_peak = jnp.take(back_peak, row_rank, axis=1)
    row_total = jnp.take(back_total, row_rank, axis=1)
    row_picked = jnp.take(back_picked, row_rank, axis=1)
    peak_max = jnp.max(jnp.where(routed, row_peak, -1e30), axis=0)
    summed = jnp.sum(
        jnp.where(routed, row_total * jnp.exp(row_peak - peak_max[None, :]), 0.0), axis=0
    )
    log_total = peak_max + jnp.log(summed)
    row_loss = log_total - jnp.sum(jnp.where(routed, row_picked, 0.0), axis=0)
    slot_lse = jnp.where(slot_used, jnp.take(log_total, slot_row), 0.0)
    got_lse = lax.all_to_all(slot_lse, "vocab", split_axis=0, concat_axis=0, tiled=True)
    slot_probs = jnp.exp(logits - got_lse[:, :, None])
    slot_grads = (
        got_weight.astype(jnp.float32)[:, :, None] * (slot_probs - target_hit.astype(jnp.float32))
    ).astype(jnp.bfloat16)
    part_grads = jnp.einsum(
        "scw,wd->scd", slot_grads, own_block, preferred_element_type=jnp.float32
    ).astype(jnp.bfloat16)
    back_grads = lax.all_to_all(part_grads, "vocab", split_axis=0, concat_axis=0, tiled=True)
    state_grad = jnp.einsum(
        "sct,scd->td", chosen.astype(jnp.bfloat16), back_grads, preferred_element_type=jnp.float32
    ).astype(jnp.bfloat16)
    head_term = jnp.einsum("scw,scd->wd", slot_grads, got_rows, preferred_element_type=jnp.float32)
    head_share = lax.psum_scatter(head_term, "dp", scatter_dimension=0, tiled=True)
    return (row_loss, state_grad, head_share[None])


def solution(mesh):
    one_each = mesh.shape["vocab"] == LANGS and mesh.shape["dp"] == 2 * LANGS
    return jax.shard_map(
        sliced if one_each else shards,
        mesh=mesh,
        in_specs=(
            P(("dp", "vocab"), None),
            P("vocab", None, None),
            P(),
            P(("dp", "vocab")),
            P(("dp", "vocab")),
            P(("dp", "vocab")),
        ),
        out_specs=(P(("dp", "vocab")), P(("dp", "vocab"), None), P("vocab", "dp", None)),
        check_vma=False,
    )
```

```python
import jax
import jax.numpy as jnp
from jax import lax
from jax.experimental import pallas as pl
from jax.experimental.pallas import tpu as pltpu
from jax.sharding import PartitionSpec as P

BLOCK = 128
LANGS = 4
MESH = pl.DeviceIdType.MESH
F32 = jnp.float32
BF16 = jnp.bfloat16
BATCHES = 2


def dot(a, b, dims):
    return lax.dot_general(a, b, ((dims[:1], dims[1:]), ((), ())), preferred_element_type=F32)


def iota(shape, dim):
    return lax.broadcasted_iota(jnp.int32, shape, dim)


def slice_width(width):
    return 128 * (-(-width // (128 * LANGS)))


def sliced_kernel(
    order_in, tags_in, words_in, weights_in, states, block,
    loss_out, back_out, head_out,
    order, tags, words, weights, cols, head, owner, part_send, part_got, grads, spread,
    back_send, term, pair_send, pair_got, line_send, line_got, plane_send,
    small_s, own_s, tag_s, tag_r, up_s, up_r, down_s, down_r, twin_s, twin_r, row_s, row_r,
    part_s, part_r, grad_s, grad_r, back_s, back_r, pair_s, pair_r, line_s, line_r, plane_s, plane_r,
):
    rows, width = states.shape
    wide = slice_width(width)
    over = LANGS * wide - width
    batch = rows // BATCHES
    half = BLOCK // 2
    share = BLOCK // (2 * LANGS)

    dp, z = lax.axis_index("dp"), lax.axis_index("vocab")
    core = lax.rem(dp, 2)
    x = lax.rem(lax.div(dp, 2), 2)
    y = lax.div(dp, 4)
    chips = [(y if r < 2 else 1 - y) * 2 + (x if r % 2 == 0 else 1 - x) for r in range(4)]
    own = chips[0]
    plane = [(c * 2 + core, z) for c in chips]
    twin = (own * 2 + 1 - core, z)
    planes = [lax.rem(z + d, LANGS) for d in range(LANGS)]
    sources = [lax.rem(z + LANGS - d, LANGS) for d in range(LANGS)]

    def remote(src, dst, send, recv, to):
        return pltpu.make_async_remote_copy(
            src_ref=src, dst_ref=dst, send_sem=send, recv_sem=recv, device_id=to, device_id_type=MESH
        )

    def features(chip):
        return pl.ds(pl.multiple_of(jnp.minimum(chip * wide, width - wide), 128), wide)

    def span(b, r):
        return pl.ds((b * 4 + r) * batch, batch)

    def words_at(plane_id, first, count):
        return pl.ds(pl.multiple_of(plane_id * BLOCK + first, 16), count)

    barrier = pltpu.get_barrier_semaphore()
    friends = plane[1:] + [(dp, planes[d]) for d in range(1, LANGS)] + [twin]
    for friend in friends:
        pl.semaphore_signal(barrier, inc=1, device_id=friend, device_id_type=MESH)

    small = [
        pltpu.make_async_copy(order_in, order, small_s.at[0]),
        pltpu.make_async_copy(tags_in, tags.at[0], small_s.at[1]),
        pltpu.make_async_copy(words_in, words, small_s.at[2]),
        pltpu.make_async_copy(weights_in, weights, small_s.at[3]),
    ]
    mine = [pltpu.make_async_copy(block.at[:, features(own)], head.at[words_at(z, 0, BLOCK), :], own_s.at[BATCHES])]
    for b in range(BATCHES):
        here = states.at[pl.ds(b * batch, batch), features(own)]
        mine.append(pltpu.make_async_copy(here, cols.at[span(b, 0), :], own_s.at[b]))
    for copy in small + mine:
        copy.start()

    pl.semaphore_wait(barrier, len(friends))

    def half_at(plane_id, which):
        return head.at[words_at(plane_id, half * which, half), :]

    own_half = block.at[pl.ds(pl.multiple_of(half * core, 16), half), features(own)]
    above, below = (dp, planes[1]), (dp, planes[LANGS - 1])

    def upward(k):
        src = half_at(sources[k], core) if k else own_half
        return remote(src, half_at(sources[k], core), up_s.at[k], up_r.at[k], above)

    def downward(k):
        src = half_at(planes[k], core) if k else own_half
        return remote(src, half_at(planes[k], core), down_s.at[k], down_r.at[k], below)

    def twin_up(k):
        return remote(half_at(sources[k], core), half_at(sources[k], core), twin_s.at[k], twin_r.at[k], twin)

    def twin_down(k):
        return remote(
            half_at(planes[k], core), half_at(planes[k], core), twin_s.at[LANGS + k], twin_r.at[LANGS + k], twin
        )

    last = LANGS - 1

    def when(condition, act):
        pl.when(condition)(act)

    when(z < last, lambda: upward(0).start())
    when(z > 0, lambda: downward(0).start())
    tag_copies = []
    for r in (3, 1, 2):
        copy = remote(tags_in, tags.at[r], tag_s.at[r - 1], tag_r.at[r - 1], plane[r])
        copy.start()
        tag_copies.append(copy)
    row_copies = [[], []]
    for b in range(BATCHES):
        for r in (3, 1, 2):
            n = b * 3 + r - 1
            copy = remote(
                states.at[pl.ds(b * batch, batch), features(chips[r])],
                cols.at[span(b, r), :],
                row_s.at[n], row_r.at[n], plane[r],
            )
            copy.start()
            row_copies[b].append(copy)

    for copy in small:
        copy.wait()
    square = iota((rows, rows), 0) == iota((rows, rows), 1)
    lane = iota((rows, BLOCK), 1)

    def column(values):
        wide_values = jnp.broadcast_to(values, (rows, rows))
        return jnp.sum(jnp.where(square, wide_values, 0.0), axis=1, keepdims=True)

    for copy in tag_copies:
        copy.wait_recv()
    for r in range(4):
        tag = column(tags[r].astype(F32))
        number = jnp.zeros((rows, 1), F32)
        for l in range(LANGS):
            number = jnp.where(tag == l, order[l].astype(F32), number)
        number = jnp.broadcast_to(number, (rows, BLOCK))
        for b in range(BATCHES):
            owner[span(b, r), :] = number[b * batch : (b + 1) * batch]
    target = column(words[...].astype(F32)).astype(jnp.int32)
    weight = column(weights[...].astype(F32))

    for k in range(1, LANGS):
        @pl.when(z >= k)
        def _(k=k):
            upward(k - 1).wait_recv()
            if k < last:
                when(z < last, lambda: upward(k).start())
            twin_up(k).start()

        @pl.when(z + k <= last)
        def _(k=k):
            downward(k - 1).wait_recv()
            if k < last:
                when(z > 0, lambda: downward(k).start())
            twin_down(k).start()

    for k in range(1, LANGS):
        when(z >= k, lambda k=k: twin_up(k).wait_recv())
        when(z + k <= last, lambda k=k: twin_down(k).wait_recv())
    mine[0].wait()

    part_copies = [[] for _ in range(BATCHES)]
    grad_copies = [[] for _ in range(BATCHES)]
    back_copies = []
    losses = []

    def whole(b):
        return pl.ds(b * 4 * batch, 4 * batch)

    def partial_logits(b):
        mine[1 + b].wait()
        for copy in row_copies[b]:
            copy.wait_recv()

        if over:
            @pl.when(own == LANGS - 1)
            def _():
                cols[whole(b), :over] = jnp.zeros((4 * batch, over), BF16)

        every = dot(cols[whole(b), :], head[...], (1, 1))
        number = owner[whole(b), :]
        kept = jnp.zeros((4 * batch, BLOCK), F32)
        for n in range(LANGS):
            kept = jnp.where(number == n, every[:, n * BLOCK : (n + 1) * BLOCK], kept)
        part_got[span(b, 0), :] = kept[:batch]
        for r in (3, 1, 2):
            n = b * 3 + r - 1
            part_send[span(b, r), :] = kept[r * batch : (r + 1) * batch]
            copy = remote(part_send.at[span(b, r), :], part_got.at[span(b, r), :], part_s.at[n], part_r.at[n], plane[r])
            copy.start()
            part_copies[b].append(copy)

    def softmax_grads(b):
        for copy in part_copies[b]:
            copy.wait_recv()
        pick = slice(b * batch, (b + 1) * batch)
        logits = (part_got[span(b, 0), :] + part_got[span(b, 1), :]) + (
            part_got[span(b, 2), :] + part_got[span(b, 3), :]
        )
        hit = lane[pick] == target[pick]
        peak = jnp.max(logits, axis=1, keepdims=True)
        total = peak + jnp.log(jnp.sum(jnp.exp(logits - peak), axis=1, keepdims=True))
        losses.append(total - jnp.sum(jnp.where(hit, logits, 0.0), axis=1, keepdims=True))
        grads[span(b, 0), :] = (weight[pick] * (jnp.exp(logits - total) - jnp.where(hit, 1.0, 0.0))).astype(BF16)
        for r in (3, 1, 2):
            n = b * 3 + r - 1
            copy = remote(grads.at[span(b, 0), :], grads.at[span(b, r), :], grad_s.at[n], grad_r.at[n], plane[r])
            copy.start()
            grad_copies[b].append(copy)

    def spread_grads(b):
        for copy in grad_copies[b]:
            copy.wait_recv()
        number = owner[whole(b), :]
        values = grads[whole(b), :].astype(F32)
        for n in range(LANGS):
            spread[whole(b), pl.ds(n * BLOCK, BLOCK)] = jnp.where(number == n, values, 0.0).astype(BF16)

    def give_back(b):
        back_send[whole(b), :] = dot(spread[whole(b), :], head[...], (1, 0)).astype(BF16)
        for r in (3, 1, 2):
            n = b * 3 + r - 1
            copy = remote(
                back_send.at[span(b, r), :],
                back_out.at[own, pl.ds(b * batch, batch), :],
                back_s.at[n], back_r.at[n], plane[r],
            )
            copy.start()
            back_copies.append(copy)
        copy = pltpu.make_async_copy(
            back_send.at[span(b, 0), :], back_out.at[own, pl.ds(b * batch, batch), :], own_s.at[BATCHES + 1 + b]
        )
        copy.start()
        mine.append(copy)

    for b in range(BATCHES):
        partial_logits(b)
    for b in range(BATCHES):
        softmax_grads(b)
    for b in range(BATCHES):
        spread_grads(b)
        if b == 0:
            give_back(0)

    def mine_of(e, which):
        return pl.ds(pl.multiple_of(2 * share * e + share * which, 16), share)

    pair_copies = {}
    line_copies = []

    def both(d, e):
        return term[d, mine_of(e, core), :] + pair_got[d, pl.ds(e * share, share), :].astype(F32)

    def head_term(d):
        picked = spread[:, pl.ds(pl.multiple_of(planes[d] * BLOCK, 128), BLOCK)]
        term[d] = dot(picked, cols[...], (0, 0))
        for e in range(LANGS):
            pair_send[d, pl.ds(e * share, share), :] = term[d, mine_of(e, 1 - core), :].astype(BF16)
        pair_copies[d] = remote(pair_send.at[d], pair_got.at[d], pair_s.at[d], pair_r.at[d], twin)
        pair_copies[d].start()

    def along_line(d):
        pair_copies[d].wait_recv()
        for e in range(LANGS):
            line_send[d - 1, pl.ds(e * share, share), :] = both(d, e).astype(BF16)
        copy = remote(
            line_send.at[d - 1], line_got.at[d - 1], line_s.at[d - 1], line_r.at[d - 1], (dp, planes[d])
        )
        copy.start()
        line_copies.append(copy)

    head_term(2)
    head_term(1)
    along_line(2)
    head_term(3)
    along_line(1)
    along_line(3)
    for b in range(1, BATCHES):
        give_back(b)
    head_term(0)

    loss = jnp.concatenate(losses, axis=0)
    loss_out[...] = jnp.sum(jnp.where(square, loss, 0.0), axis=0, keepdims=True)

    pair_copies[0].wait_recv()
    for copy in line_copies:
        copy.wait_recv()
    for e in range(LANGS):
        part = pl.ds(e * share, share)
        plane_send[e] = (
            (both(0, e) + line_got[0, part, :].astype(F32))
            + (line_got[1, part, :].astype(F32) + line_got[2, part, :].astype(F32))
        ).astype(BF16)
    plane_copies = []
    for r in (3, 1, 2):
        copy = remote(
            plane_send.at[chips[r]], head_out.at[own], plane_s.at[r - 1], plane_r.at[r - 1], plane[r]
        )
        copy.start()
        plane_copies.append(copy)
    copy = pltpu.make_async_copy(plane_send.at[own], head_out.at[own], own_s.at[2 * BATCHES + 1])
    copy.start()
    mine.append(copy)

    for copy in back_copies + plane_copies:
        copy.wait_recv()
    for copy in mine[1 + BATCHES :]:
        copy.wait()
    for k in range(LANGS - 1):
        when((z >= k) & (z < last), lambda k=k: upward(k).wait_send())
        when((z + k <= last) & (z > 0), lambda k=k: downward(k).wait_send())
    for k in range(1, LANGS):
        when(z >= k, lambda k=k: twin_up(k).wait_send())
        when(z + k <= last, lambda k=k: twin_down(k).wait_send())
    everything = (
        tag_copies + back_copies + line_copies + plane_copies
        + [c for group in row_copies + part_copies + grad_copies for c in group]
        + [pair_copies[d] for d in range(LANGS)]
    )
    for copy in everything:
        copy.wait_send()


def joined_kernel(
    loss_in, back_in, head_in, loss_out, state_out, head_out, loss_got, back_got, head_got, head_done, got, put
):
    wide = back_in.shape[2]
    over = LANGS * wide - state_out.shape[1]
    loads = [
        pltpu.make_async_copy(head_in, head_got, got.at[LANGS]),
        pltpu.make_async_copy(loss_in, loss_got, got.at[LANGS + 1]),
    ]
    loads += [pltpu.make_async_copy(back_in.at[e], back_got.at[e], got.at[e]) for e in range(LANGS)]
    for copy in loads:
        copy.start()
    skips = [over if e == LANGS - 1 else 0 for e in range(LANGS)]
    stores = []

    def store(src, dst, n):
        copy = pltpu.make_async_copy(src, dst, put.at[n])
        copy.start()
        stores.append(copy)

    loads[0].wait()
    for e, skip in enumerate(skips):
        head_done[0, :, pl.ds(e * wide, wide - skip)] = head_got[e, :, pl.ds(skip, wide - skip)].astype(F32)
    store(head_done, head_out, LANGS)
    loads[1].wait()
    store(loss_got, loss_out, LANGS + 1)
    for e, skip in enumerate(skips):
        loads[2 + e].wait()
        store(
            back_got.at[e, :, pl.ds(skip, wide - skip)], state_out.at[:, pl.ds(e * wide, wide - skip)], e
        )
    for copy in stores:
        copy.wait()


def sliced(final_states, head_blocks, block_order, row_tags, target_word, row_weight):
    rows, width = final_states.shape
    wide = slice_width(width)
    over = LANGS * wide - width
    share = BLOCK // (2 * LANGS)
    half = BLOCK // 2
    group = LANGS * rows
    hbm = pl.BlockSpec(memory_space=pl.ANY)
    vmem = pl.BlockSpec(memory_space=pltpu.VMEM)
    dma = pltpu.SemaphoreType.DMA
    three, batches = dma((3,)), dma((3 * BATCHES,))
    loss, back, head = pl.pallas_call(
        sliced_kernel,
        out_shape=(
            jax.ShapeDtypeStruct((1, rows), F32),
            jax.ShapeDtypeStruct((LANGS, rows, wide), BF16),
            jax.ShapeDtypeStruct((LANGS, share, wide), BF16),
        ),
        in_specs=[hbm] * 6,
        out_specs=(vmem, hbm, hbm),
        scratch_shapes=[
            pltpu.SMEM((LANGS,), jnp.int32),
            pltpu.VMEM((LANGS, 1, rows), jnp.int32),
            pltpu.VMEM((1, rows), jnp.int32),
            pltpu.VMEM((1, rows), BF16),
            pltpu.VMEM((group, wide), BF16),
            pltpu.VMEM((LANGS * BLOCK, wide), BF16),
            pltpu.VMEM((group, BLOCK), F32),
            pltpu.VMEM((group, BLOCK), F32),
            pltpu.VMEM((group, BLOCK), F32),
            pltpu.VMEM((group, BLOCK), BF16),
            pltpu.VMEM((group, LANGS * BLOCK), BF16),
            pltpu.VMEM((group, wide), BF16),
            pltpu.VMEM((LANGS, BLOCK, wide), F32),
            pltpu.VMEM((LANGS, half, wide), BF16),
            pltpu.VMEM((LANGS, half, wide), BF16),
            pltpu.VMEM((LANGS - 1, half, wide), BF16),
            pltpu.VMEM((LANGS - 1, half, wide), BF16),
            pltpu.VMEM((LANGS, share, wide), BF16),
            dma((4,)), dma((2 * BATCHES + 2,)), three, three, three, three, three, three,
            dma((2 * LANGS,)), dma((2 * LANGS,)), batches, batches,
            batches, batches, batches, batches, batches, batches, dma((LANGS,)), dma((LANGS,)),
            three, three, three, three,
        ],
        compiler_params=pltpu.CompilerParams(
            collective_id=0, has_side_effects=True, vmem_limit_bytes=60 * 1024 * 1024
        ),
        name="sliced",
    )(
        block_order,
        row_tags.reshape(1, rows),
        target_word.reshape(1, rows),
        row_weight.reshape(1, rows),
        final_states,
        head_blocks.reshape(BLOCK, width),
    )
    loss, state_grad, head_grad = pl.pallas_call(
        joined_kernel,
        out_shape=(
            jax.ShapeDtypeStruct((1, rows), F32),
            jax.ShapeDtypeStruct((rows, width), BF16),
            jax.ShapeDtypeStruct((1, share, width), F32),
        ),
        in_specs=[hbm] * 3,
        out_specs=[hbm] * 3,
        scratch_shapes=[
            pltpu.VMEM((1, rows), F32),
            pltpu.VMEM((LANGS, rows, wide), BF16),
            pltpu.VMEM((LANGS, share, wide), BF16),
            pltpu.VMEM((1, share, width), F32),
            dma((LANGS + 2,)),
            dma((LANGS + 2,)),
        ],
        compiler_params=pltpu.CompilerParams(vmem_limit_bytes=60 * 1024 * 1024),
        name="joined",
    )(loss, back, head)
    return loss.reshape(rows), state_grad, head_grad


def shards(final_states, head_blocks, block_order, row_tags, target_word, row_weight):
    shard_count = lax.axis_size("vocab")
    rows_here = final_states.shape[0]
    short_len = shard_count // LANGS
    capacity = rows_here * 5 // 16
    block_ids = jnp.arange(shard_count, dtype=jnp.int32)
    placed = jnp.sum(
        block_ids[:, None] * (block_order[:, None] == block_ids[None, :]).astype(jnp.int32), axis=0
    )
    owner_tag = placed // short_len
    owner_slot = placed % short_len
    tag_ids = jnp.arange(LANGS, dtype=jnp.int32)
    tag_onehot = (row_tags[:, None] == tag_ids[None, :]).astype(jnp.int32)
    row_rank = jnp.sum((jnp.cumsum(tag_onehot, axis=0) - 1) * tag_onehot, axis=1)
    routed = owner_tag[:, None] == row_tags[None, :]
    slot_ids = jnp.arange(capacity, dtype=jnp.int32)
    chosen = routed[:, None, :] & (row_rank[None, None, :] == slot_ids[None, :, None])
    chosen_int = chosen.astype(jnp.int32)
    slot_used = jnp.sum(chosen_int, axis=2) > 0
    row_ids = jnp.arange(rows_here, dtype=jnp.int32)
    slot_row = jnp.sum(chosen_int * row_ids[None, None, :], axis=2)
    sent_rows = jnp.where(
        slot_used[:, :, None], jnp.take(final_states, slot_row, axis=0), jnp.zeros((), jnp.bfloat16)
    )
    local_word = jnp.where(
        target_word[None, :] // BLOCK == owner_slot[:, None], target_word[None, :] % BLOCK, -1
    )
    slot_word = jnp.sum(chosen_int * (local_word[:, None, :] + 1), axis=2) - 1
    slot_label = jnp.where(slot_used, slot_row, -1)
    slot_weight = jnp.sum(
        jnp.where(chosen, row_weight.astype(jnp.float32)[None, None, :], 0.0), axis=2
    ).astype(jnp.bfloat16)
    got_rows, got_label, got_word, got_weight = (
        lax.all_to_all(sent_rows, "vocab", split_axis=0, concat_axis=0, tiled=True),
        lax.all_to_all(slot_label, "vocab", split_axis=0, concat_axis=0, tiled=True),
        lax.all_to_all(slot_word, "vocab", split_axis=0, concat_axis=0, tiled=True),
        lax.all_to_all(slot_weight, "vocab", split_axis=0, concat_axis=0, tiled=True),
    )
    own_block = head_blocks[0]
    logits = jnp.einsum("scd,wd->scw", got_rows, own_block, preferred_element_type=jnp.float32)
    word_ids = jnp.arange(BLOCK, dtype=jnp.int32)
    target_hit = word_ids[None, None, :] == got_word[:, :, None]
    slot_peak = jnp.max(logits, axis=2)
    slot_total = jnp.sum(jnp.exp(logits - slot_peak[:, :, None]), axis=2)
    slot_picked = jnp.sum(jnp.where(target_hit, logits, 0.0), axis=2)
    back_peak, back_total, back_picked = (
        lax.all_to_all(slot_peak, "vocab", split_axis=0, concat_axis=0, tiled=True),
        lax.all_to_all(slot_total, "vocab", split_axis=0, concat_axis=0, tiled=True),
        lax.all_to_all(slot_picked, "vocab", split_axis=0, concat_axis=0, tiled=True),
    )
    row_peak = jnp.take(back_peak, row_rank, axis=1)
    row_total = jnp.take(back_total, row_rank, axis=1)
    row_picked = jnp.take(back_picked, row_rank, axis=1)
    peak_max = jnp.max(jnp.where(routed, row_peak, -1e30), axis=0)
    summed = jnp.sum(
        jnp.where(routed, row_total * jnp.exp(row_peak - peak_max[None, :]), 0.0), axis=0
    )
    log_total = peak_max + jnp.log(summed)
    row_loss = log_total - jnp.sum(jnp.where(routed, row_picked, 0.0), axis=0)
    slot_lse = jnp.where(slot_used, jnp.take(log_total, slot_row), 0.0)
    got_lse = lax.all_to_all(slot_lse, "vocab", split_axis=0, concat_axis=0, tiled=True)
    slot_probs = jnp.exp(logits - got_lse[:, :, None])
    slot_grads = (
        got_weight.astype(jnp.float32)[:, :, None] * (slot_probs - target_hit.astype(jnp.float32))
    ).astype(jnp.bfloat16)
    part_grads = jnp.einsum(
        "scw,wd->scd", slot_grads, own_block, preferred_element_type=jnp.float32
    ).astype(jnp.bfloat16)
    back_grads = lax.all_to_all(part_grads, "vocab", split_axis=0, concat_axis=0, tiled=True)
    state_grad = jnp.einsum(
        "sct,scd->td", chosen.astype(jnp.bfloat16), back_grads, preferred_element_type=jnp.float32
    ).astype(jnp.bfloat16)
    head_term = jnp.einsum("scw,scd->wd", slot_grads, got_rows, preferred_element_type=jnp.float32)
    head_share = lax.psum_scatter(head_term, "dp", scatter_dimension=0, tiled=True)
    return (row_loss, state_grad, head_share[None])


def solution(mesh):
    one_each = mesh.shape["vocab"] == LANGS and mesh.shape["dp"] == 2 * LANGS
    return jax.shard_map(
        sliced if one_each else shards,
        mesh=mesh,
        in_specs=(
            P(("dp", "vocab"), None),
            P("vocab", None, None),
            P(),
            P(("dp", "vocab")),
            P(("dp", "vocab")),
            P(("dp", "vocab")),
        ),
        out_specs=(P(("dp", "vocab")), P(("dp", "vocab"), None), P("vocab", "dp", None)),
        check_vma=False,
    )
```

```python
import jax
import jax.numpy as jnp
from jax import lax
from jax.experimental import pallas as pl
from jax.experimental.pallas import tpu as pltpu
from jax.sharding import PartitionSpec as P

BLOCK = 128
LANGS = 4
MESH = pl.DeviceIdType.MESH
F32 = jnp.float32
BF16 = jnp.bfloat16
BATCHES = 2


def dot(a, b, dims):
    return lax.dot_general(a, b, ((dims[:1], dims[1:]), ((), ())), preferred_element_type=F32)


def iota(shape, dim):
    return lax.broadcasted_iota(jnp.int32, shape, dim)


def slice_width(width):
    return 128 * (-(-width // (128 * LANGS)))


def sliced_kernel(
    order_in, tags_in, words_in, weights_in, states, block,
    loss_out, back_out, head_out,
    order, tags, words, weights, cols, head, owner, part_send, part_got, grads, spread,
    back_send, term, pair_send, pair_got, line_send, line_got, plane_send,
    small_s, own_s, tag_s, tag_r, head_s, head_r, twin_s, twin_r, row_s, row_r,
    part_s, part_r, grad_s, grad_r, back_s, back_r, pair_s, pair_r, line_s, line_r, plane_s, plane_r,
):
    rows, width = states.shape
    wide = slice_width(width)
    over = LANGS * wide - width
    batch = rows // BATCHES
    half = BLOCK // 2
    share = BLOCK // (2 * LANGS)

    dp, z = lax.axis_index("dp"), lax.axis_index("vocab")
    core = lax.rem(dp, 2)
    x = lax.rem(lax.div(dp, 2), 2)
    y = lax.div(dp, 4)
    chips = [(y if r < 2 else 1 - y) * 2 + (x if r % 2 == 0 else 1 - x) for r in range(4)]
    own = chips[0]
    plane = [(c * 2 + core, z) for c in chips]
    twin = (own * 2 + 1 - core, z)
    planes = [lax.rem(z + d, LANGS) for d in range(LANGS)]
    sources = [lax.rem(z + LANGS - d, LANGS) for d in range(LANGS)]

    def remote(src, dst, send, recv, to):
        return pltpu.make_async_remote_copy(
            src_ref=src, dst_ref=dst, send_sem=send, recv_sem=recv, device_id=to, device_id_type=MESH
        )

    def features(chip):
        return pl.ds(pl.multiple_of(jnp.minimum(chip * wide, width - wide), 128), wide)

    def span(b, r):
        return pl.ds((b * 4 + r) * batch, batch)

    def words_at(plane_id, first, count):
        return pl.ds(pl.multiple_of(plane_id * BLOCK + first, 16), count)

    barrier = pltpu.get_barrier_semaphore()
    friends = plane[1:] + [(dp, planes[d]) for d in range(1, LANGS)] + [twin]
    for friend in friends:
        pl.semaphore_signal(barrier, inc=1, device_id=friend, device_id_type=MESH)

    small = [
        pltpu.make_async_copy(order_in, order, small_s.at[0]),
        pltpu.make_async_copy(tags_in, tags.at[0], small_s.at[1]),
        pltpu.make_async_copy(words_in, words, small_s.at[2]),
        pltpu.make_async_copy(weights_in, weights, small_s.at[3]),
    ]
    mine = [pltpu.make_async_copy(block.at[:, features(own)], head.at[words_at(z, 0, BLOCK), :], own_s.at[BATCHES])]
    for b in range(BATCHES):
        here = states.at[pl.ds(b * batch, batch), features(own)]
        mine.append(pltpu.make_async_copy(here, cols.at[span(b, 0), :], own_s.at[b]))
    for copy in small + mine:
        copy.start()

    pl.semaphore_wait(barrier, len(friends))

    head_copies = []
    for d in (2, 1, 3):
        copy = remote(
            block.at[pl.ds(pl.multiple_of(half * core, 16), half), features(own)],
            head.at[words_at(z, half * core, half), :],
            head_s.at[d - 1], head_r.at[d - 1], (dp, planes[d]),
        )
        copy.start()
        head_copies.append(copy)
    tag_copies = []
    for r in (3, 1, 2):
        copy = remote(tags_in, tags.at[r], tag_s.at[r - 1], tag_r.at[r - 1], plane[r])
        copy.start()
        tag_copies.append(copy)
    row_copies = [[] for _ in range(BATCHES)]

    def send_rows(b):
        for r in (3, 1, 2):
            n = b * 3 + r - 1
            copy = remote(
                states.at[pl.ds(b * batch, batch), features(chips[r])],
                cols.at[span(b, r), :],
                row_s.at[n], row_r.at[n], plane[r],
            )
            copy.start()
            row_copies[b].append(copy)

    send_rows(0)
    for copy in small:
        copy.wait()
    square = iota((rows, rows), 0) == iota((rows, rows), 1)
    lane = iota((rows, BLOCK), 1)

    def column(values):
        wide_values = jnp.broadcast_to(values, (rows, rows))
        return jnp.sum(jnp.where(square, wide_values, 0.0), axis=1, keepdims=True)

    for copy in tag_copies:
        copy.wait_recv()
    for r in range(4):
        tag = column(tags[r].astype(F32))
        number = jnp.zeros((rows, 1), F32)
        for l in range(LANGS):
            number = jnp.where(tag == l, order[l].astype(F32), number)
        number = jnp.broadcast_to(number, (rows, BLOCK))
        for b in range(BATCHES):
            owner[span(b, r), :] = number[b * batch : (b + 1) * batch]
    target = column(words[...].astype(F32)).astype(jnp.int32)
    weight = column(weights[...].astype(F32))

    for copy in row_copies[0]:
        copy.wait_send()
    send_rows(1)

    twin_copies = []
    for d in (1, 2, 3):
        remote(
            head.at[words_at(sources[d], half * core, half), :],
            head.at[words_at(sources[d], half * core, half), :],
            head_s.at[d - 1], head_r.at[d - 1], (dp, planes[d]),
        ).wait_recv()
        copy = remote(
            head.at[words_at(sources[d], half * core, half), :],
            head.at[words_at(sources[d], half * core, half), :],
            twin_s.at[d - 1], twin_r.at[d - 1], twin,
        )
        copy.start()
        twin_copies.append(copy)
    for copy in twin_copies:
        copy.wait_recv()
    mine[0].wait()

    part_copies = [[] for _ in range(BATCHES)]
    grad_copies = [[] for _ in range(BATCHES)]
    back_copies = []
    losses = []

    def whole(b):
        return pl.ds(b * 4 * batch, 4 * batch)

    def partial_logits(b):
        mine[1 + b].wait()
        for copy in row_copies[b]:
            copy.wait_recv()

        if over:
            @pl.when(own == LANGS - 1)
            def _():
                cols[whole(b), :over] = jnp.zeros((4 * batch, over), BF16)

        every = dot(cols[whole(b), :], head[...], (1, 1))
        number = owner[whole(b), :]
        kept = jnp.zeros((4 * batch, BLOCK), F32)
        for n in range(LANGS):
            kept = jnp.where(number == n, every[:, n * BLOCK : (n + 1) * BLOCK], kept)
        part_got[span(b, 0), :] = kept[:batch]
        for r in (3, 1, 2):
            n = b * 3 + r - 1
            part_send[span(b, r), :] = kept[r * batch : (r + 1) * batch]
            copy = remote(part_send.at[span(b, r), :], part_got.at[span(b, r), :], part_s.at[n], part_r.at[n], plane[r])
            copy.start()
            part_copies[b].append(copy)

    def softmax_grads(b):
        for copy in part_copies[b]:
            copy.wait_recv()
        pick = slice(b * batch, (b + 1) * batch)
        logits = (part_got[span(b, 0), :] + part_got[span(b, 1), :]) + (
            part_got[span(b, 2), :] + part_got[span(b, 3), :]
        )
        hit = lane[pick] == target[pick]
        peak = jnp.max(logits, axis=1, keepdims=True)
        total = peak + jnp.log(jnp.sum(jnp.exp(logits - peak), axis=1, keepdims=True))
        losses.append(total - jnp.sum(jnp.where(hit, logits, 0.0), axis=1, keepdims=True))
        grads[span(b, 0), :] = (weight[pick] * (jnp.exp(logits - total) - jnp.where(hit, 1.0, 0.0))).astype(BF16)
        for r in (3, 1, 2):
            n = b * 3 + r - 1
            copy = remote(grads.at[span(b, 0), :], grads.at[span(b, r), :], grad_s.at[n], grad_r.at[n], plane[r])
            copy.start()
            grad_copies[b].append(copy)

    def spread_grads(b):
        for copy in grad_copies[b]:
            copy.wait_recv()
        number = owner[whole(b), :]
        values = grads[whole(b), :].astype(F32)
        for n in range(LANGS):
            spread[whole(b), pl.ds(n * BLOCK, BLOCK)] = jnp.where(number == n, values, 0.0).astype(BF16)

    def give_back(b):
        back_send[whole(b), :] = dot(spread[whole(b), :], head[...], (1, 0)).astype(BF16)
        for r in (3, 1, 2):
            n = b * 3 + r - 1
            copy = remote(
                back_send.at[span(b, r), :],
                back_out.at[own, pl.ds(b * batch, batch), :],
                back_s.at[n], back_r.at[n], plane[r],
            )
            copy.start()
            back_copies.append(copy)
        copy = pltpu.make_async_copy(
            back_send.at[span(b, 0), :], back_out.at[own, pl.ds(b * batch, batch), :], own_s.at[BATCHES + 1 + b]
        )
        copy.start()
        mine.append(copy)

    partial_logits(0)
    softmax_grads(0)
    partial_logits(1)
    spread_grads(0)
    give_back(0)
    softmax_grads(1)
    spread_grads(1)

    def mine_of(e, which):
        return pl.ds(pl.multiple_of(2 * share * e + share * which, 16), share)

    pair_copies = {}
    line_copies = []

    def both(d, e):
        return term[d, mine_of(e, core), :] + pair_got[d, pl.ds(e * share, share), :].astype(F32)

    def head_term(d):
        picked = spread[:, pl.ds(pl.multiple_of(planes[d] * BLOCK, 128), BLOCK)]
        term[d] = dot(picked, cols[...], (0, 0))
        for e in range(LANGS):
            pair_send[d, pl.ds(e * share, share), :] = term[d, mine_of(e, 1 - core), :].astype(BF16)
        pair_copies[d] = remote(pair_send.at[d], pair_got.at[d], pair_s.at[d], pair_r.at[d], twin)
        pair_copies[d].start()

    def along_line(d):
        pair_copies[d].wait_recv()
        for e in range(LANGS):
            line_send[d - 1, pl.ds(e * share, share), :] = both(d, e).astype(BF16)
        copy = remote(
            line_send.at[d - 1], line_got.at[d - 1], line_s.at[d - 1], line_r.at[d - 1], (dp, planes[d])
        )
        copy.start()
        line_copies.append(copy)

    head_term(2)
    head_term(1)
    along_line(2)
    head_term(3)
    along_line(1)
    along_line(3)
    for b in range(1, BATCHES):
        give_back(b)
    head_term(0)

    loss = jnp.concatenate(losses, axis=0)
    loss_out[...] = jnp.sum(jnp.where(square, loss, 0.0), axis=0, keepdims=True)

    pair_copies[0].wait_recv()
    for copy in line_copies:
        copy.wait_recv()
    for e in range(LANGS):
        part = pl.ds(e * share, share)
        plane_send[e] = (
            (both(0, e) + line_got[0, part, :].astype(F32))
            + (line_got[1, part, :].astype(F32) + line_got[2, part, :].astype(F32))
        ).astype(BF16)
    plane_copies = []
    for r in (3, 1, 2):
        copy = remote(
            plane_send.at[chips[r]], head_out.at[own], plane_s.at[r - 1], plane_r.at[r - 1], plane[r]
        )
        copy.start()
        plane_copies.append(copy)
    copy = pltpu.make_async_copy(plane_send.at[own], head_out.at[own], own_s.at[2 * BATCHES + 1])
    copy.start()
    mine.append(copy)

    for copy in back_copies + plane_copies:
        copy.wait_recv()
    for copy in mine[1 + BATCHES :]:
        copy.wait()
    everything = (
        head_copies + tag_copies + twin_copies + back_copies + line_copies + plane_copies
        + [c for group in row_copies[1:] + part_copies + grad_copies for c in group]
        + [pair_copies[d] for d in range(LANGS)]
    )
    for copy in everything:
        copy.wait_send()


def joined_kernel(
    loss_in, back_in, head_in, loss_out, state_out, head_out, loss_got, back_got, head_got, head_done, got, put
):
    wide = back_in.shape[2]
    over = LANGS * wide - state_out.shape[1]
    loads = [
        pltpu.make_async_copy(head_in, head_got, got.at[LANGS]),
        pltpu.make_async_copy(loss_in, loss_got, got.at[LANGS + 1]),
    ]
    loads += [pltpu.make_async_copy(back_in.at[e], back_got.at[e], got.at[e]) for e in range(LANGS)]
    for copy in loads:
        copy.start()
    skips = [over if e == LANGS - 1 else 0 for e in range(LANGS)]
    stores = []

    def store(src, dst, n):
        copy = pltpu.make_async_copy(src, dst, put.at[n])
        copy.start()
        stores.append(copy)

    loads[0].wait()
    for e, skip in enumerate(skips):
        head_done[0, :, pl.ds(e * wide, wide - skip)] = head_got[e, :, pl.ds(skip, wide - skip)].astype(F32)
    store(head_done, head_out, LANGS)
    loads[1].wait()
    store(loss_got, loss_out, LANGS + 1)
    for e, skip in enumerate(skips):
        loads[2 + e].wait()
        store(
            back_got.at[e, :, pl.ds(skip, wide - skip)], state_out.at[:, pl.ds(e * wide, wide - skip)], e
        )
    for copy in stores:
        copy.wait()


def sliced(final_states, head_blocks, block_order, row_tags, target_word, row_weight):
    rows, width = final_states.shape
    wide = slice_width(width)
    over = LANGS * wide - width
    share = BLOCK // (2 * LANGS)
    half = BLOCK // 2
    group = LANGS * rows
    hbm = pl.BlockSpec(memory_space=pl.ANY)
    vmem = pl.BlockSpec(memory_space=pltpu.VMEM)
    dma = pltpu.SemaphoreType.DMA
    three, batches = dma((3,)), dma((3 * BATCHES,))
    loss, back, head = pl.pallas_call(
        sliced_kernel,
        out_shape=(
            jax.ShapeDtypeStruct((1, rows), F32),
            jax.ShapeDtypeStruct((LANGS, rows, wide), BF16),
            jax.ShapeDtypeStruct((LANGS, share, wide), BF16),
        ),
        in_specs=[hbm] * 6,
        out_specs=(vmem, hbm, hbm),
        scratch_shapes=[
            pltpu.SMEM((LANGS,), jnp.int32),
            pltpu.VMEM((LANGS, 1, rows), jnp.int32),
            pltpu.VMEM((1, rows), jnp.int32),
            pltpu.VMEM((1, rows), BF16),
            pltpu.VMEM((group, wide), BF16),
            pltpu.VMEM((LANGS * BLOCK, wide), BF16),
            pltpu.VMEM((group, BLOCK), F32),
            pltpu.VMEM((group, BLOCK), F32),
            pltpu.VMEM((group, BLOCK), F32),
            pltpu.VMEM((group, BLOCK), BF16),
            pltpu.VMEM((group, LANGS * BLOCK), BF16),
            pltpu.VMEM((group, wide), BF16),
            pltpu.VMEM((LANGS, BLOCK, wide), F32),
            pltpu.VMEM((LANGS, half, wide), BF16),
            pltpu.VMEM((LANGS, half, wide), BF16),
            pltpu.VMEM((LANGS - 1, half, wide), BF16),
            pltpu.VMEM((LANGS - 1, half, wide), BF16),
            pltpu.VMEM((LANGS, share, wide), BF16),
            dma((4,)), dma((2 * BATCHES + 2,)), three, three, three, three, three, three, batches, batches,
            batches, batches, batches, batches, batches, batches, dma((LANGS,)), dma((LANGS,)),
            three, three, three, three,
        ],
        compiler_params=pltpu.CompilerParams(
            collective_id=0, has_side_effects=True, vmem_limit_bytes=60 * 1024 * 1024
        ),
        name="sliced",
    )(
        block_order,
        row_tags.reshape(1, rows),
        target_word.reshape(1, rows),
        row_weight.reshape(1, rows),
        final_states,
        head_blocks.reshape(BLOCK, width),
    )
    loss, state_grad, head_grad = pl.pallas_call(
        joined_kernel,
        out_shape=(
            jax.ShapeDtypeStruct((1, rows), F32),
            jax.ShapeDtypeStruct((rows, width), BF16),
            jax.ShapeDtypeStruct((1, share, width), F32),
        ),
        in_specs=[hbm] * 3,
        out_specs=[hbm] * 3,
        scratch_shapes=[
            pltpu.VMEM((1, rows), F32),
            pltpu.VMEM((LANGS, rows, wide), BF16),
            pltpu.VMEM((LANGS, share, wide), BF16),
            pltpu.VMEM((1, share, width), F32),
            dma((LANGS + 2,)),
            dma((LANGS + 2,)),
        ],
        compiler_params=pltpu.CompilerParams(vmem_limit_bytes=60 * 1024 * 1024),
        name="joined",
    )(loss, back, head)
    return loss.reshape(rows), state_grad, head_grad


def shards(final_states, head_blocks, block_order, row_tags, target_word, row_weight):
    shard_count = lax.axis_size("vocab")
    rows_here = final_states.shape[0]
    short_len = shard_count // LANGS
    capacity = rows_here * 5 // 16
    block_ids = jnp.arange(shard_count, dtype=jnp.int32)
    placed = jnp.sum(
        block_ids[:, None] * (block_order[:, None] == block_ids[None, :]).astype(jnp.int32), axis=0
    )
    owner_tag = placed // short_len
    owner_slot = placed % short_len
    tag_ids = jnp.arange(LANGS, dtype=jnp.int32)
    tag_onehot = (row_tags[:, None] == tag_ids[None, :]).astype(jnp.int32)
    row_rank = jnp.sum((jnp.cumsum(tag_onehot, axis=0) - 1) * tag_onehot, axis=1)
    routed = owner_tag[:, None] == row_tags[None, :]
    slot_ids = jnp.arange(capacity, dtype=jnp.int32)
    chosen = routed[:, None, :] & (row_rank[None, None, :] == slot_ids[None, :, None])
    chosen_int = chosen.astype(jnp.int32)
    slot_used = jnp.sum(chosen_int, axis=2) > 0
    row_ids = jnp.arange(rows_here, dtype=jnp.int32)
    slot_row = jnp.sum(chosen_int * row_ids[None, None, :], axis=2)
    sent_rows = jnp.where(
        slot_used[:, :, None], jnp.take(final_states, slot_row, axis=0), jnp.zeros((), jnp.bfloat16)
    )
    local_word = jnp.where(
        target_word[None, :] // BLOCK == owner_slot[:, None], target_word[None, :] % BLOCK, -1
    )
    slot_word = jnp.sum(chosen_int * (local_word[:, None, :] + 1), axis=2) - 1
    slot_label = jnp.where(slot_used, slot_row, -1)
    slot_weight = jnp.sum(
        jnp.where(chosen, row_weight.astype(jnp.float32)[None, None, :], 0.0), axis=2
    ).astype(jnp.bfloat16)
    got_rows, got_label, got_word, got_weight = (
        lax.all_to_all(sent_rows, "vocab", split_axis=0, concat_axis=0, tiled=True),
        lax.all_to_all(slot_label, "vocab", split_axis=0, concat_axis=0, tiled=True),
        lax.all_to_all(slot_word, "vocab", split_axis=0, concat_axis=0, tiled=True),
        lax.all_to_all(slot_weight, "vocab", split_axis=0, concat_axis=0, tiled=True),
    )
    own_block = head_blocks[0]
    logits = jnp.einsum("scd,wd->scw", got_rows, own_block, preferred_element_type=jnp.float32)
    word_ids = jnp.arange(BLOCK, dtype=jnp.int32)
    target_hit = word_ids[None, None, :] == got_word[:, :, None]
    slot_peak = jnp.max(logits, axis=2)
    slot_total = jnp.sum(jnp.exp(logits - slot_peak[:, :, None]), axis=2)
    slot_picked = jnp.sum(jnp.where(target_hit, logits, 0.0), axis=2)
    back_peak, back_total, back_picked = (
        lax.all_to_all(slot_peak, "vocab", split_axis=0, concat_axis=0, tiled=True),
        lax.all_to_all(slot_total, "vocab", split_axis=0, concat_axis=0, tiled=True),
        lax.all_to_all(slot_picked, "vocab", split_axis=0, concat_axis=0, tiled=True),
    )
    row_peak = jnp.take(back_peak, row_rank, axis=1)
    row_total = jnp.take(back_total, row_rank, axis=1)
    row_picked = jnp.take(back_picked, row_rank, axis=1)
    peak_max = jnp.max(jnp.where(routed, row_peak, -1e30), axis=0)
    summed = jnp.sum(
        jnp.where(routed, row_total * jnp.exp(row_peak - peak_max[None, :]), 0.0), axis=0
    )
    log_total = peak_max + jnp.log(summed)
    row_loss = log_total - jnp.sum(jnp.where(routed, row_picked, 0.0), axis=0)
    slot_lse = jnp.where(slot_used, jnp.take(log_total, slot_row), 0.0)
    got_lse = lax.all_to_all(slot_lse, "vocab", split_axis=0, concat_axis=0, tiled=True)
    slot_probs = jnp.exp(logits - got_lse[:, :, None])
    slot_grads = (
        got_weight.astype(jnp.float32)[:, :, None] * (slot_probs - target_hit.astype(jnp.float32))
    ).astype(jnp.bfloat16)
    part_grads = jnp.einsum(
        "scw,wd->scd", slot_grads, own_block, preferred_element_type=jnp.float32
    ).astype(jnp.bfloat16)
    back_grads = lax.all_to_all(part_grads, "vocab", split_axis=0, concat_axis=0, tiled=True)
    state_grad = jnp.einsum(
        "sct,scd->td", chosen.astype(jnp.bfloat16), back_grads, preferred_element_type=jnp.float32
    ).astype(jnp.bfloat16)
    head_term = jnp.einsum("scw,scd->wd", slot_grads, got_rows, preferred_element_type=jnp.float32)
    head_share = lax.psum_scatter(head_term, "dp", scatter_dimension=0, tiled=True)
    return (row_loss, state_grad, head_share[None])


def solution(mesh):
    one_each = mesh.shape["vocab"] == LANGS and mesh.shape["dp"] == 2 * LANGS
    return jax.shard_map(
        sliced if one_each else shards,
        mesh=mesh,
        in_specs=(
            P(("dp", "vocab"), None),
            P("vocab", None, None),
            P(),
            P(("dp", "vocab")),
            P(("dp", "vocab")),
            P(("dp", "vocab")),
        ),
        out_specs=(P(("dp", "vocab")), P(("dp", "vocab"), None), P("vocab", "dp", None)),
        check_vma=False,
    )
```

```python
import jax
import jax.numpy as jnp
from jax import lax
from jax.experimental import pallas as pl
from jax.experimental.pallas import tpu as pltpu
from jax.sharding import PartitionSpec as P

BLOCK = 128
LANGS = 4
MESH = pl.DeviceIdType.MESH
F32 = jnp.float32
BF16 = jnp.bfloat16
BATCHES = 2


def dot(a, b, dims):
    return lax.dot_general(a, b, ((dims[:1], dims[1:]), ((), ())), preferred_element_type=F32)


def iota(shape, dim):
    return lax.broadcasted_iota(jnp.int32, shape, dim)


def slice_width(width):
    return 128 * (-(-width // (128 * LANGS)))


def sliced_kernel(
    order_in, tags_in, words_in, weights_in, states, block,
    loss_out, back_out, head_out,
    order, tags, words, weights, cols, head, owner, part_send, part_got, grads, spread,
    back_send, term, pair_send, pair_got, line_send, line_got, plane_send,
    small_s, own_s, tag_s, tag_r, head_s, head_r, twin_s, twin_r, row_s, row_r,
    part_s, part_r, grad_s, grad_r, back_s, back_r, pair_s, pair_r, line_s, line_r, plane_s, plane_r,
):
    rows, width = states.shape
    wide = slice_width(width)
    over = LANGS * wide - width
    batch = rows // BATCHES
    half = BLOCK // 2
    share = BLOCK // (2 * LANGS)

    dp, z = lax.axis_index("dp"), lax.axis_index("vocab")
    core = lax.rem(dp, 2)
    x = lax.rem(lax.div(dp, 2), 2)
    y = lax.div(dp, 4)
    chips = [(y if r < 2 else 1 - y) * 2 + (x if r % 2 == 0 else 1 - x) for r in range(4)]
    own = chips[0]
    plane = [(c * 2 + core, z) for c in chips]
    twin = (own * 2 + 1 - core, z)
    planes = [lax.rem(z + d, LANGS) for d in range(LANGS)]
    sources = [lax.rem(z + LANGS - d, LANGS) for d in range(LANGS)]

    def remote(src, dst, send, recv, to):
        return pltpu.make_async_remote_copy(
            src_ref=src, dst_ref=dst, send_sem=send, recv_sem=recv, device_id=to, device_id_type=MESH
        )

    def features(chip):
        return pl.ds(pl.multiple_of(jnp.minimum(chip * wide, width - wide), 128), wide)

    def span(b, r):
        return pl.ds((b * 4 + r) * batch, batch)

    def words_at(plane_id, first, count):
        return pl.ds(pl.multiple_of(plane_id * BLOCK + first, 16), count)

    barrier = pltpu.get_barrier_semaphore()
    friends = plane[1:] + [(dp, planes[d]) for d in range(1, LANGS)] + [twin]
    for friend in friends:
        pl.semaphore_signal(barrier, inc=1, device_id=friend, device_id_type=MESH)

    small = [
        pltpu.make_async_copy(order_in, order, small_s.at[0]),
        pltpu.make_async_copy(tags_in, tags.at[0], small_s.at[1]),
        pltpu.make_async_copy(words_in, words, small_s.at[2]),
        pltpu.make_async_copy(weights_in, weights, small_s.at[3]),
    ]
    mine = [pltpu.make_async_copy(block.at[:, features(own)], head.at[words_at(z, 0, BLOCK), :], own_s.at[BATCHES])]
    for b in range(BATCHES):
        here = states.at[pl.ds(b * batch, batch), features(own)]
        mine.append(pltpu.make_async_copy(here, cols.at[span(b, 0), :], own_s.at[b]))
    for copy in small + mine:
        copy.start()

    pl.semaphore_wait(barrier, len(friends))

    head_copies = []
    for d in (2, 1, 3):
        copy = remote(
            block.at[pl.ds(pl.multiple_of(half * core, 16), half), features(own)],
            head.at[words_at(z, half * core, half), :],
            head_s.at[d - 1], head_r.at[d - 1], (dp, planes[d]),
        )
        copy.start()
        head_copies.append(copy)
    tag_copies = []
    for r in (3, 1, 2):
        copy = remote(tags_in, tags.at[r], tag_s.at[r - 1], tag_r.at[r - 1], plane[r])
        copy.start()
        tag_copies.append(copy)
    row_copies = [[], []]
    for b in range(BATCHES):
        for r in (3, 1, 2):
            n = b * 3 + r - 1
            copy = remote(
                states.at[pl.ds(b * batch, batch), features(chips[r])],
                cols.at[span(b, r), :],
                row_s.at[n], row_r.at[n], plane[r],
            )
            copy.start()
            row_copies[b].append(copy)

    for copy in small:
        copy.wait()
    square = iota((rows, rows), 0) == iota((rows, rows), 1)
    lane = iota((rows, BLOCK), 1)

    def column(values):
        wide_values = jnp.broadcast_to(values, (rows, rows))
        return jnp.sum(jnp.where(square, wide_values, 0.0), axis=1, keepdims=True)

    for copy in tag_copies:
        copy.wait_recv()
    for r in range(4):
        tag = column(tags[r].astype(F32))
        number = jnp.zeros((rows, 1), F32)
        for l in range(LANGS):
            number = jnp.where(tag == l, order[l].astype(F32), number)
        number = jnp.broadcast_to(number, (rows, BLOCK))
        for b in range(BATCHES):
            owner[span(b, r), :] = number[b * batch : (b + 1) * batch]
    target = column(words[...].astype(F32)).astype(jnp.int32)
    weight = column(weights[...].astype(F32))

    twin_copies = []
    for d in (1, 2, 3):
        remote(
            head.at[words_at(sources[d], half * core, half), :],
            head.at[words_at(sources[d], half * core, half), :],
            head_s.at[d - 1], head_r.at[d - 1], (dp, planes[d]),
        ).wait_recv()
        copy = remote(
            head.at[words_at(sources[d], half * core, half), :],
            head.at[words_at(sources[d], half * core, half), :],
            twin_s.at[d - 1], twin_r.at[d - 1], twin,
        )
        copy.start()
        twin_copies.append(copy)
    for copy in twin_copies:
        copy.wait_recv()
    mine[0].wait()

    part_copies = [[] for _ in range(BATCHES)]
    grad_copies = [[] for _ in range(BATCHES)]
    back_copies = []
    losses = []

    def whole(b):
        return pl.ds(b * 4 * batch, 4 * batch)

    def partial_logits(b):
        mine[1 + b].wait()
        for copy in row_copies[b]:
            copy.wait_recv()

        if over:
            @pl.when(own == LANGS - 1)
            def _():
                cols[whole(b), :over] = jnp.zeros((4 * batch, over), BF16)

        every = dot(cols[whole(b), :], head[...], (1, 1))
        number = owner[whole(b), :]
        kept = jnp.zeros((4 * batch, BLOCK), F32)
        for n in range(LANGS):
            kept = jnp.where(number == n, every[:, n * BLOCK : (n + 1) * BLOCK], kept)
        part_got[span(b, 0), :] = kept[:batch]
        for r in (3, 1, 2):
            n = b * 3 + r - 1
            part_send[span(b, r), :] = kept[r * batch : (r + 1) * batch]
            copy = remote(part_send.at[span(b, r), :], part_got.at[span(b, r), :], part_s.at[n], part_r.at[n], plane[r])
            copy.start()
            part_copies[b].append(copy)

    def softmax_grads(b):
        for copy in part_copies[b]:
            copy.wait_recv()
        pick = slice(b * batch, (b + 1) * batch)
        logits = (part_got[span(b, 0), :] + part_got[span(b, 1), :]) + (
            part_got[span(b, 2), :] + part_got[span(b, 3), :]
        )
        hit = lane[pick] == target[pick]
        peak = jnp.max(logits, axis=1, keepdims=True)
        total = peak + jnp.log(jnp.sum(jnp.exp(logits - peak), axis=1, keepdims=True))
        losses.append(total - jnp.sum(jnp.where(hit, logits, 0.0), axis=1, keepdims=True))
        grads[span(b, 0), :] = (weight[pick] * (jnp.exp(logits - total) - jnp.where(hit, 1.0, 0.0))).astype(BF16)
        for r in (3, 1, 2):
            n = b * 3 + r - 1
            copy = remote(grads.at[span(b, 0), :], grads.at[span(b, r), :], grad_s.at[n], grad_r.at[n], plane[r])
            copy.start()
            grad_copies[b].append(copy)

    def spread_grads(b):
        for copy in grad_copies[b]:
            copy.wait_recv()
        number = owner[whole(b), :]
        values = grads[whole(b), :].astype(F32)
        for n in range(LANGS):
            spread[whole(b), pl.ds(n * BLOCK, BLOCK)] = jnp.where(number == n, values, 0.0).astype(BF16)

    def give_back(b):
        back_send[whole(b), :] = dot(spread[whole(b), :], head[...], (1, 0)).astype(BF16)
        for r in (3, 1, 2):
            n = b * 3 + r - 1
            copy = remote(
                back_send.at[span(b, r), :],
                back_out.at[own, pl.ds(b * batch, batch), :],
                back_s.at[n], back_r.at[n], plane[r],
            )
            copy.start()
            back_copies.append(copy)
        copy = pltpu.make_async_copy(
            back_send.at[span(b, 0), :], back_out.at[own, pl.ds(b * batch, batch), :], own_s.at[BATCHES + 1 + b]
        )
        copy.start()
        mine.append(copy)

    for b in range(BATCHES):
        partial_logits(b)
    for b in range(BATCHES):
        softmax_grads(b)
    for b in range(BATCHES):
        spread_grads(b)

    def mine_of(e, which):
        return pl.ds(pl.multiple_of(2 * share * e + share * which, 16), share)

    pair_copies = {}
    line_copies = []

    def both(d, e):
        return term[d, mine_of(e, core), :] + pair_got[d, pl.ds(e * share, share), :].astype(F32)

    def head_term(d):
        picked = spread[:, pl.ds(pl.multiple_of(planes[d] * BLOCK, 128), BLOCK)]
        term[d] = dot(picked, cols[...], (0, 0))
        for e in range(LANGS):
            pair_send[d, pl.ds(e * share, share), :] = term[d, mine_of(e, 1 - core), :].astype(BF16)
        pair_copies[d] = remote(pair_send.at[d], pair_got.at[d], pair_s.at[d], pair_r.at[d], twin)
        pair_copies[d].start()

    def along_line(d):
        pair_copies[d].wait_recv()
        for e in range(LANGS):
            line_send[d - 1, pl.ds(e * share, share), :] = both(d, e).astype(BF16)
        copy = remote(
            line_send.at[d - 1], line_got.at[d - 1], line_s.at[d - 1], line_r.at[d - 1], (dp, planes[d])
        )
        copy.start()
        line_copies.append(copy)

    head_term(2)
    head_term(1)
    along_line(2)
    head_term(3)
    along_line(1)
    along_line(3)
    for b in range(BATCHES):
        give_back(b)
    head_term(0)

    loss = jnp.concatenate(losses, axis=0)
    loss_out[...] = jnp.sum(jnp.where(square, loss, 0.0), axis=0, keepdims=True)

    pair_copies[0].wait_recv()
    for copy in line_copies:
        copy.wait_recv()
    for e in range(LANGS):
        part = pl.ds(e * share, share)
        plane_send[e] = (
            (both(0, e) + line_got[0, part, :].astype(F32))
            + (line_got[1, part, :].astype(F32) + line_got[2, part, :].astype(F32))
        ).astype(BF16)
    plane_copies = []
    for r in (3, 1, 2):
        copy = remote(
            plane_send.at[chips[r]], head_out.at[own], plane_s.at[r - 1], plane_r.at[r - 1], plane[r]
        )
        copy.start()
        plane_copies.append(copy)
    copy = pltpu.make_async_copy(plane_send.at[own], head_out.at[own], own_s.at[2 * BATCHES + 1])
    copy.start()
    mine.append(copy)

    for copy in back_copies + plane_copies:
        copy.wait_recv()
    for copy in mine[1 + BATCHES :]:
        copy.wait()
    everything = (
        head_copies + tag_copies + twin_copies + back_copies + line_copies + plane_copies
        + [c for group in row_copies + part_copies + grad_copies for c in group]
        + [pair_copies[d] for d in range(LANGS)]
    )
    for copy in everything:
        copy.wait_send()


def joined_kernel(
    loss_in, back_in, head_in, loss_out, state_out, head_out, loss_got, back_got, head_got, head_done, got, put
):
    wide = back_in.shape[2]
    over = LANGS * wide - state_out.shape[1]
    loads = [
        pltpu.make_async_copy(head_in, head_got, got.at[LANGS]),
        pltpu.make_async_copy(loss_in, loss_got, got.at[LANGS + 1]),
    ]
    loads += [pltpu.make_async_copy(back_in.at[e], back_got.at[e], got.at[e]) for e in range(LANGS)]
    for copy in loads:
        copy.start()
    skips = [over if e == LANGS - 1 else 0 for e in range(LANGS)]
    stores = []

    def store(src, dst, n):
        copy = pltpu.make_async_copy(src, dst, put.at[n])
        copy.start()
        stores.append(copy)

    loads[0].wait()
    for e, skip in enumerate(skips):
        head_done[0, :, pl.ds(e * wide, wide - skip)] = head_got[e, :, pl.ds(skip, wide - skip)].astype(F32)
    store(head_done, head_out, LANGS)
    loads[1].wait()
    store(loss_got, loss_out, LANGS + 1)
    for e, skip in enumerate(skips):
        loads[2 + e].wait()
        store(
            back_got.at[e, :, pl.ds(skip, wide - skip)], state_out.at[:, pl.ds(e * wide, wide - skip)], e
        )
    for copy in stores:
        copy.wait()


def sliced(final_states, head_blocks, block_order, row_tags, target_word, row_weight):
    rows, width = final_states.shape
    wide = slice_width(width)
    over = LANGS * wide - width
    share = BLOCK // (2 * LANGS)
    half = BLOCK // 2
    group = LANGS * rows
    hbm = pl.BlockSpec(memory_space=pl.ANY)
    vmem = pl.BlockSpec(memory_space=pltpu.VMEM)
    dma = pltpu.SemaphoreType.DMA
    three, batches = dma((3,)), dma((3 * BATCHES,))
    loss, back, head = pl.pallas_call(
        sliced_kernel,
        out_shape=(
            jax.ShapeDtypeStruct((1, rows), F32),
            jax.ShapeDtypeStruct((LANGS, rows, wide), BF16),
            jax.ShapeDtypeStruct((LANGS, share, wide), BF16),
        ),
        in_specs=[hbm] * 6,
        out_specs=(vmem, hbm, hbm),
        scratch_shapes=[
            pltpu.SMEM((LANGS,), jnp.int32),
            pltpu.VMEM((LANGS, 1, rows), jnp.int32),
            pltpu.VMEM((1, rows), jnp.int32),
            pltpu.VMEM((1, rows), BF16),
            pltpu.VMEM((group, wide), BF16),
            pltpu.VMEM((LANGS * BLOCK, wide), BF16),
            pltpu.VMEM((group, BLOCK), F32),
            pltpu.VMEM((group, BLOCK), F32),
            pltpu.VMEM((group, BLOCK), F32),
            pltpu.VMEM((group, BLOCK), BF16),
            pltpu.VMEM((group, LANGS * BLOCK), BF16),
            pltpu.VMEM((group, wide), BF16),
            pltpu.VMEM((LANGS, BLOCK, wide), F32),
            pltpu.VMEM((LANGS, half, wide), BF16),
            pltpu.VMEM((LANGS, half, wide), BF16),
            pltpu.VMEM((LANGS - 1, half, wide), BF16),
            pltpu.VMEM((LANGS - 1, half, wide), BF16),
            pltpu.VMEM((LANGS, share, wide), BF16),
            dma((4,)), dma((2 * BATCHES + 2,)), three, three, three, three, three, three, batches, batches,
            batches, batches, batches, batches, batches, batches, dma((LANGS,)), dma((LANGS,)),
            three, three, three, three,
        ],
        compiler_params=pltpu.CompilerParams(
            collective_id=0, has_side_effects=True, vmem_limit_bytes=60 * 1024 * 1024
        ),
        name="sliced",
    )(
        block_order,
        row_tags.reshape(1, rows),
        target_word.reshape(1, rows),
        row_weight.reshape(1, rows),
        final_states,
        head_blocks.reshape(BLOCK, width),
    )
    loss, state_grad, head_grad = pl.pallas_call(
        joined_kernel,
        out_shape=(
            jax.ShapeDtypeStruct((1, rows), F32),
            jax.ShapeDtypeStruct((rows, width), BF16),
            jax.ShapeDtypeStruct((1, share, width), F32),
        ),
        in_specs=[hbm] * 3,
        out_specs=[hbm] * 3,
        scratch_shapes=[
            pltpu.VMEM((1, rows), F32),
            pltpu.VMEM((LANGS, rows, wide), BF16),
            pltpu.VMEM((LANGS, share, wide), BF16),
            pltpu.VMEM((1, share, width), F32),
            dma((LANGS + 2,)),
            dma((LANGS + 2,)),
        ],
        compiler_params=pltpu.CompilerParams(vmem_limit_bytes=60 * 1024 * 1024),
        name="joined",
    )(loss, back, head)
    return loss.reshape(rows), state_grad, head_grad


def shards(final_states, head_blocks, block_order, row_tags, target_word, row_weight):
    shard_count = lax.axis_size("vocab")
    rows_here = final_states.shape[0]
    short_len = shard_count // LANGS
    capacity = rows_here * 5 // 16
    block_ids = jnp.arange(shard_count, dtype=jnp.int32)
    placed = jnp.sum(
        block_ids[:, None] * (block_order[:, None] == block_ids[None, :]).astype(jnp.int32), axis=0
    )
    owner_tag = placed // short_len
    owner_slot = placed % short_len
    tag_ids = jnp.arange(LANGS, dtype=jnp.int32)
    tag_onehot = (row_tags[:, None] == tag_ids[None, :]).astype(jnp.int32)
    row_rank = jnp.sum((jnp.cumsum(tag_onehot, axis=0) - 1) * tag_onehot, axis=1)
    routed = owner_tag[:, None] == row_tags[None, :]
    slot_ids = jnp.arange(capacity, dtype=jnp.int32)
    chosen = routed[:, None, :] & (row_rank[None, None, :] == slot_ids[None, :, None])
    chosen_int = chosen.astype(jnp.int32)
    slot_used = jnp.sum(chosen_int, axis=2) > 0
    row_ids = jnp.arange(rows_here, dtype=jnp.int32)
    slot_row = jnp.sum(chosen_int * row_ids[None, None, :], axis=2)
    sent_rows = jnp.where(
        slot_used[:, :, None], jnp.take(final_states, slot_row, axis=0), jnp.zeros((), jnp.bfloat16)
    )
    local_word = jnp.where(
        target_word[None, :] // BLOCK == owner_slot[:, None], target_word[None, :] % BLOCK, -1
    )
    slot_word = jnp.sum(chosen_int * (local_word[:, None, :] + 1), axis=2) - 1
    slot_label = jnp.where(slot_used, slot_row, -1)
    slot_weight = jnp.sum(
        jnp.where(chosen, row_weight.astype(jnp.float32)[None, None, :], 0.0), axis=2
    ).astype(jnp.bfloat16)
    got_rows, got_label, got_word, got_weight = (
        lax.all_to_all(sent_rows, "vocab", split_axis=0, concat_axis=0, tiled=True),
        lax.all_to_all(slot_label, "vocab", split_axis=0, concat_axis=0, tiled=True),
        lax.all_to_all(slot_word, "vocab", split_axis=0, concat_axis=0, tiled=True),
        lax.all_to_all(slot_weight, "vocab", split_axis=0, concat_axis=0, tiled=True),
    )
    own_block = head_blocks[0]
    logits = jnp.einsum("scd,wd->scw", got_rows, own_block, preferred_element_type=jnp.float32)
    word_ids = jnp.arange(BLOCK, dtype=jnp.int32)
    target_hit = word_ids[None, None, :] == got_word[:, :, None]
    slot_peak = jnp.max(logits, axis=2)
    slot_total = jnp.sum(jnp.exp(logits - slot_peak[:, :, None]), axis=2)
    slot_picked = jnp.sum(jnp.where(target_hit, logits, 0.0), axis=2)
    back_peak, back_total, back_picked = (
        lax.all_to_all(slot_peak, "vocab", split_axis=0, concat_axis=0, tiled=True),
        lax.all_to_all(slot_total, "vocab", split_axis=0, concat_axis=0, tiled=True),
        lax.all_to_all(slot_picked, "vocab", split_axis=0, concat_axis=0, tiled=True),
    )
    row_peak = jnp.take(back_peak, row_rank, axis=1)
    row_total = jnp.take(back_total, row_rank, axis=1)
    row_picked = jnp.take(back_picked, row_rank, axis=1)
    peak_max = jnp.max(jnp.where(routed, row_peak, -1e30), axis=0)
    summed = jnp.sum(
        jnp.where(routed, row_total * jnp.exp(row_peak - peak_max[None, :]), 0.0), axis=0
    )
    log_total = peak_max + jnp.log(summed)
    row_loss = log_total - jnp.sum(jnp.where(routed, row_picked, 0.0), axis=0)
    slot_lse = jnp.where(slot_used, jnp.take(log_total, slot_row), 0.0)
    got_lse = lax.all_to_all(slot_lse, "vocab", split_axis=0, concat_axis=0, tiled=True)
    slot_probs = jnp.exp(logits - got_lse[:, :, None])
    slot_grads = (
        got_weight.astype(jnp.float32)[:, :, None] * (slot_probs - target_hit.astype(jnp.float32))
    ).astype(jnp.bfloat16)
    part_grads = jnp.einsum(
        "scw,wd->scd", slot_grads, own_block, preferred_element_type=jnp.float32
    ).astype(jnp.bfloat16)
    back_grads = lax.all_to_all(part_grads, "vocab", split_axis=0, concat_axis=0, tiled=True)
    state_grad = jnp.einsum(
        "sct,scd->td", chosen.astype(jnp.bfloat16), back_grads, preferred_element_type=jnp.float32
    ).astype(jnp.bfloat16)
    head_term = jnp.einsum("scw,scd->wd", slot_grads, got_rows, preferred_element_type=jnp.float32)
    head_share = lax.psum_scatter(head_term, "dp", scatter_dimension=0, tiled=True)
    return (row_loss, state_grad, head_share[None])


def solution(mesh):
    one_each = mesh.shape["vocab"] == LANGS and mesh.shape["dp"] == 2 * LANGS
    return jax.shard_map(
        sliced if one_each else shards,
        mesh=mesh,
        in_specs=(
            P(("dp", "vocab"), None),
            P("vocab", None, None),
            P(),
            P(("dp", "vocab")),
            P(("dp", "vocab")),
            P(("dp", "vocab")),
        ),
        out_specs=(P(("dp", "vocab")), P(("dp", "vocab"), None), P("vocab", "dp", None)),
        check_vma=False,
    )
```

```python
import jax
import jax.numpy as jnp
from jax import lax
from jax.experimental import pallas as pl
from jax.experimental.pallas import tpu as pltpu
from jax.sharding import PartitionSpec as P

BLOCK = 128
LANGS = 4
MESH = pl.DeviceIdType.MESH
F32 = jnp.float32
BF16 = jnp.bfloat16
BATCHES = 2


def dot(a, b, dims):
    return lax.dot_general(a, b, ((dims[:1], dims[1:]), ((), ())), preferred_element_type=F32)


def iota(shape, dim):
    return lax.broadcasted_iota(jnp.int32, shape, dim)


def slice_width(width):
    return 128 * (-(-width // (128 * LANGS)))


def sliced_kernel(
    order_in, tags_in, words_in, weights_in, states, block,
    loss_out, back_out, head_out,
    order, tags, words, weights, cols, head, owner, part_send, part_got, grads, spread,
    back_send, term, pair_send, pair_got, line_send, line_got, plane_send,
    small_s, own_s, tag_s, tag_r, head_s, head_r, twin_s, twin_r, row_s, row_r,
    part_s, part_r, grad_s, grad_r, back_s, back_r, pair_s, pair_r, line_s, line_r, plane_s, plane_r,
):
    rows, width = states.shape
    wide = slice_width(width)
    over = LANGS * wide - width
    batch = rows // BATCHES
    half = BLOCK // 2
    share = BLOCK // (2 * LANGS)

    dp, z = lax.axis_index("dp"), lax.axis_index("vocab")
    core = lax.rem(dp, 2)
    x = lax.rem(lax.div(dp, 2), 2)
    y = lax.div(dp, 4)
    chips = [(y if r < 2 else 1 - y) * 2 + (x if r % 2 == 0 else 1 - x) for r in range(4)]
    own = chips[0]
    plane = [(c * 2 + core, z) for c in chips]
    twin = (own * 2 + 1 - core, z)
    planes = [lax.rem(z + d, LANGS) for d in range(LANGS)]
    sources = [lax.rem(z + LANGS - d, LANGS) for d in range(LANGS)]

    def remote(src, dst, send, recv, to):
        return pltpu.make_async_remote_copy(
            src_ref=src, dst_ref=dst, send_sem=send, recv_sem=recv, device_id=to, device_id_type=MESH
        )

    def features(chip):
        return pl.ds(pl.multiple_of(jnp.minimum(chip * wide, width - wide), 128), wide)

    def span(b, r):
        return pl.ds((b * 4 + r) * batch, batch)

    def words_at(plane_id, first, count):
        return pl.ds(pl.multiple_of(plane_id * BLOCK + first, 16), count)

    turns = []
    for r in (jnp.int32(3), 1 + core, 2 - core):
        chip = lax.rem(y + lax.div(r, 2), 2) * 2 + lax.rem(x + lax.rem(r, 2), 2)
        turns.append((r, chip, (chip * 2 + core, z)))

    def spot(b, r):
        return pl.ds(pl.multiple_of((b * 4 + r) * batch, batch), batch)

    barrier = pltpu.get_barrier_semaphore()
    friends = plane[1:] + [(dp, planes[d]) for d in range(1, LANGS)] + [twin]
    for friend in friends:
        pl.semaphore_signal(barrier, inc=1, device_id=friend, device_id_type=MESH)

    small = [
        pltpu.make_async_copy(order_in, order, small_s.at[0]),
        pltpu.make_async_copy(tags_in, tags.at[0], small_s.at[1]),
        pltpu.make_async_copy(words_in, words, small_s.at[2]),
        pltpu.make_async_copy(weights_in, weights, small_s.at[3]),
    ]
    mine = [pltpu.make_async_copy(block.at[:, features(own)], head.at[words_at(z, 0, BLOCK), :], own_s.at[BATCHES])]
    for b in range(BATCHES):
        here = states.at[pl.ds(b * batch, batch), features(own)]
        mine.append(pltpu.make_async_copy(here, cols.at[span(b, 0), :], own_s.at[b]))
    for copy in small + mine:
        copy.start()

    pl.semaphore_wait(barrier, len(friends))

    head_copies = []
    for d in (2, 1, 3):
        copy = remote(
            block.at[pl.ds(pl.multiple_of(half * core, 16), half), features(own)],
            head.at[words_at(z, half * core, half), :],
            head_s.at[d - 1], head_r.at[d - 1], (dp, planes[d]),
        )
        copy.start()
        head_copies.append(copy)
    tag_copies = []
    for r in (3, 1, 2):
        copy = remote(tags_in, tags.at[r], tag_s.at[r - 1], tag_r.at[r - 1], plane[r])
        copy.start()
        tag_copies.append(copy)
    row_copies = [[], []]
    for b in range(BATCHES):
        for r, chip, to in turns:
            n = b * 3 + r - 1
            copy = remote(
                states.at[pl.ds(b * batch, batch), features(chip)],
                cols.at[spot(b, r), :],
                row_s.at[n], row_r.at[n], to,
            )
            copy.start()
            row_copies[b].append(copy)

    for copy in small:
        copy.wait()
    square = iota((rows, rows), 0) == iota((rows, rows), 1)
    lane = iota((rows, BLOCK), 1)

    def column(values):
        wide_values = jnp.broadcast_to(values, (rows, rows))
        return jnp.sum(jnp.where(square, wide_values, 0.0), axis=1, keepdims=True)

    for copy in tag_copies:
        copy.wait_recv()
    for r in range(4):
        tag = column(tags[r].astype(F32))
        number = jnp.zeros((rows, 1), F32)
        for l in range(LANGS):
            number = jnp.where(tag == l, order[l].astype(F32), number)
        number = jnp.broadcast_to(number, (rows, BLOCK))
        for b in range(BATCHES):
            owner[span(b, r), :] = number[b * batch : (b + 1) * batch]
    target = column(words[...].astype(F32)).astype(jnp.int32)
    weight = column(weights[...].astype(F32))

    twin_copies = []
    for d in (1, 2, 3):
        remote(
            head.at[words_at(sources[d], half * core, half), :],
            head.at[words_at(sources[d], half * core, half), :],
            head_s.at[d - 1], head_r.at[d - 1], (dp, planes[d]),
        ).wait_recv()
        copy = remote(
            head.at[words_at(sources[d], half * core, half), :],
            head.at[words_at(sources[d], half * core, half), :],
            twin_s.at[d - 1], twin_r.at[d - 1], twin,
        )
        copy.start()
        twin_copies.append(copy)
    for copy in twin_copies:
        copy.wait_recv()
    mine[0].wait()

    part_copies = [[] for _ in range(BATCHES)]
    grad_copies = [[] for _ in range(BATCHES)]
    back_copies = []
    losses = []

    def whole(b):
        return pl.ds(b * 4 * batch, 4 * batch)

    def partial_logits(b):
        mine[1 + b].wait()
        for copy in row_copies[b]:
            copy.wait_recv()

        if over:
            @pl.when(own == LANGS - 1)
            def _():
                cols[whole(b), :over] = jnp.zeros((4 * batch, over), BF16)

        every = dot(cols[whole(b), :], head[...], (1, 1))
        number = owner[whole(b), :]
        kept = jnp.zeros((4 * batch, BLOCK), F32)
        for n in range(LANGS):
            kept = jnp.where(number == n, every[:, n * BLOCK : (n + 1) * BLOCK], kept)
        part_got[span(b, 0), :] = kept[:batch]
        for r in (3, 1, 2):
            n = b * 3 + r - 1
            part_send[span(b, r), :] = kept[r * batch : (r + 1) * batch]
            copy = remote(part_send.at[span(b, r), :], part_got.at[span(b, r), :], part_s.at[n], part_r.at[n], plane[r])
            copy.start()
            part_copies[b].append(copy)

    def softmax_grads(b):
        for copy in part_copies[b]:
            copy.wait_recv()
        pick = slice(b * batch, (b + 1) * batch)
        logits = (part_got[span(b, 0), :] + part_got[span(b, 1), :]) + (
            part_got[span(b, 2), :] + part_got[span(b, 3), :]
        )
        hit = lane[pick] == target[pick]
        peak = jnp.max(logits, axis=1, keepdims=True)
        total = peak + jnp.log(jnp.sum(jnp.exp(logits - peak), axis=1, keepdims=True))
        losses.append(total - jnp.sum(jnp.where(hit, logits, 0.0), axis=1, keepdims=True))
        grads[span(b, 0), :] = (weight[pick] * (jnp.exp(logits - total) - jnp.where(hit, 1.0, 0.0))).astype(BF16)
        for r in (3, 1, 2):
            n = b * 3 + r - 1
            copy = remote(grads.at[span(b, 0), :], grads.at[span(b, r), :], grad_s.at[n], grad_r.at[n], plane[r])
            copy.start()
            grad_copies[b].append(copy)

    def spread_grads(b):
        for copy in grad_copies[b]:
            copy.wait_recv()
        number = owner[whole(b), :]
        values = grads[whole(b), :].astype(F32)
        for n in range(LANGS):
            spread[whole(b), pl.ds(n * BLOCK, BLOCK)] = jnp.where(number == n, values, 0.0).astype(BF16)

    def give_back(b):
        back_send[whole(b), :] = dot(spread[whole(b), :], head[...], (1, 0)).astype(BF16)
        for r, _, to in turns:
            n = b * 3 + r - 1
            copy = remote(
                back_send.at[spot(b, r), :],
                back_out.at[own, pl.ds(b * batch, batch), :],
                back_s.at[n], back_r.at[n], to,
            )
            copy.start()
            back_copies.append(copy)
        copy = pltpu.make_async_copy(
            back_send.at[span(b, 0), :], back_out.at[own, pl.ds(b * batch, batch), :], own_s.at[BATCHES + 1 + b]
        )
        copy.start()
        mine.append(copy)

    for b in range(BATCHES):
        partial_logits(b)
    for b in range(BATCHES):
        softmax_grads(b)
    for b in range(BATCHES):
        spread_grads(b)
        if b == 0:
            give_back(0)

    def mine_of(e, which):
        return pl.ds(pl.multiple_of(2 * share * e + share * which, 16), share)

    pair_copies = {}
    line_copies = []

    def both(d, e):
        return term[d, mine_of(e, core), :] + pair_got[d, pl.ds(e * share, share), :].astype(F32)

    def head_term(d):
        picked = spread[:, pl.ds(pl.multiple_of(planes[d] * BLOCK, 128), BLOCK)]
        term[d] = dot(picked, cols[...], (0, 0))
        for e in range(LANGS):
            pair_send[d, pl.ds(e * share, share), :] = term[d, mine_of(e, 1 - core), :].astype(BF16)
        pair_copies[d] = remote(pair_send.at[d], pair_got.at[d], pair_s.at[d], pair_r.at[d], twin)
        pair_copies[d].start()

    def along_line(d):
        pair_copies[d].wait_recv()
        for e in range(LANGS):
            line_send[d - 1, pl.ds(e * share, share), :] = both(d, e).astype(BF16)
        copy = remote(
            line_send.at[d - 1], line_got.at[d - 1], line_s.at[d - 1], line_r.at[d - 1], (dp, planes[d])
        )
        copy.start()
        line_copies.append(copy)

    head_term(2)
    head_term(1)
    along_line(2)
    head_term(3)
    along_line(1)
    along_line(3)
    for b in range(1, BATCHES):
        give_back(b)
    head_term(0)

    loss = jnp.concatenate(losses, axis=0)
    loss_out[...] = jnp.sum(jnp.where(square, loss, 0.0), axis=0, keepdims=True)

    pair_copies[0].wait_recv()
    for copy in line_copies:
        copy.wait_recv()
    for e in range(LANGS):
        part = pl.ds(e * share, share)
        plane_send[e] = (
            (both(0, e) + line_got[0, part, :].astype(F32))
            + (line_got[1, part, :].astype(F32) + line_got[2, part, :].astype(F32))
        ).astype(BF16)
    plane_copies = []
    for r in (3, 1, 2):
        copy = remote(
            plane_send.at[chips[r]], head_out.at[own], plane_s.at[r - 1], plane_r.at[r - 1], plane[r]
        )
        copy.start()
        plane_copies.append(copy)
    copy = pltpu.make_async_copy(plane_send.at[own], head_out.at[own], own_s.at[2 * BATCHES + 1])
    copy.start()
    mine.append(copy)

    for copy in back_copies + plane_copies:
        copy.wait_recv()
    for copy in mine[1 + BATCHES :]:
        copy.wait()
    everything = (
        head_copies + tag_copies + twin_copies + back_copies + line_copies + plane_copies
        + [c for group in row_copies + part_copies + grad_copies for c in group]
        + [pair_copies[d] for d in range(LANGS)]
    )
    for copy in everything:
        copy.wait_send()


def joined_kernel(
    loss_in, back_in, head_in, loss_out, state_out, head_out, loss_got, back_got, head_got, head_done, got, put
):
    wide = back_in.shape[2]
    over = LANGS * wide - state_out.shape[1]
    loads = [
        pltpu.make_async_copy(head_in, head_got, got.at[LANGS]),
        pltpu.make_async_copy(loss_in, loss_got, got.at[LANGS + 1]),
    ]
    loads += [pltpu.make_async_copy(back_in.at[e], back_got.at[e], got.at[e]) for e in range(LANGS)]
    for copy in loads:
        copy.start()
    skips = [over if e == LANGS - 1 else 0 for e in range(LANGS)]
    stores = []

    def store(src, dst, n):
        copy = pltpu.make_async_copy(src, dst, put.at[n])
        copy.start()
        stores.append(copy)

    loads[0].wait()
    for e, skip in enumerate(skips):
        head_done[0, :, pl.ds(e * wide, wide - skip)] = head_got[e, :, pl.ds(skip, wide - skip)].astype(F32)
    store(head_done, head_out, LANGS)
    loads[1].wait()
    store(loss_got, loss_out, LANGS + 1)
    for e, skip in enumerate(skips):
        loads[2 + e].wait()
        store(
            back_got.at[e, :, pl.ds(skip, wide - skip)], state_out.at[:, pl.ds(e * wide, wide - skip)], e
        )
    for copy in stores:
        copy.wait()


def sliced(final_states, head_blocks, block_order, row_tags, target_word, row_weight):
    rows, width = final_states.shape
    wide = slice_width(width)
    over = LANGS * wide - width
    share = BLOCK // (2 * LANGS)
    half = BLOCK // 2
    group = LANGS * rows
    hbm = pl.BlockSpec(memory_space=pl.ANY)
    vmem = pl.BlockSpec(memory_space=pltpu.VMEM)
    dma = pltpu.SemaphoreType.DMA
    three, batches = dma((3,)), dma((3 * BATCHES,))
    loss, back, head = pl.pallas_call(
        sliced_kernel,
        out_shape=(
            jax.ShapeDtypeStruct((1, rows), F32),
            jax.ShapeDtypeStruct((LANGS, rows, wide), BF16),
            jax.ShapeDtypeStruct((LANGS, share, wide), BF16),
        ),
        in_specs=[hbm] * 6,
        out_specs=(vmem, hbm, hbm),
        scratch_shapes=[
            pltpu.SMEM((LANGS,), jnp.int32),
            pltpu.VMEM((LANGS, 1, rows), jnp.int32),
            pltpu.VMEM((1, rows), jnp.int32),
            pltpu.VMEM((1, rows), BF16),
            pltpu.VMEM((group, wide), BF16),
            pltpu.VMEM((LANGS * BLOCK, wide), BF16),
            pltpu.VMEM((group, BLOCK), F32),
            pltpu.VMEM((group, BLOCK), F32),
            pltpu.VMEM((group, BLOCK), F32),
            pltpu.VMEM((group, BLOCK), BF16),
            pltpu.VMEM((group, LANGS * BLOCK), BF16),
            pltpu.VMEM((group, wide), BF16),
            pltpu.VMEM((LANGS, BLOCK, wide), F32),
            pltpu.VMEM((LANGS, half, wide), BF16),
            pltpu.VMEM((LANGS, half, wide), BF16),
            pltpu.VMEM((LANGS - 1, half, wide), BF16),
            pltpu.VMEM((LANGS - 1, half, wide), BF16),
            pltpu.VMEM((LANGS, share, wide), BF16),
            dma((4,)), dma((2 * BATCHES + 2,)), three, three, three, three, three, three, batches, batches,
            batches, batches, batches, batches, batches, batches, dma((LANGS,)), dma((LANGS,)),
            three, three, three, three,
        ],
        compiler_params=pltpu.CompilerParams(
            collective_id=0, has_side_effects=True, vmem_limit_bytes=60 * 1024 * 1024
        ),
        name="sliced",
    )(
        block_order,
        row_tags.reshape(1, rows),
        target_word.reshape(1, rows),
        row_weight.reshape(1, rows),
        final_states,
        head_blocks.reshape(BLOCK, width),
    )
    loss, state_grad, head_grad = pl.pallas_call(
        joined_kernel,
        out_shape=(
            jax.ShapeDtypeStruct((1, rows), F32),
            jax.ShapeDtypeStruct((rows, width), BF16),
            jax.ShapeDtypeStruct((1, share, width), F32),
        ),
        in_specs=[hbm] * 3,
        out_specs=[hbm] * 3,
        scratch_shapes=[
            pltpu.VMEM((1, rows), F32),
            pltpu.VMEM((LANGS, rows, wide), BF16),
            pltpu.VMEM((LANGS, share, wide), BF16),
            pltpu.VMEM((1, share, width), F32),
            dma((LANGS + 2,)),
            dma((LANGS + 2,)),
        ],
        compiler_params=pltpu.CompilerParams(vmem_limit_bytes=60 * 1024 * 1024),
        name="joined",
    )(loss, back, head)
    return loss.reshape(rows), state_grad, head_grad


def shards(final_states, head_blocks, block_order, row_tags, target_word, row_weight):
    shard_count = lax.axis_size("vocab")
    rows_here = final_states.shape[0]
    short_len = shard_count // LANGS
    capacity = rows_here * 5 // 16
    block_ids = jnp.arange(shard_count, dtype=jnp.int32)
    placed = jnp.sum(
        block_ids[:, None] * (block_order[:, None] == block_ids[None, :]).astype(jnp.int32), axis=0
    )
    owner_tag = placed // short_len
    owner_slot = placed % short_len
    tag_ids = jnp.arange(LANGS, dtype=jnp.int32)
    tag_onehot = (row_tags[:, None] == tag_ids[None, :]).astype(jnp.int32)
    row_rank = jnp.sum((jnp.cumsum(tag_onehot, axis=0) - 1) * tag_onehot, axis=1)
    routed = owner_tag[:, None] == row_tags[None, :]
    slot_ids = jnp.arange(capacity, dtype=jnp.int32)
    chosen = routed[:, None, :] & (row_rank[None, None, :] == slot_ids[None, :, None])
    chosen_int = chosen.astype(jnp.int32)
    slot_used = jnp.sum(chosen_int, axis=2) > 0
    row_ids = jnp.arange(rows_here, dtype=jnp.int32)
    slot_row = jnp.sum(chosen_int * row_ids[None, None, :], axis=2)
    sent_rows = jnp.where(
        slot_used[:, :, None], jnp.take(final_states, slot_row, axis=0), jnp.zeros((), jnp.bfloat16)
    )
    local_word = jnp.where(
        target_word[None, :] // BLOCK == owner_slot[:, None], target_word[None, :] % BLOCK, -1
    )
    slot_word = jnp.sum(chosen_int * (local_word[:, None, :] + 1), axis=2) - 1
    slot_label = jnp.where(slot_used, slot_row, -1)
    slot_weight = jnp.sum(
        jnp.where(chosen, row_weight.astype(jnp.float32)[None, None, :], 0.0), axis=2
    ).astype(jnp.bfloat16)
    got_rows, got_label, got_word, got_weight = (
        lax.all_to_all(sent_rows, "vocab", split_axis=0, concat_axis=0, tiled=True),
        lax.all_to_all(slot_label, "vocab", split_axis=0, concat_axis=0, tiled=True),
        lax.all_to_all(slot_word, "vocab", split_axis=0, concat_axis=0, tiled=True),
        lax.all_to_all(slot_weight, "vocab", split_axis=0, concat_axis=0, tiled=True),
    )
    own_block = head_blocks[0]
    logits = jnp.einsum("scd,wd->scw", got_rows, own_block, preferred_element_type=jnp.float32)
    word_ids = jnp.arange(BLOCK, dtype=jnp.int32)
    target_hit = word_ids[None, None, :] == got_word[:, :, None]
    slot_peak = jnp.max(logits, axis=2)
    slot_total = jnp.sum(jnp.exp(logits - slot_peak[:, :, None]), axis=2)
    slot_picked = jnp.sum(jnp.where(target_hit, logits, 0.0), axis=2)
    back_peak, back_total, back_picked = (
        lax.all_to_all(slot_peak, "vocab", split_axis=0, concat_axis=0, tiled=True),
        lax.all_to_all(slot_total, "vocab", split_axis=0, concat_axis=0, tiled=True),
        lax.all_to_all(slot_picked, "vocab", split_axis=0, concat_axis=0, tiled=True),
    )
    row_peak = jnp.take(back_peak, row_rank, axis=1)
    row_total = jnp.take(back_total, row_rank, axis=1)
    row_picked = jnp.take(back_picked, row_rank, axis=1)
    peak_max = jnp.max(jnp.where(routed, row_peak, -1e30), axis=0)
    summed = jnp.sum(
        jnp.where(routed, row_total * jnp.exp(row_peak - peak_max[None, :]), 0.0), axis=0
    )
    log_total = peak_max + jnp.log(summed)
    row_loss = log_total - jnp.sum(jnp.where(routed, row_picked, 0.0), axis=0)
    slot_lse = jnp.where(slot_used, jnp.take(log_total, slot_row), 0.0)
    got_lse = lax.all_to_all(slot_lse, "vocab", split_axis=0, concat_axis=0, tiled=True)
    slot_probs = jnp.exp(logits - got_lse[:, :, None])
    slot_grads = (
        got_weight.astype(jnp.float32)[:, :, None] * (slot_probs - target_hit.astype(jnp.float32))
    ).astype(jnp.bfloat16)
    part_grads = jnp.einsum(
        "scw,wd->scd", slot_grads, own_block, preferred_element_type=jnp.float32
    ).astype(jnp.bfloat16)
    back_grads = lax.all_to_all(part_grads, "vocab", split_axis=0, concat_axis=0, tiled=True)
    state_grad = jnp.einsum(
        "sct,scd->td", chosen.astype(jnp.bfloat16), back_grads, preferred_element_type=jnp.float32
    ).astype(jnp.bfloat16)
    head_term = jnp.einsum("scw,scd->wd", slot_grads, got_rows, preferred_element_type=jnp.float32)
    head_share = lax.psum_scatter(head_term, "dp", scatter_dimension=0, tiled=True)
    return (row_loss, state_grad, head_share[None])


def solution(mesh):
    one_each = mesh.shape["vocab"] == LANGS and mesh.shape["dp"] == 2 * LANGS
    return jax.shard_map(
        sliced if one_each else shards,
        mesh=mesh,
        in_specs=(
            P(("dp", "vocab"), None),
            P("vocab", None, None),
            P(),
            P(("dp", "vocab")),
            P(("dp", "vocab")),
            P(("dp", "vocab")),
        ),
        out_specs=(P(("dp", "vocab")), P(("dp", "vocab"), None), P("vocab", "dp", None)),
        check_vma=False,
    )
```

```python
import jax
import jax.numpy as jnp
from jax import lax
from jax.experimental import pallas as pl
from jax.experimental.pallas import tpu as pltpu
from jax.sharding import PartitionSpec as P

BLOCK = 128
LANGS = 4
MESH = pl.DeviceIdType.MESH
F32 = jnp.float32
BF16 = jnp.bfloat16
BATCHES = 1


def dot(a, b, dims):
    return lax.dot_general(a, b, ((dims[:1], dims[1:]), ((), ())), preferred_element_type=F32)


def iota(shape, dim):
    return lax.broadcasted_iota(jnp.int32, shape, dim)


def slice_width(width):
    return 128 * (-(-width // (128 * LANGS)))


def sliced_kernel(
    order_in, tags_in, words_in, weights_in, states, block,
    loss_out, back_out, head_out,
    order, tags, words, weights, cols, head, owner, part_send, part_got, grads, spread,
    back_send, term, pair_send, pair_got, line_send, line_got, plane_send,
    small_s, own_s, tag_s, tag_r, head_s, head_r, twin_s, twin_r, row_s, row_r,
    part_s, part_r, grad_s, grad_r, back_s, back_r, pair_s, pair_r, line_s, line_r, plane_s, plane_r,
):
    rows, width = states.shape
    wide = slice_width(width)
    over = LANGS * wide - width
    batch = rows // BATCHES
    half = BLOCK // 2
    share = BLOCK // (2 * LANGS)

    dp, z = lax.axis_index("dp"), lax.axis_index("vocab")
    core = lax.rem(dp, 2)
    x = lax.rem(lax.div(dp, 2), 2)
    y = lax.div(dp, 4)
    chips = [(y if r < 2 else 1 - y) * 2 + (x if r % 2 == 0 else 1 - x) for r in range(4)]
    own = chips[0]
    plane = [(c * 2 + core, z) for c in chips]
    twin = (own * 2 + 1 - core, z)
    planes = [lax.rem(z + d, LANGS) for d in range(LANGS)]
    sources = [lax.rem(z + LANGS - d, LANGS) for d in range(LANGS)]

    def remote(src, dst, send, recv, to):
        return pltpu.make_async_remote_copy(
            src_ref=src, dst_ref=dst, send_sem=send, recv_sem=recv, device_id=to, device_id_type=MESH
        )

    def features(chip):
        return pl.ds(pl.multiple_of(jnp.minimum(chip * wide, width - wide), 128), wide)

    def span(b, r):
        return pl.ds((b * 4 + r) * batch, batch)

    def words_at(plane_id, first, count):
        return pl.ds(pl.multiple_of(plane_id * BLOCK + first, 16), count)

    barrier = pltpu.get_barrier_semaphore()
    friends = plane[1:] + [(dp, planes[d]) for d in range(1, LANGS)] + [twin]
    for friend in friends:
        pl.semaphore_signal(barrier, inc=1, device_id=friend, device_id_type=MESH)

    small = [
        pltpu.make_async_copy(order_in, order, small_s.at[0]),
        pltpu.make_async_copy(tags_in, tags.at[0], small_s.at[1]),
        pltpu.make_async_copy(words_in, words, small_s.at[2]),
        pltpu.make_async_copy(weights_in, weights, small_s.at[3]),
    ]
    mine = [pltpu.make_async_copy(block.at[:, features(own)], head.at[words_at(z, 0, BLOCK), :], own_s.at[BATCHES])]
    for b in range(BATCHES):
        here = states.at[pl.ds(b * batch, batch), features(own)]
        mine.append(pltpu.make_async_copy(here, cols.at[span(b, 0), :], own_s.at[b]))
    for copy in small + mine:
        copy.start()

    pl.semaphore_wait(barrier, len(friends))

    head_copies = []
    for d in (2, 1, 3):
        copy = remote(
            block.at[pl.ds(pl.multiple_of(half * core, 16), half), features(own)],
            head.at[words_at(z, half * core, half), :],
            head_s.at[d - 1], head_r.at[d - 1], (dp, planes[d]),
        )
        copy.start()
        head_copies.append(copy)
    tag_copies = []
    for r in (3, 1, 2):
        copy = remote(tags_in, tags.at[r], tag_s.at[r - 1], tag_r.at[r - 1], plane[r])
        copy.start()
        tag_copies.append(copy)
    row_copies = [{} for _ in range(BATCHES)]
    for b in range(BATCHES):
        for r in (3, 1, 2):
            n = b * 3 + r - 1
            copy = remote(
                states.at[pl.ds(b * batch, batch), features(chips[r])],
                cols.at[span(b, r), :],
                row_s.at[n], row_r.at[n], plane[r],
            )
            copy.start()
            row_copies[b][r] = copy

    for copy in small:
        copy.wait()
    square = iota((rows, rows), 0) == iota((rows, rows), 1)
    lane = iota((rows, BLOCK), 1)

    def column(values):
        wide_values = jnp.broadcast_to(values, (rows, rows))
        return jnp.sum(jnp.where(square, wide_values, 0.0), axis=1, keepdims=True)

    for copy in tag_copies:
        copy.wait_recv()
    for r in range(4):
        tag = column(tags[r].astype(F32))
        number = jnp.zeros((rows, 1), F32)
        for l in range(LANGS):
            number = jnp.where(tag == l, order[l].astype(F32), number)
        number = jnp.broadcast_to(number, (rows, BLOCK))
        for b in range(BATCHES):
            owner[span(b, r), :] = number[b * batch : (b + 1) * batch]
    target = column(words[...].astype(F32)).astype(jnp.int32)
    weight = column(weights[...].astype(F32))

    twin_copies = []
    for d in (1, 2, 3):
        remote(
            head.at[words_at(sources[d], half * core, half), :],
            head.at[words_at(sources[d], half * core, half), :],
            head_s.at[d - 1], head_r.at[d - 1], (dp, planes[d]),
        ).wait_recv()
        copy = remote(
            head.at[words_at(sources[d], half * core, half), :],
            head.at[words_at(sources[d], half * core, half), :],
            twin_s.at[d - 1], twin_r.at[d - 1], twin,
        )
        copy.start()
        twin_copies.append(copy)
    for copy in twin_copies:
        copy.wait_recv()
    mine[0].wait()

    part_copies = [[] for _ in range(BATCHES)]
    grad_copies = [{} for _ in range(BATCHES)]
    back_copies = []
    losses = []

    def partial_logits(b, r):
        here = span(b, r)
        if r:
            row_copies[b][r].wait_recv()
        else:
            mine[1 + b].wait()

        if over:
            @pl.when(own == LANGS - 1)
            def _():
                cols[here, :over] = jnp.zeros((batch, over), BF16)

        every = dot(cols[here, :], head[...], (1, 1))
        number = owner[here, :]
        kept = jnp.zeros((batch, BLOCK), F32)
        for n in range(LANGS):
            kept = jnp.where(number == n, every[:, n * BLOCK : (n + 1) * BLOCK], kept)
        if r == 0:
            part_got[here, :] = kept
            return
        n = b * 3 + r - 1
        part_send[here, :] = kept
        copy = remote(part_send.at[here, :], part_got.at[here, :], part_s.at[n], part_r.at[n], plane[r])
        copy.start()
        part_copies[b].append(copy)

    def softmax_grads(b):
        for copy in part_copies[b]:
            copy.wait_recv()
        pick = slice(b * batch, (b + 1) * batch)
        logits = (part_got[span(b, 0), :] + part_got[span(b, 1), :]) + (
            part_got[span(b, 2), :] + part_got[span(b, 3), :]
        )
        hit = lane[pick] == target[pick]
        peak = jnp.max(logits, axis=1, keepdims=True)
        total = peak + jnp.log(jnp.sum(jnp.exp(logits - peak), axis=1, keepdims=True))
        losses.append(total - jnp.sum(jnp.where(hit, logits, 0.0), axis=1, keepdims=True))
        grads[span(b, 0), :] = (weight[pick] * (jnp.exp(logits - total) - jnp.where(hit, 1.0, 0.0))).astype(BF16)
        for r in (3, 1, 2):
            n = b * 3 + r - 1
            copy = remote(grads.at[span(b, 0), :], grads.at[span(b, r), :], grad_s.at[n], grad_r.at[n], plane[r])
            copy.start()
            grad_copies[b][r] = copy

    def spread_grads(b, r):
        here = span(b, r)
        if r:
            grad_copies[b][r].wait_recv()
        number = owner[here, :]
        values = grads[here, :].astype(F32)
        for n in range(LANGS):
            spread[here, pl.ds(n * BLOCK, BLOCK)] = jnp.where(number == n, values, 0.0).astype(BF16)

    def give_back(b, r):
        here = span(b, r)
        back_send[here, :] = dot(spread[here, :], head[...], (1, 0)).astype(BF16)
        there = back_out.at[own, pl.ds(b * batch, batch), :]
        if r:
            n = b * 3 + r - 1
            copy = remote(back_send.at[here, :], there, back_s.at[n], back_r.at[n], plane[r])
            back_copies.append(copy)
        else:
            copy = pltpu.make_async_copy(back_send.at[here, :], there, own_s.at[BATCHES + 1 + b])
            mine.append(copy)
        copy.start()

    for b in range(BATCHES):
        for r in (3, 1, 2, 0):
            partial_logits(b, r)
    for b in range(BATCHES):
        softmax_grads(b)
    for b in range(BATCHES):
        for r in (3, 1, 2, 0):
            spread_grads(b, r)
            if r in (3, 1):
                give_back(b, r)

    def mine_of(e, which):
        return pl.ds(pl.multiple_of(2 * share * e + share * which, 16), share)

    pair_copies = {}
    line_copies = []

    def both(d, e):
        return term[d, mine_of(e, core), :] + pair_got[d, pl.ds(e * share, share), :].astype(F32)

    def head_term(d):
        picked = spread[:, pl.ds(pl.multiple_of(planes[d] * BLOCK, 128), BLOCK)]
        term[d] = dot(picked, cols[...], (0, 0))
        for e in range(LANGS):
            pair_send[d, pl.ds(e * share, share), :] = term[d, mine_of(e, 1 - core), :].astype(BF16)
        pair_copies[d] = remote(pair_send.at[d], pair_got.at[d], pair_s.at[d], pair_r.at[d], twin)
        pair_copies[d].start()

    def along_line(d):
        pair_copies[d].wait_recv()
        for e in range(LANGS):
            line_send[d - 1, pl.ds(e * share, share), :] = both(d, e).astype(BF16)
        copy = remote(
            line_send.at[d - 1], line_got.at[d - 1], line_s.at[d - 1], line_r.at[d - 1], (dp, planes[d])
        )
        copy.start()
        line_copies.append(copy)

    head_term(2)
    head_term(1)
    along_line(2)
    head_term(3)
    along_line(1)
    along_line(3)
    for b in range(BATCHES):
        give_back(b, 2)
        give_back(b, 0)
    head_term(0)

    loss = jnp.concatenate(losses, axis=0)
    loss_out[...] = jnp.sum(jnp.where(square, loss, 0.0), axis=0, keepdims=True)

    pair_copies[0].wait_recv()
    for copy in line_copies:
        copy.wait_recv()
    for e in range(LANGS):
        part = pl.ds(e * share, share)
        plane_send[e] = (
            (both(0, e) + line_got[0, part, :].astype(F32))
            + (line_got[1, part, :].astype(F32) + line_got[2, part, :].astype(F32))
        ).astype(BF16)
    plane_copies = []
    for r in (3, 1, 2):
        copy = remote(
            plane_send.at[chips[r]], head_out.at[own], plane_s.at[r - 1], plane_r.at[r - 1], plane[r]
        )
        copy.start()
        plane_copies.append(copy)
    copy = pltpu.make_async_copy(plane_send.at[own], head_out.at[own], own_s.at[2 * BATCHES + 1])
    copy.start()
    mine.append(copy)

    for copy in back_copies + plane_copies:
        copy.wait_recv()
    for copy in mine[1 + BATCHES :]:
        copy.wait()
    everything = (
        head_copies + tag_copies + twin_copies + back_copies + line_copies + plane_copies
        + [c for group in part_copies for c in group]
        + [c for group in row_copies + grad_copies for c in group.values()]
        + [pair_copies[d] for d in range(LANGS)]
    )
    for copy in everything:
        copy.wait_send()


def joined_kernel(
    loss_in, back_in, head_in, loss_out, state_out, head_out, loss_got, back_got, head_got, head_done, got, put
):
    wide = back_in.shape[2]
    over = LANGS * wide - state_out.shape[1]
    loads = [
        pltpu.make_async_copy(head_in, head_got, got.at[LANGS]),
        pltpu.make_async_copy(loss_in, loss_got, got.at[LANGS + 1]),
    ]
    loads += [pltpu.make_async_copy(back_in.at[e], back_got.at[e], got.at[e]) for e in range(LANGS)]
    for copy in loads:
        copy.start()
    skips = [over if e == LANGS - 1 else 0 for e in range(LANGS)]
    stores = []

    def store(src, dst, n):
        copy = pltpu.make_async_copy(src, dst, put.at[n])
        copy.start()
        stores.append(copy)

    loads[0].wait()
    for e, skip in enumerate(skips):
        head_done[0, :, pl.ds(e * wide, wide - skip)] = head_got[e, :, pl.ds(skip, wide - skip)].astype(F32)
    store(head_done, head_out, LANGS)
    loads[1].wait()
    store(loss_got, loss_out, LANGS + 1)
    for e, skip in enumerate(skips):
        loads[2 + e].wait()
        store(
            back_got.at[e, :, pl.ds(skip, wide - skip)], state_out.at[:, pl.ds(e * wide, wide - skip)], e
        )
    for copy in stores:
        copy.wait()


def sliced(final_states, head_blocks, block_order, row_tags, target_word, row_weight):
    rows, width = final_states.shape
    wide = slice_width(width)
    over = LANGS * wide - width
    share = BLOCK // (2 * LANGS)
    half = BLOCK // 2
    group = LANGS * rows
    hbm = pl.BlockSpec(memory_space=pl.ANY)
    vmem = pl.BlockSpec(memory_space=pltpu.VMEM)
    dma = pltpu.SemaphoreType.DMA
    three, batches = dma((3,)), dma((3 * BATCHES,))
    loss, back, head = pl.pallas_call(
        sliced_kernel,
        out_shape=(
            jax.ShapeDtypeStruct((1, rows), F32),
            jax.ShapeDtypeStruct((LANGS, rows, wide), BF16),
            jax.ShapeDtypeStruct((LANGS, share, wide), BF16),
        ),
        in_specs=[hbm] * 6,
        out_specs=(vmem, hbm, hbm),
        scratch_shapes=[
            pltpu.SMEM((LANGS,), jnp.int32),
            pltpu.VMEM((LANGS, 1, rows), jnp.int32),
            pltpu.VMEM((1, rows), jnp.int32),
            pltpu.VMEM((1, rows), BF16),
            pltpu.VMEM((group, wide), BF16),
            pltpu.VMEM((LANGS * BLOCK, wide), BF16),
            pltpu.VMEM((group, BLOCK), F32),
            pltpu.VMEM((group, BLOCK), F32),
            pltpu.VMEM((group, BLOCK), F32),
            pltpu.VMEM((group, BLOCK), BF16),
            pltpu.VMEM((group, LANGS * BLOCK), BF16),
            pltpu.VMEM((group, wide), BF16),
            pltpu.VMEM((LANGS, BLOCK, wide), F32),
            pltpu.VMEM((LANGS, half, wide), BF16),
            pltpu.VMEM((LANGS, half, wide), BF16),
            pltpu.VMEM((LANGS - 1, half, wide), BF16),
            pltpu.VMEM((LANGS - 1, half, wide), BF16),
            pltpu.VMEM((LANGS, share, wide), BF16),
            dma((4,)), dma((2 * BATCHES + 2,)), three, three, three, three, three, three, batches, batches,
            batches, batches, batches, batches, batches, batches, dma((LANGS,)), dma((LANGS,)),
            three, three, three, three,
        ],
        compiler_params=pltpu.CompilerParams(
            collective_id=0, has_side_effects=True, vmem_limit_bytes=60 * 1024 * 1024
        ),
        name="sliced",
    )(
        block_order,
        row_tags.reshape(1, rows),
        target_word.reshape(1, rows),
        row_weight.reshape(1, rows),
        final_states,
        head_blocks.reshape(BLOCK, width),
    )
    loss, state_grad, head_grad = pl.pallas_call(
        joined_kernel,
        out_shape=(
            jax.ShapeDtypeStruct((1, rows), F32),
            jax.ShapeDtypeStruct((rows, width), BF16),
            jax.ShapeDtypeStruct((1, share, width), F32),
        ),
        in_specs=[hbm] * 3,
        out_specs=[hbm] * 3,
        scratch_shapes=[
            pltpu.VMEM((1, rows), F32),
            pltpu.VMEM((LANGS, rows, wide), BF16),
            pltpu.VMEM((LANGS, share, wide), BF16),
            pltpu.VMEM((1, share, width), F32),
            dma((LANGS + 2,)),
            dma((LANGS + 2,)),
        ],
        compiler_params=pltpu.CompilerParams(vmem_limit_bytes=60 * 1024 * 1024),
        name="joined",
    )(loss, back, head)
    return loss.reshape(rows), state_grad, head_grad


def shards(final_states, head_blocks, block_order, row_tags, target_word, row_weight):
    shard_count = lax.axis_size("vocab")
    rows_here = final_states.shape[0]
    short_len = shard_count // LANGS
    capacity = rows_here * 5 // 16
    block_ids = jnp.arange(shard_count, dtype=jnp.int32)
    placed = jnp.sum(
        block_ids[:, None] * (block_order[:, None] == block_ids[None, :]).astype(jnp.int32), axis=0
    )
    owner_tag = placed // short_len
    owner_slot = placed % short_len
    tag_ids = jnp.arange(LANGS, dtype=jnp.int32)
    tag_onehot = (row_tags[:, None] == tag_ids[None, :]).astype(jnp.int32)
    row_rank = jnp.sum((jnp.cumsum(tag_onehot, axis=0) - 1) * tag_onehot, axis=1)
    routed = owner_tag[:, None] == row_tags[None, :]
    slot_ids = jnp.arange(capacity, dtype=jnp.int32)
    chosen = routed[:, None, :] & (row_rank[None, None, :] == slot_ids[None, :, None])
    chosen_int = chosen.astype(jnp.int32)
    slot_used = jnp.sum(chosen_int, axis=2) > 0
    row_ids = jnp.arange(rows_here, dtype=jnp.int32)
    slot_row = jnp.sum(chosen_int * row_ids[None, None, :], axis=2)
    sent_rows = jnp.where(
        slot_used[:, :, None], jnp.take(final_states, slot_row, axis=0), jnp.zeros((), jnp.bfloat16)
    )
    local_word = jnp.where(
        target_word[None, :] // BLOCK == owner_slot[:, None], target_word[None, :] % BLOCK, -1
    )
    slot_word = jnp.sum(chosen_int * (local_word[:, None, :] + 1), axis=2) - 1
    slot_label = jnp.where(slot_used, slot_row, -1)
    slot_weight = jnp.sum(
        jnp.where(chosen, row_weight.astype(jnp.float32)[None, None, :], 0.0), axis=2
    ).astype(jnp.bfloat16)
    got_rows, got_label, got_word, got_weight = (
        lax.all_to_all(sent_rows, "vocab", split_axis=0, concat_axis=0, tiled=True),
        lax.all_to_all(slot_label, "vocab", split_axis=0, concat_axis=0, tiled=True),
        lax.all_to_all(slot_word, "vocab", split_axis=0, concat_axis=0, tiled=True),
        lax.all_to_all(slot_weight, "vocab", split_axis=0, concat_axis=0, tiled=True),
    )
    own_block = head_blocks[0]
    logits = jnp.einsum("scd,wd->scw", got_rows, own_block, preferred_element_type=jnp.float32)
    word_ids = jnp.arange(BLOCK, dtype=jnp.int32)
    target_hit = word_ids[None, None, :] == got_word[:, :, None]
    slot_peak = jnp.max(logits, axis=2)
    slot_total = jnp.sum(jnp.exp(logits - slot_peak[:, :, None]), axis=2)
    slot_picked = jnp.sum(jnp.where(target_hit, logits, 0.0), axis=2)
    back_peak, back_total, back_picked = (
        lax.all_to_all(slot_peak, "vocab", split_axis=0, concat_axis=0, tiled=True),
        lax.all_to_all(slot_total, "vocab", split_axis=0, concat_axis=0, tiled=True),
        lax.all_to_all(slot_picked, "vocab", split_axis=0, concat_axis=0, tiled=True),
    )
    row_peak = jnp.take(back_peak, row_rank, axis=1)
    row_total = jnp.take(back_total, row_rank, axis=1)
    row_picked = jnp.take(back_picked, row_rank, axis=1)
    peak_max = jnp.max(jnp.where(routed, row_peak, -1e30), axis=0)
    summed = jnp.sum(
        jnp.where(routed, row_total * jnp.exp(row_peak - peak_max[None, :]), 0.0), axis=0
    )
    log_total = peak_max + jnp.log(summed)
    row_loss = log_total - jnp.sum(jnp.where(routed, row_picked, 0.0), axis=0)
    slot_lse = jnp.where(slot_used, jnp.take(log_total, slot_row), 0.0)
    got_lse = lax.all_to_all(slot_lse, "vocab", split_axis=0, concat_axis=0, tiled=True)
    slot_probs = jnp.exp(logits - got_lse[:, :, None])
    slot_grads = (
        got_weight.astype(jnp.float32)[:, :, None] * (slot_probs - target_hit.astype(jnp.float32))
    ).astype(jnp.bfloat16)
    part_grads = jnp.einsum(
        "scw,wd->scd", slot_grads, own_block, preferred_element_type=jnp.float32
    ).astype(jnp.bfloat16)
    back_grads = lax.all_to_all(part_grads, "vocab", split_axis=0, concat_axis=0, tiled=True)
    state_grad = jnp.einsum(
        "sct,scd->td", chosen.astype(jnp.bfloat16), back_grads, preferred_element_type=jnp.float32
    ).astype(jnp.bfloat16)
    head_term = jnp.einsum("scw,scd->wd", slot_grads, got_rows, preferred_element_type=jnp.float32)
    head_share = lax.psum_scatter(head_term, "dp", scatter_dimension=0, tiled=True)
    return (row_loss, state_grad, head_share[None])


def solution(mesh):
    one_each = mesh.shape["vocab"] == LANGS and mesh.shape["dp"] == 2 * LANGS
    return jax.shard_map(
        sliced if one_each else shards,
        mesh=mesh,
        in_specs=(
            P(("dp", "vocab"), None),
            P("vocab", None, None),
            P(),
            P(("dp", "vocab")),
            P(("dp", "vocab")),
            P(("dp", "vocab")),
        ),
        out_specs=(P(("dp", "vocab")), P(("dp", "vocab"), None), P("vocab", "dp", None)),
        check_vma=False,
    )
```

```python
import jax
import jax.numpy as jnp
from jax import lax
from jax.experimental import pallas as pl
from jax.experimental.pallas import tpu as pltpu
from jax.sharding import PartitionSpec as P

BLOCK = 128
LANGS = 4
MESH = pl.DeviceIdType.MESH
F32 = jnp.float32
BF16 = jnp.bfloat16
BATCHES = 2


def dot(a, b, dims):
    return lax.dot_general(a, b, ((dims[:1], dims[1:]), ((), ())), preferred_element_type=F32)


def iota(shape, dim):
    return lax.broadcasted_iota(jnp.int32, shape, dim)


def slice_width(width):
    return 128 * (-(-width // (128 * LANGS)))


def sliced_kernel(
    order_in, tags_in, words_in, weights_in, states, block,
    loss_out, back_out, head_out,
    order, tags, words, weights, loss_row, cols, head, owner, part_send, part_got, grads, spread,
    back_send, term, pair_send, pair_got, line_send, line_got, plane_send,
    small_s, own_s, tag_s, tag_r, head_s, head_r, twin_s, twin_r, row_s, row_r,
    part_s, part_r, grad_s, grad_r, back_s, back_r, pair_s, pair_r, line_s, line_r, plane_s, plane_r,
):
    rows, width = states.shape
    wide = slice_width(width)
    over = LANGS * wide - width
    batch = rows // BATCHES
    half = BLOCK // 2
    share = BLOCK // (2 * LANGS)

    dp, z = lax.axis_index("dp"), lax.axis_index("vocab")
    core = lax.rem(dp, 2)
    x = lax.rem(lax.div(dp, 2), 2)
    y = lax.div(dp, 4)
    chips = [(y if r < 2 else 1 - y) * 2 + (x if r % 2 == 0 else 1 - x) for r in range(4)]
    own = chips[0]
    plane = [(c * 2 + core, z) for c in chips]
    twin = (own * 2 + 1 - core, z)
    planes = [lax.rem(z + d, LANGS) for d in range(LANGS)]
    sources = [lax.rem(z + LANGS - d, LANGS) for d in range(LANGS)]

    def remote(src, dst, send, recv, to):
        return pltpu.make_async_remote_copy(
            src_ref=src, dst_ref=dst, send_sem=send, recv_sem=recv, device_id=to, device_id_type=MESH
        )

    def features(chip):
        return pl.ds(pl.multiple_of(jnp.minimum(chip * wide, width - wide), 128), wide)

    def span(b, r):
        return pl.ds((b * 4 + r) * batch, batch)

    def words_at(plane_id, first, count):
        return pl.ds(pl.multiple_of(plane_id * BLOCK + first, 16), count)

    barrier = pltpu.get_barrier_semaphore()
    friends = plane[1:] + [(dp, planes[d]) for d in range(1, LANGS)] + [twin]
    for friend in friends:
        pl.semaphore_signal(barrier, inc=1, device_id=friend, device_id_type=MESH)

    small = [
        pltpu.make_async_copy(order_in, order, small_s.at[0]),
        pltpu.make_async_copy(tags_in, tags.at[0], small_s.at[1]),
        pltpu.make_async_copy(words_in, words, small_s.at[2]),
        pltpu.make_async_copy(weights_in, weights, small_s.at[3]),
    ]
    mine = [pltpu.make_async_copy(block.at[:, features(own)], head.at[words_at(z, 0, BLOCK), :], own_s.at[BATCHES])]
    for b in range(BATCHES):
        here = states.at[pl.ds(b * batch, batch), features(own)]
        mine.append(pltpu.make_async_copy(here, cols.at[span(b, 0), :], own_s.at[b]))
    for copy in small + mine:
        copy.start()

    pl.semaphore_wait(barrier, len(friends))

    head_copies = []
    for d in (2, 1, 3):
        copy = remote(
            block.at[pl.ds(pl.multiple_of(half * core, 16), half), features(own)],
            head.at[words_at(z, half * core, half), :],
            head_s.at[d - 1], head_r.at[d - 1], (dp, planes[d]),
        )
        copy.start()
        head_copies.append(copy)
    tag_copies = []
    for r in (3, 1, 2):
        copy = remote(tags_in, tags.at[r], tag_s.at[r - 1], tag_r.at[r - 1], plane[r])
        copy.start()
        tag_copies.append(copy)
    row_copies = [[], []]
    for b in range(BATCHES):
        for r in (3, 1, 2):
            n = b * 3 + r - 1
            copy = remote(
                states.at[pl.ds(b * batch, batch), features(chips[r])],
                cols.at[span(b, r), :],
                row_s.at[n], row_r.at[n], plane[r],
            )
            copy.start()
            row_copies[b].append(copy)

    for copy in small:
        copy.wait()
    square = iota((rows, rows), 0) == iota((rows, rows), 1)
    lane = iota((rows, BLOCK), 1)

    def column(values):
        wide_values = jnp.broadcast_to(values, (rows, rows))
        return jnp.sum(jnp.where(square, wide_values, 0.0), axis=1, keepdims=True)

    for copy in tag_copies:
        copy.wait_recv()
    for r in range(4):
        tag = column(tags[r].astype(F32))
        number = jnp.zeros((rows, 1), F32)
        for l in range(LANGS):
            number = jnp.where(tag == l, order[l].astype(F32), number)
        number = jnp.broadcast_to(number, (rows, BLOCK))
        for b in range(BATCHES):
            owner[span(b, r), :] = number[b * batch : (b + 1) * batch]
    target = column(words[...].astype(F32)).astype(jnp.int32)
    weight = column(weights[...].astype(F32))

    twin_copies = []
    for d in (1, 2, 3):
        remote(
            head.at[words_at(sources[d], half * core, half), :],
            head.at[words_at(sources[d], half * core, half), :],
            head_s.at[d - 1], head_r.at[d - 1], (dp, planes[d]),
        ).wait_recv()
        copy = remote(
            head.at[words_at(sources[d], half * core, half), :],
            head.at[words_at(sources[d], half * core, half), :],
            twin_s.at[d - 1], twin_r.at[d - 1], twin,
        )
        copy.start()
        twin_copies.append(copy)
    for copy in twin_copies:
        copy.wait_recv()
    mine[0].wait()

    part_copies = [[] for _ in range(BATCHES)]
    grad_copies = [[] for _ in range(BATCHES)]
    back_copies = []
    losses = []

    def whole(b):
        return pl.ds(b * 4 * batch, 4 * batch)

    def partial_logits(b):
        mine[1 + b].wait()
        for copy in row_copies[b]:
            copy.wait_recv()

        if over:
            @pl.when(own == LANGS - 1)
            def _():
                cols[whole(b), :over] = jnp.zeros((4 * batch, over), BF16)

        every = dot(cols[whole(b), :], head[...], (1, 1))
        number = owner[whole(b), :]
        kept = jnp.zeros((4 * batch, BLOCK), F32)
        for n in range(LANGS):
            kept = jnp.where(number == n, every[:, n * BLOCK : (n + 1) * BLOCK], kept)
        part_got[span(b, 0), :] = kept[:batch]
        for r in (3, 1, 2):
            n = b * 3 + r - 1
            part_send[span(b, r), :] = kept[r * batch : (r + 1) * batch]
            copy = remote(part_send.at[span(b, r), :], part_got.at[span(b, r), :], part_s.at[n], part_r.at[n], plane[r])
            copy.start()
            part_copies[b].append(copy)

    def softmax_grads(b):
        for copy in part_copies[b]:
            copy.wait_recv()
        pick = slice(b * batch, (b + 1) * batch)
        logits = (part_got[span(b, 0), :] + part_got[span(b, 1), :]) + (
            part_got[span(b, 2), :] + part_got[span(b, 3), :]
        )
        hit = lane[pick] == target[pick]
        peak = jnp.max(logits, axis=1, keepdims=True)
        total = peak + jnp.log(jnp.sum(jnp.exp(logits - peak), axis=1, keepdims=True))
        losses.append(total - jnp.sum(jnp.where(hit, logits, 0.0), axis=1, keepdims=True))
        grads[span(b, 0), :] = (weight[pick] * (jnp.exp(logits - total) - jnp.where(hit, 1.0, 0.0))).astype(BF16)
        for r in (3, 1, 2):
            n = b * 3 + r - 1
            copy = remote(grads.at[span(b, 0), :], grads.at[span(b, r), :], grad_s.at[n], grad_r.at[n], plane[r])
            copy.start()
            grad_copies[b].append(copy)

    def spread_grads(b):
        for copy in grad_copies[b]:
            copy.wait_recv()
        number = owner[whole(b), :]
        values = grads[whole(b), :].astype(F32)
        for n in range(LANGS):
            spread[whole(b), pl.ds(n * BLOCK, BLOCK)] = jnp.where(number == n, values, 0.0).astype(BF16)

    def give_back(b):
        back_send[whole(b), :] = dot(spread[whole(b), :], head[...], (1, 0)).astype(BF16)
        for r in (3, 1, 2):
            n = b * 3 + r - 1
            copy = remote(
                back_send.at[span(b, r), :],
                back_out.at[own, pl.ds(b * batch, batch), :],
                back_s.at[n], back_r.at[n], plane[r],
            )
            copy.start()
            back_copies.append(copy)
        copy = pltpu.make_async_copy(
            back_send.at[span(b, 0), :], back_out.at[own, pl.ds(b * batch, batch), :], own_s.at[BATCHES + 1 + b]
        )
        copy.start()
        mine.append(copy)

    for b in range(BATCHES):
        partial_logits(b)
    for b in range(BATCHES):
        softmax_grads(b)
    for b in range(BATCHES):
        spread_grads(b)
        if b == 0:
            give_back(0)

    def mine_of(e, which):
        return pl.ds(pl.multiple_of(2 * share * e + share * which, 16), share)

    pair_copies = {}
    line_copies = []

    def both(d, e):
        return term[d, mine_of(e, core), :] + pair_got[d, pl.ds(e * share, share), :].astype(F32)

    def head_term(d):
        picked = spread[:, pl.ds(pl.multiple_of(planes[d] * BLOCK, 128), BLOCK)]
        term[d] = dot(picked, cols[...], (0, 0))
        for e in range(LANGS):
            pair_send[d, pl.ds(e * share, share), :] = term[d, mine_of(e, 1 - core), :].astype(BF16)
        pair_copies[d] = remote(pair_send.at[d], pair_got.at[d], pair_s.at[d], pair_r.at[d], twin)
        pair_copies[d].start()

    def along_line(d):
        pair_copies[d].wait_recv()
        for e in range(LANGS):
            line_send[d - 1, pl.ds(e * share, share), :] = both(d, e).astype(BF16)
        copy = remote(
            line_send.at[d - 1], line_got.at[d - 1], line_s.at[d - 1], line_r.at[d - 1], (dp, planes[d])
        )
        copy.start()
        line_copies.append(copy)

    head_term(2)
    head_term(1)
    along_line(2)
    head_term(3)
    along_line(1)
    along_line(3)
    for b in range(1, BATCHES):
        give_back(b)
    head_term(0)

    loss = jnp.concatenate(losses, axis=0)
    loss_row[...] = jnp.sum(jnp.where(square, loss, 0.0), axis=0, keepdims=True)
    copy = pltpu.make_async_copy(loss_row, loss_out, own_s.at[2 * BATCHES + 2])
    copy.start()
    mine.append(copy)

    pair_copies[0].wait_recv()
    for copy in line_copies:
        copy.wait_recv()
    plane_copies = []
    for r in (3, 1, 2, 0):
        e = chips[r]
        part = pl.ds(pl.multiple_of(e * share, share), share)
        plane_send[r] = (
            (term[0, mine_of(e, core), :] + pair_got[0, part, :].astype(F32) + line_got[0, part, :].astype(F32))
            + (line_got[1, part, :].astype(F32) + line_got[2, part, :].astype(F32))
        ).astype(BF16)
        if r:
            copy = remote(plane_send.at[r], head_out.at[own], plane_s.at[r - 1], plane_r.at[r - 1], plane[r])
            plane_copies.append(copy)
        else:
            copy = pltpu.make_async_copy(plane_send.at[0], head_out.at[own], own_s.at[2 * BATCHES + 1])
            mine.append(copy)
        copy.start()

    for copy in back_copies + plane_copies:
        copy.wait_recv()
    for copy in mine[1 + BATCHES :]:
        copy.wait()
    everything = (
        head_copies + tag_copies + twin_copies + back_copies + line_copies + plane_copies
        + [c for group in row_copies + part_copies + grad_copies for c in group]
        + [pair_copies[d] for d in range(LANGS)]
    )
    for copy in everything:
        copy.wait_send()


def joined_kernel(
    loss_in, back_in, head_in, loss_out, state_out, head_out, loss_got, back_got, head_got, head_done, got, put
):
    wide = back_in.shape[2]
    over = LANGS * wide - state_out.shape[1]
    loads = [
        pltpu.make_async_copy(head_in, head_got, got.at[LANGS]),
        pltpu.make_async_copy(loss_in, loss_got, got.at[LANGS + 1]),
    ]
    piece = back_in.shape[1] // 2
    pieces = [(e, h) for h in range(2) for e in range(LANGS)]
    for e, h in pieces:
        here = pl.ds(h * piece, piece)
        loads.append(
            pltpu.make_async_copy(back_in.at[e, here, :], back_got.at[e, here, :], got.at[LANGS + 2 + h * LANGS + e])
        )
    for copy in loads:
        copy.start()
    skips = [over if e == LANGS - 1 else 0 for e in range(LANGS)]
    stores = []

    def store(src, dst, n):
        copy = pltpu.make_async_copy(src, dst, put.at[n])
        copy.start()
        stores.append(copy)

    loads[0].wait()
    for e, skip in enumerate(skips):
        head_done[0, :, pl.ds(e * wide, wide - skip)] = head_got[e, :, pl.ds(skip, wide - skip)].astype(F32)
    store(head_done, head_out, LANGS)
    loads[1].wait()
    store(loss_got, loss_out, LANGS + 1)
    for n, (e, h) in enumerate(pieces):
        loads[2 + n].wait()
        skip = skips[e]
        here = pl.ds(h * piece, piece)
        store(
            back_got.at[e, here, pl.ds(skip, wide - skip)],
            state_out.at[here, pl.ds(e * wide, wide - skip)],
            LANGS + 2 + n,
        )
    for copy in stores:
        copy.wait()


def sliced(final_states, head_blocks, block_order, row_tags, target_word, row_weight):
    rows, width = final_states.shape
    wide = slice_width(width)
    over = LANGS * wide - width
    share = BLOCK // (2 * LANGS)
    half = BLOCK // 2
    group = LANGS * rows
    hbm = pl.BlockSpec(memory_space=pl.ANY)
    dma = pltpu.SemaphoreType.DMA
    three, batches = dma((3,)), dma((3 * BATCHES,))
    loss, back, head = pl.pallas_call(
        sliced_kernel,
        out_shape=(
            jax.ShapeDtypeStruct((1, rows), F32),
            jax.ShapeDtypeStruct((LANGS, rows, wide), BF16),
            jax.ShapeDtypeStruct((LANGS, share, wide), BF16),
        ),
        in_specs=[hbm] * 6,
        out_specs=[hbm] * 3,
        scratch_shapes=[
            pltpu.SMEM((LANGS,), jnp.int32),
            pltpu.VMEM((LANGS, 1, rows), jnp.int32),
            pltpu.VMEM((1, rows), jnp.int32),
            pltpu.VMEM((1, rows), BF16),
            pltpu.VMEM((1, rows), F32),
            pltpu.VMEM((group, wide), BF16),
            pltpu.VMEM((LANGS * BLOCK, wide), BF16),
            pltpu.VMEM((group, BLOCK), F32),
            pltpu.VMEM((group, BLOCK), F32),
            pltpu.VMEM((group, BLOCK), F32),
            pltpu.VMEM((group, BLOCK), BF16),
            pltpu.VMEM((group, LANGS * BLOCK), BF16),
            pltpu.VMEM((group, wide), BF16),
            pltpu.VMEM((LANGS, BLOCK, wide), F32),
            pltpu.VMEM((LANGS, half, wide), BF16),
            pltpu.VMEM((LANGS, half, wide), BF16),
            pltpu.VMEM((LANGS - 1, half, wide), BF16),
            pltpu.VMEM((LANGS - 1, half, wide), BF16),
            pltpu.VMEM((LANGS, share, wide), BF16),
            dma((4,)), dma((2 * BATCHES + 3,)), three, three, three, three, three, three, batches, batches,
            batches, batches, batches, batches, batches, batches, dma((LANGS,)), dma((LANGS,)),
            three, three, three, three,
        ],
        compiler_params=pltpu.CompilerParams(
            collective_id=0, has_side_effects=True, vmem_limit_bytes=60 * 1024 * 1024
        ),
        name="sliced",
    )(
        block_order,
        row_tags.reshape(1, rows),
        target_word.reshape(1, rows),
        row_weight.reshape(1, rows),
        final_states,
        head_blocks.reshape(BLOCK, width),
    )
    loss, state_grad, head_grad = pl.pallas_call(
        joined_kernel,
        out_shape=(
            jax.ShapeDtypeStruct((1, rows), F32),
            jax.ShapeDtypeStruct((rows, width), BF16),
            jax.ShapeDtypeStruct((1, share, width), F32),
        ),
        in_specs=[hbm] * 3,
        out_specs=[hbm] * 3,
        scratch_shapes=[
            pltpu.VMEM((1, rows), F32),
            pltpu.VMEM((LANGS, rows, wide), BF16),
            pltpu.VMEM((LANGS, share, wide), BF16),
            pltpu.VMEM((1, share, width), F32),
            dma((3 * LANGS + 2,)),
            dma((3 * LANGS + 2,)),
        ],
        compiler_params=pltpu.CompilerParams(vmem_limit_bytes=60 * 1024 * 1024),
        name="joined",
    )(loss, back, head)
    return loss.reshape(rows), state_grad, head_grad


def shards(final_states, head_blocks, block_order, row_tags, target_word, row_weight):
    shard_count = lax.axis_size("vocab")
    rows_here = final_states.shape[0]
    short_len = shard_count // LANGS
    capacity = rows_here * 5 // 16
    block_ids = jnp.arange(shard_count, dtype=jnp.int32)
    placed = jnp.sum(
        block_ids[:, None] * (block_order[:, None] == block_ids[None, :]).astype(jnp.int32), axis=0
    )
    owner_tag = placed // short_len
    owner_slot = placed % short_len
    tag_ids = jnp.arange(LANGS, dtype=jnp.int32)
    tag_onehot = (row_tags[:, None] == tag_ids[None, :]).astype(jnp.int32)
    row_rank = jnp.sum((jnp.cumsum(tag_onehot, axis=0) - 1) * tag_onehot, axis=1)
    routed = owner_tag[:, None] == row_tags[None, :]
    slot_ids = jnp.arange(capacity, dtype=jnp.int32)
    chosen = routed[:, None, :] & (row_rank[None, None, :] == slot_ids[None, :, None])
    chosen_int = chosen.astype(jnp.int32)
    slot_used = jnp.sum(chosen_int, axis=2) > 0
    row_ids = jnp.arange(rows_here, dtype=jnp.int32)
    slot_row = jnp.sum(chosen_int * row_ids[None, None, :], axis=2)
    sent_rows = jnp.where(
        slot_used[:, :, None], jnp.take(final_states, slot_row, axis=0), jnp.zeros((), jnp.bfloat16)
    )
    local_word = jnp.where(
        target_word[None, :] // BLOCK == owner_slot[:, None], target_word[None, :] % BLOCK, -1
    )
    slot_word = jnp.sum(chosen_int * (local_word[:, None, :] + 1), axis=2) - 1
    slot_label = jnp.where(slot_used, slot_row, -1)
    slot_weight = jnp.sum(
        jnp.where(chosen, row_weight.astype(jnp.float32)[None, None, :], 0.0), axis=2
    ).astype(jnp.bfloat16)
    got_rows, got_label, got_word, got_weight = (
        lax.all_to_all(sent_rows, "vocab", split_axis=0, concat_axis=0, tiled=True),
        lax.all_to_all(slot_label, "vocab", split_axis=0, concat_axis=0, tiled=True),
        lax.all_to_all(slot_word, "vocab", split_axis=0, concat_axis=0, tiled=True),
        lax.all_to_all(slot_weight, "vocab", split_axis=0, concat_axis=0, tiled=True),
    )
    own_block = head_blocks[0]
    logits = jnp.einsum("scd,wd->scw", got_rows, own_block, preferred_element_type=jnp.float32)
    word_ids = jnp.arange(BLOCK, dtype=jnp.int32)
    target_hit = word_ids[None, None, :] == got_word[:, :, None]
    slot_peak = jnp.max(logits, axis=2)
    slot_total = jnp.sum(jnp.exp(logits - slot_peak[:, :, None]), axis=2)
    slot_picked = jnp.sum(jnp.where(target_hit, logits, 0.0), axis=2)
    back_peak, back_total, back_picked = (
        lax.all_to_all(slot_peak, "vocab", split_axis=0, concat_axis=0, tiled=True),
        lax.all_to_all(slot_total, "vocab", split_axis=0, concat_axis=0, tiled=True),
        lax.all_to_all(slot_picked, "vocab", split_axis=0, concat_axis=0, tiled=True),
    )
    row_peak = jnp.take(back_peak, row_rank, axis=1)
    row_total = jnp.take(back_total, row_rank, axis=1)
    row_picked = jnp.take(back_picked, row_rank, axis=1)
    peak_max = jnp.max(jnp.where(routed, row_peak, -1e30), axis=0)
    summed = jnp.sum(
        jnp.where(routed, row_total * jnp.exp(row_peak - peak_max[None, :]), 0.0), axis=0
    )
    log_total = peak_max + jnp.log(summed)
    row_loss = log_total - jnp.sum(jnp.where(routed, row_picked, 0.0), axis=0)
    slot_lse = jnp.where(slot_used, jnp.take(log_total, slot_row), 0.0)
    got_lse = lax.all_to_all(slot_lse, "vocab", split_axis=0, concat_axis=0, tiled=True)
    slot_probs = jnp.exp(logits - got_lse[:, :, None])
    slot_grads = (
        got_weight.astype(jnp.float32)[:, :, None] * (slot_probs - target_hit.astype(jnp.float32))
    ).astype(jnp.bfloat16)
    part_grads = jnp.einsum(
        "scw,wd->scd", slot_grads, own_block, preferred_element_type=jnp.float32
    ).astype(jnp.bfloat16)
    back_grads = lax.all_to_all(part_grads, "vocab", split_axis=0, concat_axis=0, tiled=True)
    state_grad = jnp.einsum(
        "sct,scd->td", chosen.astype(jnp.bfloat16), back_grads, preferred_element_type=jnp.float32
    ).astype(jnp.bfloat16)
    head_term = jnp.einsum("scw,scd->wd", slot_grads, got_rows, preferred_element_type=jnp.float32)
    head_share = lax.psum_scatter(head_term, "dp", scatter_dimension=0, tiled=True)
    return (row_loss, state_grad, head_share[None])


def solution(mesh):
    one_each = mesh.shape["vocab"] == LANGS and mesh.shape["dp"] == 2 * LANGS
    return jax.shard_map(
        sliced if one_each else shards,
        mesh=mesh,
        in_specs=(
            P(("dp", "vocab"), None),
            P("vocab", None, None),
            P(),
            P(("dp", "vocab")),
            P(("dp", "vocab")),
            P(("dp", "vocab")),
        ),
        out_specs=(P(("dp", "vocab")), P(("dp", "vocab"), None), P("vocab", "dp", None)),
        check_vma=False,
    )
```
